128 devices in a mesh: prow: 8 (over y, core), pcol: 16 (over z, x).
Axes of the slice: x: 4, y: 4, z: 4, core: 2. Of those that a mesh axis runs over, the one named last changes fastest.
Arguments:
- right_side: float32 [120, 262144], P(None, ('prow', 'pcol')), may hold values from -6 to 6
- part_count: int32 [128], P(('prow', 'pcol')), may hold values from 1024 to 2048, as said below
- elem_class: int32 [262144], P(('prow', 'pcol')), may hold values from 0 to 255
- face_link: int32 [1048576], P(('prow', 'pcol')), may hold values from -1 to 11263, as said below
- face_orient: int32 [1048576], P(('prow', 'pcol')), may hold values from 0 to 5
- face_normal: float32 [3, 1048576], P(None, ('prow', 'pcol')), may hold values from -1 to 1, as said below
- boundary_metric_quotient: float32 [1048576], P(('prow', 'pcol')), may hold values from 0.5 to 2
- bound_face: int32 [128, 8, 384], P(('prow', 'pcol')), may hold values from -1 to 8191, as said below
- lift: float32 [4, 20, 10], replicated, may hold values from -2.5 to 2.5
- inverse_table: bfloat16 [256, 120, 120], replicated
Outputs:
- basis: float32 [3, 120, 262144], P(None, None, ('prow', 'pcol'))
- hess: float32 [3, 2], replicated
The draws below stay inside these ranges and needn't reach their ends.
Inputs may be any that keep to these rules, and one draw needn't show every extreme that they name: Partition p's live elements take its first part_count[p] slots; one partition is full. `bound_face`: slots of list k of a partition hold faces s * 2048 + e of its live elements (repeats possible); -1 marks an empty slot and empty slots follow the filled ones; lists toward directions outside the grid are empty, every other list fills at least half of its 384 slots, and one partition fills all slots of those lists. `face_link`: a code q in 0 to 3071 names filled slot q % 384 of list 7 - q // 384 of the partition at the offset of direction q // 384, which exists; each filled slot of a list toward a partition is named by exactly one face of that partition; q >= 3072 names a face of a live element of the same partition; -1 is the physical boundary; all faces of empty element slots are -1. `face_normal`: unit vectors.
All inputs are finite; a program needn't handle non-finite values.
Results may differ from the reference program's by a relative error of at most 0.003.
Values sent between devices are 32-bit elements; how exact they have to be, the bound alone decides.
A program may use at most 128 MiB of HBM per device.

```python
import math
import jax
import jax.numpy as jnp
import numpy as np
from jax import lax

UNK = 120
CLASSES = 256
CELL_SLOT_LIMIT = 2048
BSLOT = 384
NE = 262144
N_PROW = 8
N_PCOL = 16


ROW_STEPS = (-1, -1, -1, 0, 0, 1, 1, 1)


COL_STEPS = (-1, 0, 1, -1, 1, -1, 0, 1)


def face_node_mask():
    element_points = [(coord_a, coord_b, coord_c, 3 - coord_a - coord_b - coord_c) for coord_a in range(4) for coord_b in range(4 - coord_a) for coord_c in range(4 - coord_a - coord_b)]
    face_points = [(coord_a, coord_b, 3 - coord_a - coord_b) for coord_a in range(4) for coord_b in range(4 - coord_a)]
    table = np.zeros((4, 20, 10), np.float32)
    for opposite in range(4):
        corners = [vertex for vertex in range(4) if vertex != opposite]
        for position_j in range(10):
            triple = face_points[position_j]
            coords = [0, 0, 0, 0]
            for position in range(3):
                coords[corners[position]] = triple[position]
            table[opposite, element_points.index(tuple(coords)), position_j] = 1.0
    return table


def layout_counts(key):
    all_subdomains = N_PROW * N_PCOL
    count_key, pick_key, fill_key = jax.random.split(jax.random.fold_in(key, 101), 3)
    slots = jnp.arange(all_subdomains)
    counts = jax.random.randint(count_key, (all_subdomains,), CELL_SLOT_LIMIT // 2, CELL_SLOT_LIMIT + 1)
    chosen = jax.random.randint(pick_key, (), 0, all_subdomains)
    counts = jnp.where(slots == chosen, CELL_SLOT_LIMIT, counts)
    fills = jax.random.randint(fill_key, (all_subdomains, 8), (BSLOT + 1) // 2, BSLOT + 1)
    fills = jnp.where((slots == chosen)[:, None], BSLOT, fills)
    row_steps = jnp.array(ROW_STEPS, jnp.int32)[None, :]
    col_steps = jnp.array(COL_STEPS, jnp.int32)[None, :]
    target_row = slots[:, None] // N_PCOL + row_steps
    target_col = slots[:, None] % N_PCOL + col_steps
    inside = (target_row >= 0) & (target_row < N_PROW) & (target_col >= 0) & (target_col < N_PCOL)
    fills = jnp.where(inside, fills, 0)
    source = jnp.clip(target_row, 0, N_PROW - 1) * N_PCOL + jnp.clip(target_col, 0, N_PCOL - 1)
    return (counts.astype(jnp.int32), fills.astype(jnp.int32), chosen, inside, source)


def draw_right_side(key, part):
    key = jax.random.fold_in(key, 19)
    sign_key, amplitude_key, node_key, level_key, noise_key = jax.random.split(key, 5)
    all_subdomains = N_PROW * N_PCOL
    sign_values = jnp.where(jax.random.randint(sign_key, (6, 1), 0, 2) == 0, -1.0, 1.0).astype(jnp.float32)
    amplitude_low, amplitude_high, level_low, level_high, ramp_total = (0.6, 1.0, 0.5, 1.5, 3.0)
    amplitude = jax.random.uniform(amplitude_key, (6, 1), jnp.float32, amplitude_low, amplitude_high)
    node_factor = 1.0 + 0.25 * jax.random.uniform(node_key, (6, 20), jnp.float32, -1.0, 1.0)
    pattern = (sign_values * amplitude * node_factor).reshape(UNK, 1)
    owner = (jnp.arange(NE) // CELL_SLOT_LIMIT).astype(jnp.float32)
    ramp_factor = jnp.exp(math.log(ramp_total) * owner / max(all_subdomains - 1, 1))
    levels = jax.random.uniform(level_key, (NE,), jnp.float32, level_low, level_high) * ramp_factor
    noise_part = 0.6 * jax.random.normal(noise_key, (UNK, NE), jnp.float32)
    return jnp.clip(pattern * levels[None, :] + noise_part, -6.0, 6.0).astype(jnp.float32)


def draw_lift(key, part):
    key = jax.random.fold_in(key, 23)
    noise_key, strength_key = jax.random.split(key)
    structure = jnp.asarray(face_node_mask())
    spread = jax.random.normal(noise_key, (4, 20, 10), jnp.float32) * math.sqrt(0.1)
    strength = jax.random.uniform(strength_key, (4, 1, 10), jnp.float32, 0.7, 1.3)
    return jnp.clip(spread + structure * strength, -2.5, 2.5).astype(jnp.float32)


def draw_part_count(key, part):
    counts, fills, chosen, inside, source = layout_counts(key)
    return counts


def draw_bound_face(key, part):
    all_subdomains = N_PROW * N_PCOL
    counts, fills, chosen, inside, source = layout_counts(key)
    key = jax.random.fold_in(key, 7)
    side_key, member_key = jax.random.split(key)
    shape = (all_subdomains, 8, BSLOT)
    sides = jax.random.randint(side_key, shape, 0, 4)
    members = jax.random.randint(member_key, shape, 0, jnp.broadcast_to(counts[:, None, None], shape))
    entries = sides * CELL_SLOT_LIMIT + members
    position = jnp.arange(BSLOT)[None, None, :]
    entries = jnp.where(position < fills[:, :, None], entries, -1)
    device_rows = jnp.arange(all_subdomains)[:, None, None]
    entries = jnp.where((device_rows == chosen) & (position == 0) & (entries >= 0), 4 * CELL_SLOT_LIMIT - 1, entries)
    return entries.astype(jnp.int32)


def draw_face_link(key, part):
    all_subdomains = N_PROW * N_PCOL
    counts, fills, chosen, inside, source = layout_counts(key)
    key = jax.random.fold_in(key, 11)
    kind_key, shift_key, side_key, member_key = jax.random.split(key, 4)
    shape = (all_subdomains, 4 * CELL_SLOT_LIMIT)
    opposite = (7 - jnp.arange(8))[None, :]
    need = jnp.where(inside, fills[source, jnp.broadcast_to(opposite, source.shape)], 0)
    ends = jnp.cumsum(need, axis=1)
    starts = ends - need
    total = ends[:, 7]
    shifts = jax.random.randint(shift_key, (all_subdomains,), 0, counts)
    device_rows = jnp.arange(all_subdomains)[:, None]
    face_index = jnp.arange(4 * CELL_SLOT_LIMIT)[None, :]
    side = face_index // CELL_SLOT_LIMIT
    element = face_index % CELL_SLOT_LIMIT
    alive = element < counts[:, None]
    rank = (element + shifts[:, None]) % counts[:, None]
    order = rank * 4 + side
    direction = jnp.minimum(jnp.sum((order[:, :, None] >= ends[:, None, :]).astype(jnp.int32), axis=2), 7)
    slot = order - jnp.take_along_axis(starts, direction, axis=1)
    remote = order < total[:, None]
    kind = jax.random.randint(kind_key, shape, 0, 20)
    local_side = jax.random.randint(side_key, shape, 0, 4)
    local_member = jax.random.randint(member_key, shape, 0, jnp.broadcast_to(counts[:, None], shape))
    local_code = 8 * BSLOT + local_side * CELL_SLOT_LIMIT + local_member
    code = jnp.where(remote, direction * BSLOT + slot, jnp.where(kind < 18, local_code, -1))
    code = jnp.where(alive, code, -1)
    top_face = (device_rows == chosen) & (side == 3) & (rank == counts[:, None] - 1)
    code = jnp.where(top_face, 8 * BSLOT + 4 * CELL_SLOT_LIMIT - 1, code)
    return code.reshape(-1).astype(jnp.int32)


def draw_face_normal(key, part):
    key = jax.random.fold_in(key, 13)
    height_key, angle_key = jax.random.split(key)
    height = jax.random.uniform(height_key, (4 * NE,), jnp.float32, -1.0, 1.0)
    azimuth = jax.random.uniform(angle_key, (4 * NE,), jnp.float32, -math.pi, math.pi)
    radial = jnp.sqrt(jnp.maximum(1.0 - height * height, 0.0))
    return jnp.stack([radial * jnp.cos(azimuth), radial * jnp.sin(azimuth), height]).astype(jnp.float32)


def draw_inverse_table(key, part):
    key = jax.random.fold_in(key, 17)
    diagonal_key, spread_key = jax.random.split(key)
    diagonal = jnp.exp(jax.random.uniform(diagonal_key, (CLASSES, UNK), jnp.float32, math.log(0.5), math.log(2.0)))
    spread = jax.random.normal(spread_key, (CLASSES, UNK, UNK), jnp.float32) * (0.4 / math.sqrt(UNK))
    identity = jnp.eye(UNK, dtype=jnp.float32)
    table = spread + identity[None, :, :] * diagonal[:, :, None]
    return table.astype(jnp.bfloat16)


def with_ends(values, stream_key, least, largest):
    longest = values.shape.index(max(values.shape))
    spots = []
    for shift in (0, 1):
        where = [jax.random.randint(jax.random.fold_in(stream_key, axis), (), 0, length) for axis, length in enumerate(values.shape)]
        where[longest] = (where[longest] + shift) % values.shape[longest]
        spots.append(tuple(where))
    return values.at[spots[0]].set(least).at[spots[1]].set(largest)


def block_scale(key, dims, pieces, low, largest):
    def one(dim, parts):
        draws = jax.random.uniform(jax.random.fold_in(jax.random.fold_in(key, 6), dim), (parts,), jnp.float32, low / len(pieces), largest / len(pieces))
        return jnp.repeat(jnp.exp(draws), dims[dim] // parts).reshape((-1,) + (1,) * (len(dims) - dim - 1))

    factor_of = one(*pieces[0])
    for cut in pieces[1:]:
        factor_of = factor_of * one(*cut)
    return factor_of


def setup_inputs(seed: int = 0) -> dict:
    splits = jax.random.split(jax.random.key(seed), 11)
    right_side = draw_right_side(jax.random.fold_in(splits[10], 71), 0)
    part_count = draw_part_count(jax.random.fold_in(splits[10], 71), 0)
    elem_class = with_ends(jax.random.randint(splits[2], (NE,), 0, CLASSES), jax.random.fold_in(splits[2], 1), 0, CLASSES - 1).astype(jnp.int32)
    face_link = draw_face_link(jax.random.fold_in(splits[10], 71), 0)
    face_orient = with_ends(jax.random.randint(splits[4], (4 * NE,), 0, 6), jax.random.fold_in(splits[4], 1), 0, 5).astype(jnp.int32)
    face_normal = draw_face_normal(jax.random.fold_in(splits[10], 71), 0)
    boundary_metric_quotient = jnp.clip(jnp.exp(math.log(2.0) - 1.3862944 * jax.random.uniform(splits[6], (4 * NE,), jnp.float32) ** block_scale(splits[6], (4 * NE,), ((0, 128),), -0.2, 0.2)), 0.5, 2.0)
    bound_face = draw_bound_face(jax.random.fold_in(splits[10], 71), 0)
    lift = draw_lift(jax.random.fold_in(splits[10], 71), 0)
    inverse_table = draw_inverse_table(jax.random.fold_in(splits[10], 71), 0)
    return {"right_side": right_side, "part_count": part_count, "elem_class": elem_class, "face_link": face_link, "face_orient": face_orient, "face_normal": face_normal, "boundary_metric_quotient": boundary_metric_quotient, "bound_face": bound_face, "lift": lift, "inverse_table": inverse_table}


EPSILON = 1e-06
PERMUTATIONS = ((0, 1, 2), (0, 2, 1), (1, 0, 2), (1, 2, 0), (2, 0, 1), (2, 1, 0))
OFFSETS = tuple(((direction // 3 - 1, direction % 3 - 1) for direction in (0, 1, 2, 3, 5, 6, 7, 8)))

def trace_tables():
    element_points = [(coord_a, coord_b, coord_c, 3 - coord_a - coord_b - coord_c) for coord_a in range(4) for coord_b in range(4 - coord_a) for coord_c in range(4 - coord_a - coord_b)]
    face_points = [(coord_a, coord_b, 3 - coord_a - coord_b) for coord_a in range(4) for coord_b in range(4 - coord_a)]
    select_rows = []
    for opposite in range(4):
        corners = [vertex for vertex in range(4) if vertex != opposite]
        members = []
        for triple in face_points:
            coords = [0, 0, 0, 0]
            for position in range(3):
                coords[corners[position]] = triple[position]
            members.append(element_points.index(tuple(coords)))
        select_rows.append([component * 20 + members[position] for component in range(6) for position in range(10)])
    turn_rows = [[face_points.index((triple[sigma_row[0]], triple[sigma_row[1]], triple[sigma_row[2]])) for triple in face_points] for sigma_row in PERMUTATIONS]
    return (np.array(select_rows, np.int32), np.array(turn_rows, np.int32))

def cross_with(normal, field_part):
    return jnp.stack([normal[1] * field_part[2] - normal[2] * field_part[1], normal[2] * field_part[0] - normal[0] * field_part[2], normal[0] * field_part[1] - normal[1] * field_part[0]])

def upwind_flux(neighbour, normal, scaling):
    fields = neighbour.reshape(6, 10, -1)
    electric = fields[:3]
    magnetic = fields[3:]
    outward = normal[:, None, :]
    along_electric = lax.optimization_barrier(jnp.sum(outward * electric, axis=0))
    along_magnetic = lax.optimization_barrier(jnp.sum(outward * magnetic, axis=0))
    flux_electric = electric - outward * along_electric - cross_with(outward, magnetic)
    flux_magnetic = magnetic - outward * along_magnetic + cross_with(outward, electric)
    return 0.5 * scaling * jnp.concatenate([flux_electric, flux_magnetic], axis=0)

def neighbour_traces(own_traces, incoming_boundary_values, links, turns, turn_rows):
    extended = jnp.concatenate([incoming_boundary_values, own_traces], axis=1)
    picked = jnp.take(extended, jnp.maximum(links, 0), axis=1)
    mirror = jnp.concatenate([-own_traces[:30], own_traces[30:]], axis=0)
    picked = jnp.where(links[None, :] < 0, mirror, picked)
    shaped = picked.reshape(6, 10, -1)
    turned = jnp.zeros_like(shaped)
    for option in range(6):
        turned = turned + jnp.where(turns[None, None, :] == option, shaped[:, turn_rows[option], :], 0.0)
    return turned.reshape(60, -1)

def lift_faces(flux, lift):
    grouped = flux.reshape(6, 10, 4, -1)
    return jnp.einsum('fij,cjfe->cie', lift, grouped, precision=lax.Precision.HIGHEST).reshape(120, -1)

def reference(right_side, part_count, elem_class, face_link, face_orient, face_normal, boundary_metric_quotient, bound_face, lift, inverse_table):
    all_subdomains = N_PROW * N_PCOL
    select_rows, turn_rows = trace_tables()
    field_dev = right_side.reshape(UNK, all_subdomains, CELL_SLOT_LIMIT).transpose(1, 0, 2)
    live_cell_flags = (jnp.arange(CELL_SLOT_LIMIT).astype(jnp.int32)[None, :] < part_count[:, None]).astype(jnp.float32)[:, None, :]
    cell_categories = elem_class.reshape(all_subdomains, CELL_SLOT_LIMIT)
    subdomain_connections = face_link.reshape(all_subdomains, 4 * CELL_SLOT_LIMIT)
    subdomain_rotations = face_orient.reshape(all_subdomains, 4 * CELL_SLOT_LIMIT)
    boundary_unit_directions = face_normal.reshape(3, all_subdomains, 4 * CELL_SLOT_LIMIT).transpose(1, 0, 2)
    boundary_weight_factors = boundary_metric_quotient.reshape(all_subdomains, 4 * CELL_SLOT_LIMIT)
    list_flat = bound_face.reshape(all_subdomains, 8 * BSLOT)

    def lone_subdomain(device_items):
        vector, own_traces, received_dev, link_row, turn_row, normal, scaling, class_row, live_row = device_items
        neighbour = neighbour_traces(own_traces, received_dev, link_row, turn_row, turn_rows)
        coupled = lift_faces(upwind_flux(neighbour, normal, scaling), lift).astype(jnp.bfloat16)
        blocks = jnp.take(inverse_table, class_row, axis=0).astype(jnp.float32)
        applied = jnp.einsum('eij,je->ie', blocks, coupled.astype(jnp.float32), precision=lax.Precision.HIGHEST)
        return vector + live_row * applied

    def operator(subspace_basis_columns):
        held_by_all_subdomains = subspace_basis_columns[:, select_rows, :].transpose(0, 2, 1, 3).reshape(all_subdomains, 60, 4 * CELL_SLOT_LIMIT)
        kept_index = jnp.maximum(list_flat, 0)
        sent_traces = jnp.take_along_axis(held_by_all_subdomains, kept_index[:, None, :], axis=2) * (list_flat >= 0)[:, None, :].astype(jnp.float32)
        layout = sent_traces.reshape(N_PROW, N_PCOL, 60, 8, BSLOT)
        padded = jnp.pad(layout, ((1, 1), (1, 1), (0, 0), (0, 0), (0, 0)))
        windows = []
        for direction_index in range(8):
            row_off, col_off = OFFSETS[direction_index]
            windows.append(padded[1 + row_off:1 + row_off + N_PROW, 1 + col_off:1 + col_off + N_PCOL, :, 7 - direction_index, :])
        incoming_boundary_values = jnp.stack(windows, axis=3).reshape(all_subdomains, 60, 8 * BSLOT)
        return lax.map(lone_subdomain, (subspace_basis_columns, held_by_all_subdomains, incoming_boundary_values, subdomain_connections, subdomain_rotations, boundary_unit_directions, boundary_weight_factors, cell_categories, live_cell_flags))

    def inner(left_vec, right_vec):
        return jnp.sum(left_vec * right_vec) / (UNK * NE)
    first_vec = field_dev * live_cell_flags
    scale_now = jnp.sqrt(inner(first_vec, first_vec) + EPSILON)
    basis_list = [first_vec / scale_now]
    columns = []
    for step_index in range(2):
        image_vec = operator(basis_list[step_index])
        coefficients = [inner(earlier, image_vec) for earlier in basis_list]
        remainder = image_vec
        for earlier_index in range(len(basis_list)):
            remainder = remainder - coefficients[earlier_index] * basis_list[earlier_index]
        scale_now = jnp.sqrt(inner(remainder, remainder) + EPSILON)
        columns.append((coefficients, scale_now))
        basis_list.append(remainder / scale_now)
    first_col, second_col = columns
    zero_entry = jnp.zeros((), jnp.float32)
    hess = jnp.stack([jnp.stack([first_col[0][0], second_col[0][0]]), jnp.stack([first_col[1], second_col[0][1]]), jnp.stack([zero_entry, second_col[1]])])
    basis = jnp.stack([vector.transpose(1, 0, 2).reshape(UNK, NE) for vector in basis_list])
    return (basis, hess)
```

```python
import jax
import jax.numpy as jnp
import numpy as np
from jax import lax
from jax.sharding import PartitionSpec as P

EPSILON = 1e-06
PERMUTATIONS = ((0, 1, 2), (0, 2, 1), (1, 0, 2), (1, 2, 0), (2, 0, 1), (2, 1, 0))
OFFSETS = tuple(((direction // 3 - 1, direction % 3 - 1) for direction in (0, 1, 2, 3, 5, 6, 7, 8)))


def passed_along(value, axis, steps):
    count = lax.axis_size(axis)
    leading, last = (max(0, -steps), min(count, count - steps))
    return lax.ppermute(value, axis, [(source, source + steps) for source in range(leading, last)])


def trace_tables():
    element_points = [
        (coord_a, coord_b, coord_c, 3 - coord_a - coord_b - coord_c)
        for coord_a in range(4)
        for coord_b in range(4 - coord_a)
        for coord_c in range(4 - coord_a - coord_b)
    ]
    face_points = [
        (coord_a, coord_b, 3 - coord_a - coord_b)
        for coord_a in range(4)
        for coord_b in range(4 - coord_a)
    ]
    select_rows = []
    for opposite in range(4):
        corners = [vertex for vertex in range(4) if vertex != opposite]
        members = []
        for triple in face_points:
            coords = [0, 0, 0, 0]
            for position in range(3):
                coords[corners[position]] = triple[position]
            members.append(element_points.index(tuple(coords)))
        select_rows.append(
            [component * 20 + members[position] for component in range(6) for position in range(10)]
        )
    turn_rows = [
        [
            face_points.index((triple[sigma_row[0]], triple[sigma_row[1]], triple[sigma_row[2]]))
            for triple in face_points
        ]
        for sigma_row in PERMUTATIONS
    ]
    return (np.array(select_rows, np.int32), np.array(turn_rows, np.int32))


def turn_matrices(turn_rows):
    tables = np.zeros((6, 10, 10), np.float32)
    for option in range(6):
        for position in range(10):
            tables[option, position, turn_rows[option][position]] = 1.0
    return tables


def cross_with(normal, field_part):
    return jnp.stack(
        [
            normal[1] * field_part[2] - normal[2] * field_part[1],
            normal[2] * field_part[0] - normal[0] * field_part[2],
            normal[0] * field_part[1] - normal[1] * field_part[0],
        ]
    )


def upwind_flux(neighbour, normal, scaling):
    fields = neighbour.reshape(6, 10, -1)
    electric = fields[:3]
    magnetic = fields[3:]
    outward = normal[:, None, :]
    along_electric = jnp.sum(outward * electric, axis=0)
    along_magnetic = jnp.sum(outward * magnetic, axis=0)
    flux_electric = electric - outward * along_electric - cross_with(outward, magnetic)
    flux_magnetic = magnetic - outward * along_magnetic + cross_with(outward, electric)
    return 0.5 * scaling * jnp.concatenate([flux_electric, flux_magnetic], axis=0)


def neighbour_traces(own_traces, incoming_boundary_values, links, turns, turn_tables):
    extended = jnp.concatenate([incoming_boundary_values, own_traces], axis=1)
    picked = jnp.take(extended, jnp.maximum(links, 0), axis=1)
    mirror = jnp.concatenate([-own_traces[:30], own_traces[30:]], axis=0)
    picked = jnp.where(links[None, :] < 0, mirror, picked)
    shaped = picked.reshape(6, 10, -1)
    turned = jnp.zeros_like(shaped)
    for option in range(6):
        rotated = jnp.einsum(
            "jk,ckf->cjf", turn_tables[option], shaped, precision=lax.Precision.HIGHEST
        )
        turned = turned + jnp.where(turns[None, None, :] == option, rotated, 0.0)
    return turned.reshape(60, -1)


def lift_faces(flux, lift):
    grouped = flux.reshape(6, 10, 4, -1)
    return jnp.einsum("fij,cjfe->cie", lift, grouped, precision=lax.Precision.HIGHEST).reshape(
        120, -1
    )


def precondition(coupled, cell_categories, inverse_table):
    unknowns, elements = coupled.shape
    block_size = min(256, elements)
    block_count = elements // block_size

    def one_block(block_index, result):
        first_col = block_index * block_size
        block_class = lax.dynamic_slice_in_dim(cell_categories, first_col, block_size)
        columns = lax.dynamic_slice_in_dim(coupled, first_col, block_size, 1)
        gathered = jnp.take(inverse_table, block_class, axis=0)
        product = jnp.einsum("eij,je->ie", gathered, columns, preferred_element_type=jnp.float32)
        return lax.dynamic_update_slice_in_dim(result, product, first_col, 1)

    empty = jnp.zeros((unknowns, elements), jnp.float32)
    return lax.fori_loop(0, block_count, one_block, empty)


def route_lists(outgoing):
    arrived = [None] * 8
    for index in range(8):
        row_step, col_step = OFFSETS[index]
        value = outgoing[:, 7 - index]
        if row_step != 0:
            value = passed_along(value, "prow", -row_step)
        if col_step != 0:
            value = passed_along(value, "pcol", -col_step)
        arrived[index] = value
    return jnp.stack(arrived, axis=1)


def shards(
    right_side,
    part_count,
    elem_class,
    face_link,
    face_orient,
    face_normal,
    boundary_metric_quotient,
    bound_face,
    lift,
    inverse_table,
):
    unknowns, elements = right_side.shape
    all_subdomains = lax.axis_size("prow") * lax.axis_size("pcol")
    weight = 1.0 / (unknowns * elements * all_subdomains)
    select_rows, turn_rows = trace_tables()
    trace_index = select_rows.T.reshape(-1)
    turn_tables = turn_matrices(turn_rows)
    live_cell_flags = (jnp.arange(elements) < part_count[0]).astype(jnp.float32)[None, :]
    lists = bound_face[0]
    list_slots = lists.shape[1]
    flat_lists = lists.reshape(-1)
    list_mask = (flat_lists >= 0)[None, :].astype(jnp.float32)

    def coupled_image(vector):
        own_traces = vector[trace_index].reshape(60, 4 * elements)
        outgoing = (jnp.take(own_traces, jnp.maximum(flat_lists, 0), axis=1) * list_mask).reshape(
            60, 8, list_slots
        )
        incoming_boundary_values = route_lists(outgoing).reshape(60, 8 * list_slots)
        neighbour = neighbour_traces(
            own_traces, incoming_boundary_values, face_link, face_orient, turn_tables
        )
        coupled = lift_faces(upwind_flux(neighbour, face_normal, boundary_metric_quotient), lift)
        return live_cell_flags * precondition(coupled.astype(jnp.bfloat16), elem_class, inverse_table)

    def local_inner(left_vec, right_vec):
        return jnp.sum(left_vec * right_vec) * weight

    first = right_side * live_cell_flags
    second = coupled_image(first)
    third = coupled_image(second)
    gram = lax.psum(
        jnp.stack(
            [
                local_inner(first, first),
                local_inner(first, second),
                local_inner(second, second),
                local_inner(first, third),
                local_inner(second, third),
                local_inner(third, third),
            ]
        ),
        ("prow", "pcol"),
    )
    ff, ft, tt, fu, tu, uu = (gram[index] for index in range(6))
    beta = jnp.sqrt(ff + EPSILON)
    h00 = (ff + ft) / (beta * beta)
    p = (EPSILON - ft) / (beta * beta)
    h10 = jnp.sqrt((tt + 2 * p * ft + p * p * ff) / (beta * beta) + EPSILON)
    k1 = 1.0 / (beta * h10)
    h01 = k1 / beta * (fu + (1 + p) * ft + p * ff)
    h11 = k1 * k1 * (tu + (1 + p) * tt + p * ft + p * fu + p * (1 + p) * ft + p * p * ff)
    q = 1 + p - h11
    w = p * (1 - h11) - h01 * h10
    h21 = jnp.sqrt(
        k1 * k1 * (uu + 2 * q * tu + 2 * w * fu + q * q * tt + 2 * q * w * ft + w * w * ff) + EPSILON
    )
    k2 = k1 / h21
    basis = jnp.stack(
        [
            first * (1.0 / beta),
            second * k1 + first * (p * k1),
            third * k2 + second * (q * k2) + first * (w * k2),
        ]
    )
    zero_entry = jnp.zeros((), jnp.float32)
    hess = jnp.stack(
        [jnp.stack([h00, h01]), jnp.stack([h10, h11]), jnp.stack([zero_entry, h21])]
    )
    return (basis, hess)


def solution(mesh):
    in_specs = (
        P(None, ("prow", "pcol")),
        P(("prow", "pcol")),
        P(("prow", "pcol")),
        P(("prow", "pcol")),
        P(("prow", "pcol")),
        P(None, ("prow", "pcol")),
        P(("prow", "pcol")),
        P(("prow", "pcol"), None, None),
        P(),
        P(),
    )
    out_specs = (P(None, None, ("prow", "pcol")), P())
    return jax.shard_map(shards, mesh=mesh, in_specs=in_specs, out_specs=out_specs, check_vma=False)
```

```python
import functools

import jax
import jax.numpy as jnp
import numpy as np
from jax import lax
from jax.experimental import pallas as pl
from jax.experimental.pallas import tpu as pltpu
from jax.sharding import PartitionSpec as P

EPSILON = 1e-06
PERMUTATIONS = ((0, 1, 2), (0, 2, 1), (1, 0, 2), (1, 2, 0), (2, 0, 1), (2, 1, 0))
OFFSETS = tuple(((direction // 3 - 1, direction % 3 - 1) for direction in (0, 1, 2, 3, 5, 6, 7, 8)))
MESH = pl.DeviceIdType.MESH
F32, BF16, I32 = jnp.float32, jnp.bfloat16, jnp.int32
VMEM_LIMIT = 48 * 1024 * 1024
UNK, CLASSES, LANES = 120, 256, 128
TILE = 16
COMP = 16
SIDE = 6 * COMP
LANE_BLOCK = 256


def trace_tables():
    element_points = [
        (coord_a, coord_b, coord_c, 3 - coord_a - coord_b - coord_c)
        for coord_a in range(4)
        for coord_b in range(4 - coord_a)
        for coord_c in range(4 - coord_a - coord_b)
    ]
    face_points = [
        (coord_a, coord_b, 3 - coord_a - coord_b)
        for coord_a in range(4)
        for coord_b in range(4 - coord_a)
    ]
    select_rows = []
    for opposite in range(4):
        corners = [vertex for vertex in range(4) if vertex != opposite]
        members = []
        for triple in face_points:
            coords = [0, 0, 0, 0]
            for position in range(3):
                coords[corners[position]] = triple[position]
            members.append(element_points.index(tuple(coords)))
        select_rows.append(members)
    turn_rows = [
        [
            face_points.index((triple[sigma_row[0]], triple[sigma_row[1]], triple[sigma_row[2]]))
            for triple in face_points
        ]
        for sigma_row in PERMUTATIONS
    ]
    return select_rows, turn_rows


def trace_selector():
    select_rows, _ = trace_tables()
    table = np.zeros((2 * LANES, 4 * LANES), np.float32)
    for side in range(4):
        for half in range(2):
            for c in range(6):
                for j in range(10):
                    column = side * LANES + half * 64 + c * 10 + j
                    table[c * 20 + select_rows[side][j], column] = 1.0
                    table[LANES + c * 20 + select_rows[side][j], column] = 1.0
    return table


def turn_selector():
    _, turn_rows = trace_tables()
    table = np.zeros((2, 6, SIDE, 2 * LANES), np.float32)
    for half in range(2):
        for option in range(6):
            for c in range(6):
                for j in range(10):
                    source = half * 64 + c * 10 + turn_rows[option][j]
                    table[half, option, c * COMP + j, source] = 1.0
                    table[half, option, c * COMP + j, LANES + source] = 1.0
    return table.reshape(2 * 6 * SIDE, 2 * LANES)


def lift_spreaders():
    rows = np.zeros((LANES, 20), np.float32)
    columns = np.zeros((4, 10, 4 * SIDE), np.float32)
    mask = np.zeros((LANES, 4 * SIDE), np.float32)
    for c in range(6):
        for i in range(20):
            rows[c * 20 + i, i] = 1.0
        for s in range(4):
            for j in range(10):
                columns[s, j, s * SIDE + c * COMP + j] = 1.0
            mask[c * 20 : c * 20 + 20, s * SIDE + c * COMP : s * SIDE + (c + 1) * COMP] = 1.0
    return rows, columns, mask


def split(value):
    high = value.astype(BF16)
    return high, (value - high.astype(F32)).astype(BF16)


def dot(a, b, dims=(((1,), (0,)), ((), ()))):
    return lax.dot_general(a, b, dims, preferred_element_type=F32)


NT = (((1,), (1,)), ((), ()))


def live_lanes(count, first, width):
    return ((lax.broadcasted_iota(I32, (1, width), 1) + first) < count).astype(F32)


def prep_kernel(
    count_ref, field_ref, class_ref, lift_ref, spread_ref, column_ref, mask_ref,
    rows_ref, pos_ref, tile_ref, lift_hi_ref, lift_lo_ref,
):
    elements = field_ref.shape[1]
    blocks = elements // LANES
    count = count_ref[0]
    for block in range(blocks):
        lanes = slice(block * LANES, (block + 1) * LANES)
        value = field_ref[:, lanes] * live_lanes(count, block * LANES, LANES)
        value = jnp.concatenate([value, jnp.zeros((LANES - UNK, LANES), F32)], axis=0)
        rows_ref[lanes, :] = value.T

    class_row = lax.broadcasted_iota(I32, (CLASSES, LANES), 0)
    totals = jnp.zeros((CLASSES, LANES), F32)
    for block in range(blocks):
        totals = totals + (class_ref[block : block + 1, :] == class_row).astype(F32)
    total = jnp.sum(totals, axis=1, keepdims=True)
    tiles = jnp.floor((total + (TILE - 1)) * (1.0 / TILE))
    tiles = jnp.broadcast_to(tiles, (CLASSES, LANES))
    lower = (
        lax.broadcasted_iota(I32, (CLASSES, CLASSES), 1)
        < lax.broadcasted_iota(I32, (CLASSES, CLASSES), 0)
    ).astype(BF16)
    start = dot(lower, tiles.astype(BF16))
    end = start + tiles
    earlier = (
        lax.broadcasted_iota(I32, (LANES, 2 * LANES), 0)
        < lax.broadcasted_iota(I32, (LANES, 2 * LANES), 1)
    ).astype(BF16)
    carry = start * TILE
    for block in range(blocks):
        member = (class_ref[block : block + 1, :] == class_row).astype(F32)
        ranks = dot(member.astype(BF16), earlier)
        position = jnp.sum(member * (ranks[:, :LANES] + carry), axis=0, keepdims=True)
        pos_ref[block : block + 1, :] = position.astype(I32)
        carry = carry + ranks[:, LANES:]
    for row in range(3):
        tile = (lax.broadcasted_iota(I32, (CLASSES, LANES), 1) + row * LANES).astype(F32)
        owner = jnp.sum((end <= tile).astype(F32), axis=0, keepdims=True)
        tile_ref[row : row + 1, :] = jnp.minimum(owner.astype(I32), CLASSES - 1)
    tile_ref[3:4, :] = end[CLASSES - 1 :, :].astype(I32)
    tile_ref[4:, :] = jnp.zeros((4, LANES), I32)

    spread = jnp.zeros((LANES, 4 * SIDE), F32)
    for side in range(4):
        rows = lax.dot_general(
            spread_ref[...], lift_ref[side], (((1,), (0,)), ((), ())),
            precision=lax.Precision.HIGHEST, preferred_element_type=F32,
        )
        spread = spread + lax.dot_general(
            rows, column_ref[side], (((1,), (0,)), ((), ())),
            precision=lax.Precision.HIGHEST, preferred_element_type=F32,
        )
    high, low = split(spread * mask_ref[...])
    lift_hi_ref[...] = high
    lift_lo_ref[...] = low


def prepare(part_count, right_side, elem_class, lift):
    elements = right_side.shape[1]
    rows, columns, mask = lift_spreaders()
    vmem = pl.BlockSpec(memory_space=pltpu.VMEM)
    return pl.pallas_call(
        prep_kernel,
        out_shape=(
            jax.ShapeDtypeStruct((elements, LANES), F32),
            jax.ShapeDtypeStruct((elements // LANES, LANES), I32),
            jax.ShapeDtypeStruct((8, LANES), I32),
            jax.ShapeDtypeStruct((LANES, 4 * SIDE), BF16),
            jax.ShapeDtypeStruct((LANES, 4 * SIDE), BF16),
        ),
        in_specs=[pl.BlockSpec(memory_space=pltpu.SMEM)] + [vmem] * 6,
        out_specs=(vmem,) * 5,
        compiler_params=pltpu.CompilerParams(vmem_limit_bytes=VMEM_LIMIT),
        name="prepare",
    )(
        part_count, right_side, elem_class.reshape(elements // LANES, LANES), lift,
        jnp.asarray(rows), jnp.asarray(columns), jnp.asarray(mask),
    )


def write_traces(rows_ref, selector_ref, table_ref, first):
    elements = rows_ref.shape[0]

    def block(index, carry):
        base = pl.multiple_of(index * LANES, LANES)
        high, low = split(rows_ref[pl.ds(base, LANES), :])
        traces = dot(jnp.concatenate([high, low], axis=1), selector_ref[...])
        for side in range(4):
            table_ref[pl.ds(first + side * elements + base, LANES), :] = traces[
                :, side * LANES : (side + 1) * LANES
            ]
        return carry

    lax.fori_loop(0, elements // LANES, block, 0)


def gather_pairs(table_ref, index_ref, out_ref, first_a, first_b, out_first, count):
    left = lax.broadcasted_iota(I32, (1, LANES), 1) < 64
    unroll = 16

    def block(index, carry):
        base = pl.multiple_of(index * unroll, unroll)
        for step in range(unroll):
            row_a = table_ref[pl.ds(index_ref[first_a + base + step], 1), :]
            row_b = table_ref[pl.ds(index_ref[first_b + base + step], 1), :]
            out_ref[pl.ds(out_first + base + step, 1), :] = jnp.where(left, row_a, row_b)
        return carry

    lax.fori_loop(0, count // unroll, block, 0)


def exchange_kernel(
    grid_rows, grid_columns, rows_ref, selector_ref, list_ref, received_ref,
    table_ref, outgoing_ref, send_sem, recv_sem,
):
    slots = outgoing_ref.shape[1]
    row, column = lax.axis_index("prow"), lax.axis_index("pcol")

    def present(index):
        a, b = OFFSETS[index]
        inside = None
        for at, step, size in ((row, a, grid_rows), (column, b, grid_columns)):
            if step == 0:
                continue
            term = at > 0 if step < 0 else at < size - 1
            inside = term if inside is None else jnp.logical_and(inside, term)
        return inside

    def partner(index):
        a, b = OFFSETS[index]
        return (row + a, column + b)

    def transfer(index):
        return pltpu.make_async_remote_copy(
            src_ref=outgoing_ref.at[index],
            dst_ref=received_ref.at[7 - index],
            send_sem=send_sem.at[index],
            recv_sem=recv_sem.at[7 - index],
            device_id=partner(index),
            device_id_type=MESH,
        )

    barrier = pltpu.get_barrier_semaphore()
    for index in range(8):
        @pl.when(present(index))
        def _(index=index):
            pl.semaphore_signal(barrier, inc=1, device_id=partner(index), device_id_type=MESH)

    write_traces(rows_ref, selector_ref, table_ref, 0)

    near_rows = 1 + (row > 0).astype(I32) + (row < grid_rows - 1).astype(I32)
    near_columns = 1 + (column > 0).astype(I32) + (column < grid_columns - 1).astype(I32)
    pl.semaphore_wait(barrier, near_rows * near_columns - 1)

    for index in (0, 2, 5, 7, 3, 4, 1, 6):
        first = index * 2 * slots
        gather_pairs(
            table_ref, list_ref, outgoing_ref.at[index], first, first + slots, 0, slots
        )

        @pl.when(present(index))
        def _(index=index):
            transfer(index).start()

    for index in range(8):
        @pl.when(present(index))
        def _(index=index):
            transfer(index).wait_send()
            transfer(7 - index).wait_recv()


def exchange(rows, selector, lists):
    slots = lists.shape[0] // 16
    vmem = pl.BlockSpec(memory_space=pltpu.VMEM)
    return pl.pallas_call(
        functools.partial(exchange_kernel, lax.axis_size("prow"), lax.axis_size("pcol")),
        out_shape=jax.ShapeDtypeStruct((8, slots, LANES), F32),
        in_specs=[vmem, vmem, pl.BlockSpec(memory_space=pltpu.SMEM)],
        out_specs=vmem,
        scratch_shapes=[
            pltpu.VMEM((4 * rows.shape[0], LANES), F32),
            pltpu.VMEM((8, slots, LANES), F32),
            pltpu.SemaphoreType.DMA((8,)),
            pltpu.SemaphoreType.DMA((8,)),
        ],
        compiler_params=pltpu.CompilerParams(
            collective_id=0, has_side_effects=True, vmem_limit_bytes=VMEM_LIMIT
        ),
        name="exchange",
    )(rows, selector, lists)


def face_flux(nodes, normal, scale, sign):
    electric = [nodes[c * COMP : (c + 1) * COMP] * sign for c in range(3)]
    magnetic = [nodes[(3 + c) * COMP : (4 + c) * COMP] for c in range(3)]
    along_e = normal[0] * electric[0] + normal[1] * electric[1] + normal[2] * electric[2]
    along_h = normal[0] * magnetic[0] + normal[1] * magnetic[1] + normal[2] * magnetic[2]
    flux = []
    for c in range(3):
        a, b = (c + 1) % 3, (c + 2) % 3
        cross = normal[a] * magnetic[b] - normal[b] * magnetic[a]
        flux.append(scale * (electric[c] - normal[c] * along_e - cross))
    for c in range(3):
        a, b = (c + 1) % 3, (c + 2) % 3
        cross = normal[a] * electric[b] - normal[b] * electric[a]
        flux.append(scale * (magnetic[c] - normal[c] * along_h + cross))
    return jnp.concatenate(flux, axis=0)


def image_kernel(
    count_ref, index_ref, pos_ref, tile_ref,
    rows_ref, received_ref, selector_ref, turn_ref, lift_hi_ref, lift_lo_ref,
    link_ref, orient_ref, normal_ref, quotient_ref, inverse_hbm,
    image_ref,
    table_ref, picked_ref, coupled_ref, sorted_ref, solved_ref, inverse_ref, inverse_sem,
):
    elements = rows_ref.shape[0]
    remote = received_ref.shape[0] * 2
    inverse_copy = pltpu.make_async_copy(inverse_hbm, inverse_ref, inverse_sem)
    inverse_copy.start()

    write_traces(rows_ref, selector_ref, table_ref, remote)

    slots = remote // 16
    left = lax.broadcasted_iota(I32, (slots, LANES), 1) < 64
    for index in range(8):
        packed = received_ref[index * slots : (index + 1) * slots, :]
        swapped = pltpu.roll(packed, 64, 1)
        first = index * 2 * slots
        table_ref[first : first + slots, :] = jnp.where(left, packed, swapped)
        table_ref[first + slots : first + 2 * slots, :] = jnp.where(left, swapped, packed)

    gather_pairs(table_ref, index_ref, picked_ref, 0, 2 * elements, 0, 2 * elements)

    count = count_ref[0]

    def lane_block(index, carry):
        base = pl.multiple_of(index * LANE_BLOCK, LANE_BLOCK)
        alive = ((lax.broadcasted_iota(I32, (1, LANE_BLOCK), 1) + base) < count).astype(F32)
        fluxes = [None] * 4
        for pair in range(2):
            high, low = split(picked_ref[pl.ds(pair * elements + base, LANE_BLOCK), :])
            stacked = jnp.concatenate([high, low], axis=1)
            for half in range(2):
                side = pair + 2 * half
                lanes = pl.ds(side * elements + base, LANE_BLOCK)
                turned = dot(turn_ref[half * 6 * SIDE : (half + 1) * 6 * SIDE, :], stacked, NT)
                orient = orient_ref[:, lanes]
                nodes = turned[:SIDE]
                for option in range(1, 6):
                    nodes = jnp.where(
                        orient == option, turned[option * SIDE : (option + 1) * SIDE], nodes
                    )
                scale = 0.5 * quotient_ref[:, lanes] * alive
                sign = jnp.where(link_ref[:, lanes] < 0, -1.0, 1.0)
                normal = [normal_ref[c : c + 1, lanes] for c in range(3)]
                fluxes[side] = face_flux(nodes, normal, scale, sign)
        high, low = split(jnp.concatenate(fluxes, axis=0))
        coupled = dot(lift_hi_ref[...], high) + dot(lift_hi_ref[...], low) + dot(lift_lo_ref[...], high)
        coupled_ref[pl.ds(base, LANE_BLOCK), :] = coupled.T
        return carry

    lax.fori_loop(0, elements // LANE_BLOCK, lane_block, 0)

    unroll = 16

    def place(index, carry):
        base = pl.multiple_of(index * unroll, unroll)
        for step in range(unroll):
            sorted_ref[pl.ds(pos_ref[base + step], 1), :] = coupled_ref[pl.ds(base + step, 1), :]
        return carry

    lax.fori_loop(0, elements // unroll, place, 0)
    inverse_copy.wait()

    def solve(index, carry):
        base = pl.multiple_of(index * TILE, TILE)
        high, low = split(sorted_ref[pl.ds(base, TILE), :])
        both = jnp.concatenate([high, low], axis=0)[:, :UNK]
        result = dot(both, inverse_ref[tile_ref[index]], NT)
        solved_ref[pl.ds(base, TILE), :UNK] = result[:TILE] + result[TILE:]
        return carry

    group = 4
    groups = (tile_ref[3 * LANES] + (group - 1)) // group

    def solve_group(index, carry):
        for step in range(group):
            solve(index * group + step, 0)
        return carry

    lax.fori_loop(0, groups, solve_group, 0)

    keep = lax.broadcasted_iota(I32, (1, LANES), 1) < UNK

    def fetch(index, carry):
        base = pl.multiple_of(index * unroll, unroll)
        for step in range(unroll):
            value = solved_ref[pl.ds(pos_ref[base + step], 1), :]
            image_ref[pl.ds(base + step, 1), :] = jnp.where(keep, value, 0.0)
        return carry

    lax.fori_loop(0, elements // unroll, fetch, 0)


def image(part_count, indices, pos, tiles, rows, received, selector, turns, lift_hi, lift_lo,
          link, orient, normal, quotient, inverse_table):
    elements = rows.shape[0]
    remote = received.shape[0] * received.shape[1] * 2
    slots = 3 * LANES * TILE
    vmem = pl.BlockSpec(memory_space=pltpu.VMEM)
    smem = pl.BlockSpec(memory_space=pltpu.SMEM)
    return pl.pallas_call(
        image_kernel,
        out_shape=jax.ShapeDtypeStruct((elements, LANES), F32),
        in_specs=[smem] * 4 + [vmem] * 10 + [pl.BlockSpec(memory_space=pl.ANY)],
        out_specs=vmem,
        scratch_shapes=[
            pltpu.VMEM((remote + 4 * elements, LANES), F32),
            pltpu.VMEM((2 * elements, LANES), F32),
            pltpu.VMEM((elements, LANES), F32),
            pltpu.VMEM((slots, LANES), F32),
            pltpu.VMEM((slots, LANES), F32),
            pltpu.VMEM(inverse_table.shape, BF16),
            pltpu.SemaphoreType.DMA(()),
        ],
        compiler_params=pltpu.CompilerParams(vmem_limit_bytes=VMEM_LIMIT),
        name="image",
    )(
        part_count, indices, pos, tiles, rows, received.reshape(-1, LANES), selector, turns,
        lift_hi, lift_lo, link.reshape(1, -1), orient.reshape(1, -1), normal,
        quotient.reshape(1, -1), inverse_table,
    )


def gram_kernel(first_ref, second_ref, third_ref, second_out, third_out, gram_ref):
    elements = first_ref.shape[0]

    def block(index, sums):
        base = pl.multiple_of(index * LANES, LANES)
        lanes = pl.ds(base, LANES)
        f, t, u = first_ref[lanes, :], second_ref[lanes, :], third_ref[lanes, :]
        second_out[:, lanes] = t.T[:UNK]
        third_out[:, lanes] = u.T[:UNK]
        pairs = (f * f, f * t, t * t, f * u, t * u, u * u)
        return tuple(
            total + jnp.sum(pair.reshape(LANES // 8, 8, LANES), axis=0)
            for total, pair in zip(sums, pairs)
        )

    zero = jnp.zeros((8, LANES), F32)
    sums = lax.fori_loop(0, elements // LANES, block, (zero,) * 6)
    for index in range(6):
        gram_ref[index : index + 1, :] = jnp.sum(sums[index], axis=0, keepdims=True)
    gram_ref[6:, :] = jnp.zeros((2, LANES), F32)


def gram_partials(first, second, third):
    elements = first.shape[0]
    vmem = pl.BlockSpec(memory_space=pltpu.VMEM)
    return pl.pallas_call(
        gram_kernel,
        out_shape=(
            jax.ShapeDtypeStruct((UNK, elements), F32),
            jax.ShapeDtypeStruct((UNK, elements), F32),
            jax.ShapeDtypeStruct((8, LANES), F32),
        ),
        in_specs=[vmem] * 3,
        out_specs=(vmem,) * 3,
        compiler_params=pltpu.CompilerParams(vmem_limit_bytes=VMEM_LIMIT),
        name="gram",
    )(first, second, third)


def total_kernel(grid_rows, grid_columns, part_ref, total_ref, over_rows, over_columns,
                 send_row, recv_row, send_column, recv_column):
    row, column = lax.axis_index("prow"), lax.axis_index("pcol")

    def row_partner(step):
        return lax.rem(row + step, grid_rows)

    def column_partner(step):
        return lax.rem(column + step, grid_columns)

    barrier = pltpu.get_barrier_semaphore()
    for step in range(1, grid_rows):
        pl.semaphore_signal(
            barrier, inc=1, device_id=(row_partner(step), column), device_id_type=MESH
        )
    for step in range(1, grid_columns):
        pl.semaphore_signal(
            barrier, inc=1, device_id=(row, column_partner(step)), device_id_type=MESH
        )
    pl.semaphore_wait(barrier, grid_rows + grid_columns - 2)

    def row_copy(step):
        return pltpu.make_async_remote_copy(
            src_ref=part_ref,
            dst_ref=over_rows.at[step],
            send_sem=send_row.at[step],
            recv_sem=recv_row.at[step],
            device_id=(row_partner(step), column),
            device_id_type=MESH,
        )

    for step in range(1, grid_rows):
        row_copy(step).start()
    over_rows[0] = part_ref[...]
    for step in range(1, grid_rows):
        row_copy(step).wait()
    total = over_rows[row]
    for source in range(1, grid_rows):
        total = total + over_rows[lax.rem(row - source + grid_rows, grid_rows)]
    over_columns[0] = total

    def column_copy(step):
        return pltpu.make_async_remote_copy(
            src_ref=over_columns.at[0],
            dst_ref=over_columns.at[step],
            send_sem=send_column.at[step],
            recv_sem=recv_column.at[step],
            device_id=(row, column_partner(step)),
            device_id_type=MESH,
        )

    for step in range(1, grid_columns):
        column_copy(step).start()
    for step in range(1, grid_columns):
        column_copy(step).wait()
    total = over_columns[column]
    for source in range(1, grid_columns):
        total = total + over_columns[lax.rem(column - source + grid_columns, grid_columns)]
    total_ref[...] = total


def total_over_devices(part):
    grid_rows, grid_columns = lax.axis_size("prow"), lax.axis_size("pcol")
    vmem = pl.BlockSpec(memory_space=pltpu.VMEM)
    return pl.pallas_call(
        functools.partial(total_kernel, grid_rows, grid_columns),
        out_shape=jax.ShapeDtypeStruct(part.shape, F32),
        in_specs=[vmem],
        out_specs=vmem,
        scratch_shapes=[
            pltpu.VMEM((grid_rows,) + part.shape, F32),
            pltpu.VMEM((grid_columns,) + part.shape, F32),
            pltpu.SemaphoreType.DMA((grid_rows,)),
            pltpu.SemaphoreType.DMA((grid_rows,)),
            pltpu.SemaphoreType.DMA((grid_columns,)),
            pltpu.SemaphoreType.DMA((grid_columns,)),
        ],
        compiler_params=pltpu.CompilerParams(collective_id=1, has_side_effects=True),
        name="total",
    )(part)


def finish_kernel(weight, count_ref, total_ref, field_ref, second_ref, third_ref, basis_ref, hess_ref):
    width = field_ref.shape[1]
    gram = jnp.sum(total_ref[...], axis=1, keepdims=True) * weight
    ff, ft, tt, fu, tu, uu = (gram[index : index + 1, :] for index in range(6))
    beta = jnp.sqrt(ff + EPSILON)
    square = beta * beta
    h00 = (ff + ft) / square
    p = (EPSILON - ft) / square
    h10 = jnp.sqrt((tt + 2 * p * ft + p * p * ff) / square + EPSILON)
    k1 = 1.0 / (beta * h10)
    h01 = k1 / beta * (fu + (1 + p) * ft + p * ff)
    h11 = k1 * k1 * (tu + (1 + p) * tt + p * ft + p * fu + p * (1 + p) * ft + p * p * ff)
    q = 1 + p - h11
    w = p * (1 - h11) - h01 * h10
    h21 = jnp.sqrt(
        k1 * k1 * (uu + 2 * q * tu + 2 * w * fu + q * q * tt + 2 * q * w * ft + w * w * ff)
        + EPSILON
    )
    k2 = k1 / h21

    alive = live_lanes(count_ref[0], pl.program_id(0) * width, width)
    f = field_ref[...] * alive
    t = second_ref[...]
    basis_ref[0] = f * (1.0 / beta)
    basis_ref[1] = t * k1 + f * (p * k1)
    basis_ref[2] = third_ref[...] * k2 + t * (q * k2) + f * (w * k2)

    at_row = lax.broadcasted_iota(I32, (3, 2), 0)
    at_column = lax.broadcasted_iota(I32, (3, 2), 1)
    hess = jnp.zeros((3, 2), F32)
    for i, j, value in ((0, 0, h00), (1, 0, h10), (0, 1, h01), (1, 1, h11), (2, 1, h21)):
        hess = jnp.where(jnp.logical_and(at_row == i, at_column == j), value, hess)
    hess_ref[...] = hess


def finish(weight, part_count, total, right_side, second, third):
    elements = right_side.shape[1]
    width = 512
    field = pl.BlockSpec((UNK, width), lambda i: (0, i))
    return pl.pallas_call(
        functools.partial(finish_kernel, weight),
        grid=(elements // width,),
        out_shape=(
            jax.ShapeDtypeStruct((3, UNK, elements), F32),
            jax.ShapeDtypeStruct((3, 2), F32),
        ),
        in_specs=[
            pl.BlockSpec(memory_space=pltpu.SMEM),
            pl.BlockSpec((8, LANES), lambda i: (0, 0)),
            field, field, field,
        ],
        out_specs=(
            pl.BlockSpec((3, UNK, width), lambda i: (0, 0, i)),
            pl.BlockSpec((3, 2), lambda i: (0, 0)),
        ),
        compiler_params=pltpu.CompilerParams(vmem_limit_bytes=VMEM_LIMIT),
        name="finish",
    )(part_count, total, right_side, second, third)


def shards(
    right_side,
    part_count,
    elem_class,
    face_link,
    face_orient,
    face_normal,
    boundary_metric_quotient,
    bound_face,
    lift,
    inverse_table,
):
    unknowns, elements = right_side.shape
    all_subdomains = lax.axis_size("prow") * lax.axis_size("pcol")
    weight = 1.0 / (unknowns * elements * all_subdomains)
    lists = jnp.maximum(bound_face.reshape(-1), 0)
    remote = lists.shape[0]
    faces = face_link.shape[0]
    indices = jnp.where(face_link < 0, jnp.arange(faces, dtype=I32) + remote, face_link)
    selector = jnp.asarray(trace_selector(), BF16)
    turns = jnp.asarray(turn_selector(), BF16)

    first, pos, tiles, lift_hi, lift_lo = prepare(part_count, right_side, elem_class, lift)
    pos, tiles = pos.reshape(-1), tiles.reshape(-1)

    def coupled_image(rows):
        received = exchange(rows, selector, lists)
        return image(
            part_count, indices, pos, tiles, rows, received, selector, turns, lift_hi, lift_lo,
            face_link, face_orient, face_normal, boundary_metric_quotient, inverse_table,
        )

    second = coupled_image(first)
    third = coupled_image(second)
    second_columns, third_columns, part = gram_partials(first, second, third)
    total = total_over_devices(part)
    return finish(weight, part_count, total, right_side, second_columns, third_columns)


def solution(mesh):
    in_specs = (
        P(None, ("prow", "pcol")),
        P(("prow", "pcol")),
        P(("prow", "pcol")),
        P(("prow", "pcol")),
        P(("prow", "pcol")),
        P(None, ("prow", "pcol")),
        P(("prow", "pcol")),
        P(("prow", "pcol"), None, None),
        P(),
        P(),
    )
    out_specs = (P(None, None, ("prow", "pcol")), P())
    return jax.shard_map(shards, mesh=mesh, in_specs=in_specs, out_specs=out_specs, check_vma=False)
```

```python
import functools

import jax
import jax.numpy as jnp
import numpy as np
from jax import lax
from jax.experimental import pallas as pl
from jax.experimental.pallas import tpu as pltpu
from jax.sharding import PartitionSpec as P

EPSILON = 1e-06
PERMUTATIONS = ((0, 1, 2), (0, 2, 1), (1, 0, 2), (1, 2, 0), (2, 0, 1), (2, 1, 0))
OFFSETS = tuple(((direction // 3 - 1, direction % 3 - 1) for direction in (0, 1, 2, 3, 5, 6, 7, 8)))
MESH = pl.DeviceIdType.MESH
F32, BF16, I32 = jnp.float32, jnp.bfloat16, jnp.int32
MIB = 1024 * 1024
UNK, CLASSES, LANES = 120, 256, 128
TILE = 16
HALF = 64
GROUP = 32
TILE_ROWS = 12 * GROUP
NODE_PITCH = 136
FLUX_PITCH = 264
STAGE_PITCH = 24


def trace_tables():
    element_points = [
        (coord_a, coord_b, coord_c, 3 - coord_a - coord_b - coord_c)
        for coord_a in range(4)
        for coord_b in range(4 - coord_a)
        for coord_c in range(4 - coord_a - coord_b)
    ]
    face_points = [
        (coord_a, coord_b, 3 - coord_a - coord_b)
        for coord_a in range(4)
        for coord_b in range(4 - coord_a)
    ]
    select_rows = []
    for opposite in range(4):
        corners = [vertex for vertex in range(4) if vertex != opposite]
        members = []
        for triple in face_points:
            coords = [0, 0, 0, 0]
            for position in range(3):
                coords[corners[position]] = triple[position]
            members.append(element_points.index(tuple(coords)))
        select_rows.append(members)
    turn_rows = [
        [
            face_points.index((triple[sigma_row[0]], triple[sigma_row[1]], triple[sigma_row[2]]))
            for triple in face_points
        ]
        for sigma_row in PERMUTATIONS
    ]
    return select_rows, turn_rows


def trace_selector():
    select_rows, _ = trace_tables()
    table = np.zeros((2 * LANES, 4 * HALF), np.float32)
    for side in range(4):
        for c in range(6):
            for j in range(10):
                column = side * HALF + c * 10 + j
                table[c * 20 + select_rows[side][j], column] = 1.0
                table[LANES + c * 20 + select_rows[side][j], column] = 1.0
    return table


def split(value):
    high = value.astype(BF16)
    return high, (value - high.astype(F32)).astype(BF16)


def dot(a, b, dims=(((1,), (0,)), ((), ()))):
    return lax.dot_general(a, b, dims, preferred_element_type=F32)


NT = (((1,), (1,)), ((), ()))
VMEM = pl.BlockSpec(memory_space=pltpu.VMEM)
SMEM = pl.BlockSpec(memory_space=pltpu.SMEM)
ANY = pl.BlockSpec(memory_space=pl.ANY)


def live_lanes(count, first, width):
    return ((lax.broadcasted_iota(I32, (1, width), 1) + first) < count).astype(F32)


def prep_kernel(
    remote, count_ref, field_hbm, class_ref, lift_ref, link_ref,
    rows_ref, pos_ref, tile_ref, index_ref, lift_hi_ref, lift_lo_ref,
    field_ref, spread_ref, field_sem,
):
    elements = field_ref.shape[1]
    blocks = elements // LANES
    count = count_ref[0]
    field_copy = pltpu.make_async_copy(field_hbm, field_ref, field_sem)
    field_copy.start()

    class_row = lax.broadcasted_iota(I32, (CLASSES, LANES), 0)
    totals = jnp.zeros((CLASSES, LANES), F32)
    for block in range(blocks):
        totals = totals + (class_ref[block : block + 1, :] == class_row).astype(F32)
    total = jnp.sum(totals, axis=1, keepdims=True)
    tiles = jnp.floor((total + (TILE - 1)) * (1.0 / TILE))
    tiles = jnp.broadcast_to(tiles, (CLASSES, LANES))
    lower = (
        lax.broadcasted_iota(I32, (CLASSES, CLASSES), 1)
        < lax.broadcasted_iota(I32, (CLASSES, CLASSES), 0)
    ).astype(BF16)
    start = dot(lower, tiles.astype(BF16))
    end = start + tiles
    earlier = (
        lax.broadcasted_iota(I32, (LANES, 2 * LANES), 0)
        < lax.broadcasted_iota(I32, (LANES, 2 * LANES), 1)
    ).astype(BF16)
    carry = start * TILE
    for block in range(blocks):
        member = (class_ref[block : block + 1, :] == class_row).astype(F32)
        ranks = dot(member.astype(BF16), earlier)
        position = jnp.sum(member * (ranks[:, :LANES] + carry), axis=0, keepdims=True)
        pos_ref[block : block + 1, :] = position.astype(I32)
        carry = carry + ranks[:, LANES:]
    tile_ref[...] = jnp.zeros((8, LANES), I32)
    for row in range(4):
        tile = (lax.broadcasted_iota(I32, (CLASSES, LANES), 1) + row * LANES).astype(F32)
        owner = jnp.sum((end <= tile).astype(F32), axis=0, keepdims=True)
        tile_ref[row : row + 1, :] = jnp.minimum(owner.astype(I32), CLASSES - 1)
    tile_ref[4:5, :] = end[CLASSES - 1 :, :].astype(I32)

    link = link_ref[...]
    own = (
        lax.broadcasted_iota(I32, link.shape, 0) * LANES
        + lax.broadcasted_iota(I32, link.shape, 1)
        + remote
    )
    index_ref[...] = jnp.where(link < 0, own, link)

    spread_ref[...] = jnp.zeros(spread_ref.shape, F32)
    for side in range(4):
        block = lift_ref[side]
        for c in range(6):
            first = side * HALF + c * 10
            spread_ref[c * 20 : (c + 1) * 20, first : first + 10] = block
    high, low = split(spread_ref[...])
    lift_hi_ref[...] = high
    lift_lo_ref[...] = low

    field_copy.wait()
    for block in range(blocks):
        lanes = slice(block * LANES, (block + 1) * LANES)
        value = field_ref[:, lanes] * live_lanes(count, block * LANES, LANES)
        value = jnp.concatenate([value, jnp.zeros((LANES - UNK, LANES), F32)], axis=0)
        rows_ref[lanes, :] = value.T


def prepare(part_count, right_side, elem_class, lift, link, remote):
    elements = right_side.shape[1]
    faces = link.shape[0]
    return pl.pallas_call(
        functools.partial(prep_kernel, remote),
        out_shape=(
            jax.ShapeDtypeStruct((elements, LANES), F32),
            jax.ShapeDtypeStruct((elements // LANES, LANES), I32),
            jax.ShapeDtypeStruct((8, LANES), I32),
            jax.ShapeDtypeStruct((faces // LANES, LANES), I32),
            jax.ShapeDtypeStruct((LANES, 4 * HALF), BF16),
            jax.ShapeDtypeStruct((LANES, 4 * HALF), BF16),
        ),
        in_specs=[SMEM, ANY, VMEM, VMEM, VMEM],
        out_specs=(VMEM,) * 6,
        scratch_shapes=[
            pltpu.VMEM(right_side.shape, F32),
            pltpu.VMEM((LANES, 4 * HALF), F32),
            pltpu.SemaphoreType.DMA(()),
        ],
        compiler_params=pltpu.CompilerParams(vmem_limit_bytes=8 * MIB),
        name="prepare",
    )(
        part_count, right_side, elem_class.reshape(elements // LANES, LANES), lift,
        link.reshape(faces // LANES, LANES),
    )


def write_traces(rows_ref, selector_ref, table_ref, first):
    elements = rows_ref.shape[0]
    width = 2 * LANES
    left = lax.broadcasted_iota(I32, (width, LANES), 1) < HALF

    def block(index, carry):
        base = pl.multiple_of(index * width, width)
        high, low = split(rows_ref[pl.ds(base, width), :])
        traces = dot(jnp.concatenate([high, low], axis=1), selector_ref[...])
        for pair in range(2):
            both = traces[:, pair * LANES : (pair + 1) * LANES]
            swapped = pltpu.roll(both, HALF, 1)
            even, odd = first + 2 * pair * elements, first + (2 * pair + 1) * elements
            table_ref[pl.ds(even + base, width), :] = jnp.where(left, both, swapped)
            table_ref[pl.ds(odd + base, width), :] = jnp.where(left, swapped, both)
        return carry

    lax.fori_loop(0, elements // width, block, 0, unroll=4)


def gather_pairs(table_ref, index_ref, out_ref, first_a, first_b, offset, count, unroll):
    left = lax.broadcasted_iota(I32, (1, LANES), 1) < HALF

    def block(index, carry):
        base = pl.multiple_of(index * unroll, unroll)
        for step in range(unroll):
            row_a = table_ref[pl.ds(index_ref[first_a + base + step] + offset, 1), :]
            row_b = table_ref[pl.ds(index_ref[first_b + base + step] + offset, 1), :]
            out_ref[pl.ds(base + step, 1), :] = jnp.where(left, row_a, row_b)
        return carry

    lax.fori_loop(0, count // unroll, block, 0)


def class_major(native_ref, stage_ref, class_ref):
    rows = 16
    pad = jnp.zeros((LANES - UNK, CLASSES), F32)

    def chunk(index, carry):
        for row in range(rows):
            source = index * rows + row
            value = native_ref[jnp.minimum(source, UNK - 1)].astype(F32)
            value = jnp.where(source < UNK, value, 0.0)
            value = jnp.concatenate([value, pad], axis=0).T
            stage_ref[pl.ds(row, CLASSES, stride=STAGE_PITCH), :] = value
        first = pl.multiple_of(index * rows, rows)
        stage = stage_ref[...].reshape(CLASSES, STAGE_PITCH, LANES)[:, :rows].astype(BF16)
        class_ref[:, pl.ds(first, rows), :] = stage
        return carry

    lax.fori_loop(0, LANES // rows, chunk, 0)


def exchange_kernel(grid_rows, grid_columns, with_classes, *refs):
    if with_classes:
        (rows_ref, selector_ref, list_ref, native_hbm, table_ref, class_ref,
         outgoing_ref, received_ref, send_sem, recv_sem, native_ref, stage_ref, native_sem) = refs
        native_copy = pltpu.make_async_copy(native_hbm, native_ref, native_sem)
        native_copy.start()
    else:
        (rows_ref, selector_ref, list_ref, table_ref,
         outgoing_ref, received_ref, send_sem, recv_sem) = refs
    slots = outgoing_ref.shape[1]
    row, column = lax.axis_index("prow"), lax.axis_index("pcol")

    def present(index):
        a, b = OFFSETS[index]
        inside = None
        for at, step, size in ((row, a, grid_rows), (column, b, grid_columns)):
            if step == 0:
                continue
            term = at > 0 if step < 0 else at < size - 1
            inside = term if inside is None else jnp.logical_and(inside, term)
        return inside

    def partner(index):
        a, b = OFFSETS[index]
        return (row + a, column + b)

    def transfer(index):
        return pltpu.make_async_remote_copy(
            src_ref=outgoing_ref.at[index],
            dst_ref=received_ref.at[7 - index],
            send_sem=send_sem.at[index],
            recv_sem=recv_sem.at[7 - index],
            device_id=partner(index),
            device_id_type=MESH,
        )

    barrier = pltpu.get_barrier_semaphore()
    for index in range(8):
        @pl.when(present(index))
        def _(index=index):
            pl.semaphore_signal(barrier, inc=1, device_id=partner(index), device_id_type=MESH)

    write_traces(rows_ref, selector_ref, table_ref, 16 * slots)

    near_rows = 1 + (row > 0).astype(I32) + (row < grid_rows - 1).astype(I32)
    near_columns = 1 + (column > 0).astype(I32) + (column < grid_columns - 1).astype(I32)
    pl.semaphore_wait(barrier, near_rows * near_columns - 1)

    for index in (0, 2, 5, 7, 3, 4, 1, 6):
        first = index * 2 * slots
        gather_pairs(
            table_ref, list_ref, outgoing_ref.at[index], first, first + slots, 0, slots, 32
        )

        @pl.when(present(index))
        def _(index=index):
            transfer(index).start()

    if with_classes:
        native_copy.wait()
        class_major(native_ref, stage_ref, class_ref)

    left = lax.broadcasted_iota(I32, (slots, LANES), 1) < HALF
    for index in (1, 6, 3, 4, 0, 2, 5, 7):
        @pl.when(present(index))
        def _(index=index):
            transfer(7 - index).wait_recv()
            packed = received_ref[index]
            swapped = pltpu.roll(packed, HALF, 1)
            first = index * 2 * slots
            table_ref[first : first + slots, :] = jnp.where(left, packed, swapped)
            table_ref[first + slots : first + 2 * slots, :] = jnp.where(left, swapped, packed)

    for index in range(8):
        @pl.when(present(index))
        def _(index=index):
            transfer(index).wait_send()


def exchange(rows, selector, lists, native=None):
    slots = lists.shape[0] // 16
    with_classes = native is not None
    out_shape = [jax.ShapeDtypeStruct((16 * slots + 4 * rows.shape[0], LANES), F32)]
    scratch = [
        pltpu.VMEM((8, slots, LANES), F32),
        pltpu.VMEM((8, slots, LANES), F32),
        pltpu.SemaphoreType.DMA((8,)),
        pltpu.SemaphoreType.DMA((8,)),
    ]
    operands = [rows, selector, lists]
    if with_classes:
        out_shape.append(jax.ShapeDtypeStruct((CLASSES, LANES, LANES), BF16))
        scratch += [
            pltpu.VMEM(native.shape, BF16),
            pltpu.VMEM((CLASSES * STAGE_PITCH, LANES), F32),
            pltpu.SemaphoreType.DMA(()),
        ]
        operands.append(native)
    return pl.pallas_call(
        functools.partial(
            exchange_kernel, lax.axis_size("prow"), lax.axis_size("pcol"), with_classes
        ),
        out_shape=tuple(out_shape),
        in_specs=[VMEM, VMEM, SMEM] + [ANY] * with_classes,
        out_specs=(VMEM,) * len(out_shape),
        scratch_shapes=scratch,
        compiler_params=pltpu.CompilerParams(
            collective_id=2 if with_classes else 0, has_side_effects=True,
            vmem_limit_bytes=(36 if with_classes else 16) * MIB,
        ),
        name="exchange_first" if with_classes else "exchange",
    )(*operands)


def turn_choices():
    _, turn_rows = trace_tables()
    choices = []
    for j in range(10):
        sources = {}
        for option in range(6):
            sources.setdefault(turn_rows[option][j], []).append(option)
        choices.append([(source, tuple(options)) for source, options in sources.items()])
    return choices


def turn_faces(node_ref, first, stride, orient):
    masks = {}

    def mask(options):
        if options not in masks:
            value = orient == options[0]
            for option in options[1:]:
                value = jnp.logical_or(value, orient == option)
            masks[options] = value
        return masks[options]

    choices = turn_choices()
    for c in range(6):
        at = [pl.ds(first + c * 10 + j, 8, stride=stride) for j in range(10)]
        nodes = [node_ref[at[j], :] for j in range(10)]
        for j in range(10):
            (source, _), *others = choices[j]
            value = nodes[source]
            for source, options in others:
                value = jnp.where(mask(options), nodes[source], value)
            if others:
                node_ref[at[j], :] = value


def face_flux(electric, magnetic, normal, scale):
    along_e = normal[0] * electric[0] + normal[1] * electric[1] + normal[2] * electric[2]
    along_h = normal[0] * magnetic[0] + normal[1] * magnetic[1] + normal[2] * magnetic[2]
    flux = []
    for c in range(3):
        a, b = (c + 1) % 3, (c + 2) % 3
        cross = normal[a] * magnetic[b] - normal[b] * magnetic[a]
        flux.append(scale * (electric[c] - normal[c] * along_e - cross))
    for c in range(3):
        a, b = (c + 1) % 3, (c + 2) % 3
        cross = normal[a] * electric[b] - normal[b] * electric[a]
        flux.append(scale * (magnetic[c] - normal[c] * along_h + cross))
    return flux


def image_kernel(
    count_ref, index_ref, pos_ref, tile_ref,
    table_ref, lift_hi_ref, lift_lo_ref,
    link_ref, orient_ref, normal_ref, quotient_ref, class_ref,
    image_ref,
    picked_ref, node_ref, flux_ref, coupled_ref, sorted_ref, solved_ref,
):
    elements = image_ref.shape[0]
    blocks = elements // LANES
    chunks = blocks // 8

    gather_pairs(table_ref, index_ref, picked_ref, 0, 2 * elements, 0, 2 * elements, 64)

    def transpose(index, carry):
        for step in range(4):
            block = index * 4 + step
            rows = pl.ds(pl.multiple_of(block * LANES, LANES), LANES)
            target = pl.multiple_of(block * NODE_PITCH, 8)
            node_ref[pl.ds(target, LANES), :] = picked_ref[rows, :].T
        return carry

    lax.fori_loop(0, 2 * blocks // 4, transpose, 0)

    for block in range(blocks):
        for side in range(4):
            last = block * FLUX_PITCH + (side + 1) * HALF
            flux_ref[last - 8 : last, :] = jnp.zeros((8, LANES), F32)

    count = count_ref[0]
    lane = (
        lax.broadcasted_iota(I32, (8, LANES), 0) * LANES + lax.broadcasted_iota(I32, (8, LANES), 1)
    )

    def chunk(index, carry):
        side, part = index // chunks, index % chunks
        pair, half = side % 2, side // 2
        faces = pl.ds(pl.multiple_of(side * blocks + part * 8, 8), 8)
        first = (pair * blocks + part * 8) * NODE_PITCH + half * HALF
        turn_faces(node_ref, first, NODE_PITCH, orient_ref[faces, :])
        alive = ((lane + part * (8 * LANES)) < count).astype(F32)
        scale = 0.5 * quotient_ref[faces, :] * alive
        sign = jnp.where(link_ref[faces, :] < 0, -1.0, 1.0)
        normal = [normal_ref[c, faces, :] for c in range(3)]
        target = part * (8 * FLUX_PITCH) + side * HALF
        for j in range(10):
            nodes = [node_ref[pl.ds(first + c * 10 + j, 8, stride=NODE_PITCH), :] for c in range(6)]
            electric = [value * sign for value in nodes[:3]]
            flux = face_flux(electric, nodes[3:], normal, scale)
            for c in range(6):
                flux_ref[pl.ds(target + c * 10 + j, 8, stride=FLUX_PITCH), :] = flux[c]
        return carry

    lax.fori_loop(0, 4 * chunks, chunk, 0)

    def lift(index, carry):
        rows = 4 * HALF
        first = pl.multiple_of(index * (2 * FLUX_PITCH), 8)
        second = pl.multiple_of(first + FLUX_PITCH, 8)
        value = jnp.concatenate(
            [flux_ref[pl.ds(first, rows), :], flux_ref[pl.ds(second, rows), :]], axis=1
        )
        high, low = split(value)
        coupled = dot(lift_hi_ref[...], high) + dot(lift_hi_ref[...], low) + dot(lift_lo_ref[...], high)
        base = pl.multiple_of(index * (2 * LANES), 2 * LANES)
        coupled_ref[pl.ds(base, 2 * LANES), :] = coupled.T
        return carry

    lax.fori_loop(0, blocks // 2, lift, 0, unroll=4)

    unroll = 16

    def place(index, carry):
        base = pl.multiple_of(index * unroll, unroll)
        for step in range(unroll):
            sorted_ref[pl.ds(pos_ref[base + step], 1), :] = coupled_ref[pl.ds(base + step, 1), :]
        return carry

    lax.fori_loop(0, elements // unroll, place, 0)

    def solve(index, carry):
        for step in range(GROUP):
            tile = index * GROUP + step
            base = pl.multiple_of(tile * TILE, TILE)
            high, low = split(sorted_ref[pl.ds(base, TILE), :])
            result = dot(jnp.concatenate([high, low], axis=0), class_ref[tile_ref[tile]], NT)
            solved_ref[pl.ds(base, TILE), :] = result[:TILE] + result[TILE:]
        return carry

    lax.fori_loop(0, (tile_ref[4 * LANES] + (GROUP - 1)) // GROUP, solve, 0)

    def fetch(index, carry):
        base = pl.multiple_of(index * unroll, unroll)
        for step in range(unroll):
            image_ref[pl.ds(base + step, 1), :] = solved_ref[pl.ds(pos_ref[base + step], 1), :]
        return carry

    lax.fori_loop(0, elements // unroll, fetch, 0)


def image(part_count, indices, pos, tiles, table, lift_hi, lift_lo,
          link, orient, normal, quotient, classes):
    elements = pos.shape[0]
    slots = TILE_ROWS * TILE
    return pl.pallas_call(
        image_kernel,
        out_shape=jax.ShapeDtypeStruct((elements, LANES), F32),
        in_specs=[SMEM] * 4 + [VMEM] * 8,
        out_specs=VMEM,
        scratch_shapes=[
            pltpu.VMEM((2 * elements, LANES), F32),
            pltpu.VMEM((2 * elements // LANES * NODE_PITCH, LANES), F32),
            pltpu.VMEM((elements // LANES * FLUX_PITCH, LANES), F32),
            pltpu.VMEM((elements, LANES), F32),
            pltpu.VMEM((slots, LANES), F32),
            pltpu.VMEM((slots, LANES), F32),
        ],
        compiler_params=pltpu.CompilerParams(vmem_limit_bytes=24 * MIB),
        name="image",
    )(
        part_count, indices, pos, tiles, table, lift_hi, lift_lo,
        link.reshape(-1, LANES), orient.reshape(-1, LANES), normal.reshape(3, -1, LANES),
        quotient.reshape(-1, LANES), classes,
    )


def gram_partials(first_ref, second_ref, third_ref, gram_ref):
    elements = first_ref.shape[0]

    def block(index, sums):
        rows = pl.ds(pl.multiple_of(index * LANES, LANES), LANES)
        f, t, u = first_ref[rows, :], second_ref[rows, :], third_ref[rows, :]
        pairs = (f * f, f * t, t * t, f * u, t * u, u * u)
        return tuple(
            total + jnp.sum(pair.reshape(LANES // 8, 8, LANES), axis=0)
            for total, pair in zip(sums, pairs)
        )

    zero = jnp.zeros((8, LANES), F32)
    sums = lax.fori_loop(0, elements // LANES, block, (zero,) * 6)
    for index in range(6):
        gram_ref[index : index + 1, :] = jnp.sum(sums[index], axis=0, keepdims=True)
    gram_ref[6:, :] = jnp.zeros((2, LANES), F32)


def total_kernel(grid_rows, grid_columns, first_ref, second_ref, third_ref, total_ref,
                 part_ref, over_rows, over_columns, send_row, recv_row, send_column, recv_column):
    row, column = lax.axis_index("prow"), lax.axis_index("pcol")

    def row_partner(step):
        return lax.rem(row + step, grid_rows)

    def column_partner(step):
        return lax.rem(column + step, grid_columns)

    barrier = pltpu.get_barrier_semaphore()
    for step in range(1, grid_rows):
        pl.semaphore_signal(
            barrier, inc=1, device_id=(row_partner(step), column), device_id_type=MESH
        )
    for step in range(1, grid_columns):
        pl.semaphore_signal(
            barrier, inc=1, device_id=(row, column_partner(step)), device_id_type=MESH
        )
    gram_partials(first_ref, second_ref, third_ref, part_ref)
    pl.semaphore_wait(barrier, grid_rows + grid_columns - 2)

    def row_copy(step):
        return pltpu.make_async_remote_copy(
            src_ref=part_ref,
            dst_ref=over_rows.at[step],
            send_sem=send_row.at[step],
            recv_sem=recv_row.at[step],
            device_id=(row_partner(step), column),
            device_id_type=MESH,
        )

    for step in range(1, grid_rows):
        row_copy(step).start()
    over_rows[0] = part_ref[...]
    for step in range(1, grid_rows):
        row_copy(step).wait()
    total = over_rows[row]
    for source in range(1, grid_rows):
        total = total + over_rows[lax.rem(row - source + grid_rows, grid_rows)]
    over_columns[0] = total

    def column_copy(step):
        return pltpu.make_async_remote_copy(
            src_ref=over_columns.at[0],
            dst_ref=over_columns.at[step],
            send_sem=send_column.at[step],
            recv_sem=recv_column.at[step],
            device_id=(row, column_partner(step)),
            device_id_type=MESH,
        )

    for step in range(1, grid_columns):
        column_copy(step).start()
    for step in range(1, grid_columns):
        column_copy(step).wait()
    total = over_columns[column]
    for source in range(1, grid_columns):
        total = total + over_columns[lax.rem(column - source + grid_columns, grid_columns)]
    total_ref[...] = total


def total_over_devices(first, second, third):
    grid_rows, grid_columns = lax.axis_size("prow"), lax.axis_size("pcol")
    part = (8, LANES)
    return pl.pallas_call(
        functools.partial(total_kernel, grid_rows, grid_columns),
        out_shape=jax.ShapeDtypeStruct(part, F32),
        in_specs=[VMEM] * 3,
        out_specs=VMEM,
        scratch_shapes=[
            pltpu.VMEM(part, F32),
            pltpu.VMEM((grid_rows,) + part, F32),
            pltpu.VMEM((grid_columns,) + part, F32),
            pltpu.SemaphoreType.DMA((grid_rows,)),
            pltpu.SemaphoreType.DMA((grid_rows,)),
            pltpu.SemaphoreType.DMA((grid_columns,)),
            pltpu.SemaphoreType.DMA((grid_columns,)),
        ],
        compiler_params=pltpu.CompilerParams(
            collective_id=1, has_side_effects=True, vmem_limit_bytes=8 * MIB
        ),
        name="total",
    )(first, second, third)


def finish_kernel(weight, count_ref, total_ref, field_ref, second_ref, third_ref, basis_ref, hess_ref):
    width = field_ref.shape[1]
    gram = jnp.sum(total_ref[...], axis=1, keepdims=True) * weight
    ff, ft, tt, fu, tu, uu = (gram[index : index + 1, :] for index in range(6))
    beta = jnp.sqrt(ff + EPSILON)
    square = beta * beta
    h00 = (ff + ft) / square
    p = (EPSILON - ft) / square
    h10 = jnp.sqrt((tt + 2 * p * ft + p * p * ff) / square + EPSILON)
    k1 = 1.0 / (beta * h10)
    h01 = k1 / beta * (fu + (1 + p) * ft + p * ff)
    h11 = k1 * k1 * (tu + (1 + p) * tt + p * ft + p * fu + p * (1 + p) * ft + p * p * ff)
    q = 1 + p - h11
    w = p * (1 - h11) - h01 * h10
    h21 = jnp.sqrt(
        k1 * k1 * (uu + 2 * q * tu + 2 * w * fu + q * q * tt + 2 * q * w * ft + w * w * ff)
        + EPSILON
    )
    k2 = k1 / h21

    alive = live_lanes(count_ref[0], pl.program_id(0) * width, width)
    f = field_ref[...] * alive
    t, u = second_ref[...].T[:UNK], third_ref[...].T[:UNK]
    basis_ref[0] = f * (1.0 / beta)
    basis_ref[1] = t * k1 + f * (p * k1)
    basis_ref[2] = u * k2 + t * (q * k2) + f * (w * k2)

    at_row = lax.broadcasted_iota(I32, (3, 2), 0)
    at_column = lax.broadcasted_iota(I32, (3, 2), 1)
    hess = jnp.zeros((3, 2), F32)
    for i, j, value in ((0, 0, h00), (1, 0, h10), (0, 1, h01), (1, 1, h11), (2, 1, h21)):
        hess = jnp.where(jnp.logical_and(at_row == i, at_column == j), value, hess)
    hess_ref[...] = hess


def finish(weight, part_count, total, right_side, second, third):
    elements = right_side.shape[1]
    width = 512
    rows = pl.BlockSpec((width, LANES), lambda i: (i, 0))
    field = pl.BlockSpec((UNK, width), lambda i: (0, i))
    return pl.pallas_call(
        functools.partial(finish_kernel, weight),
        grid=(elements // width,),
        out_shape=(
            jax.ShapeDtypeStruct((3, UNK, elements), F32),
            jax.ShapeDtypeStruct((3, 2), F32),
        ),
        in_specs=[
            pl.BlockSpec(memory_space=pltpu.SMEM),
            pl.BlockSpec((8, LANES), lambda i: (0, 0)),
            field, rows, rows,
        ],
        out_specs=(
            pl.BlockSpec((3, UNK, width), lambda i: (0, 0, i)),
            pl.BlockSpec((3, 2), lambda i: (0, 0)),
        ),
        compiler_params=pltpu.CompilerParams(vmem_limit_bytes=12 * MIB),
        name="finish",
    )(part_count, total, right_side, second, third)


def shards(
    right_side,
    part_count,
    elem_class,
    face_link,
    face_orient,
    face_normal,
    boundary_metric_quotient,
    bound_face,
    lift,
    inverse_table,
):
    unknowns, elements = right_side.shape
    all_subdomains = lax.axis_size("prow") * lax.axis_size("pcol")
    weight = 1.0 / (unknowns * elements * all_subdomains)
    lists = bound_face.reshape(-1)
    lists = jnp.maximum(lists, 0) + lists.shape[0]
    selector = jnp.asarray(trace_selector(), BF16)
    native = jnp.transpose(inverse_table, (1, 2, 0))

    first, pos, tiles, indices, lift_hi, lift_lo = prepare(
        part_count, right_side, elem_class, lift, face_link, lists.shape[0]
    )
    pos, tiles, indices = pos.reshape(-1), tiles.reshape(-1), indices.reshape(-1)
    first_table, classes = exchange(first, selector, lists, native)

    def operator_image(table):
        return image(
            part_count, indices, pos, tiles, table, lift_hi, lift_lo, face_link, face_orient,
            face_normal, boundary_metric_quotient, classes,
        )

    second = operator_image(first_table)
    (second_table,) = exchange(second, selector, lists)
    third = operator_image(second_table)
    total = total_over_devices(first, second, third)
    return finish(weight, part_count, total, right_side, second, third)


def solution(mesh):
    in_specs = (
        P(None, ("prow", "pcol")),
        P(("prow", "pcol")),
        P(("prow", "pcol")),
        P(("prow", "pcol")),
        P(("prow", "pcol")),
        P(None, ("prow", "pcol")),
        P(("prow", "pcol")),
        P(("prow", "pcol"), None, None),
        P(),
        P(),
    )
    out_specs = (P(None, None, ("prow", "pcol")), P())
    return jax.shard_map(shards, mesh=mesh, in_specs=in_specs, out_specs=out_specs, check_vma=False)
```

```python
import functools

import jax
import jax.numpy as jnp
import numpy as np
from jax import lax
from jax.experimental import pallas as pl
from jax.experimental.pallas import tpu as pltpu
from jax.sharding import PartitionSpec as P

EPSILON = 1e-06
PERMUTATIONS = ((0, 1, 2), (0, 2, 1), (1, 0, 2), (1, 2, 0), (2, 0, 1), (2, 1, 0))
OFFSETS = tuple(((direction // 3 - 1, direction % 3 - 1) for direction in (0, 1, 2, 3, 5, 6, 7, 8)))
MESH = pl.DeviceIdType.MESH
F32, BF16, I32 = jnp.float32, jnp.bfloat16, jnp.int32
MIB = 1024 * 1024
UNK, CLASSES, LANES = 120, 256, 128
TILE = 16
HALF = 64
GROUP = 32
TILE_ROWS = 12 * GROUP
NODE_PITCH = 136
FLUX_PITCH = 264
STAGE_PITCH = 24
CHUNK = 16


def trace_tables():
    element_points = [
        (coord_a, coord_b, coord_c, 3 - coord_a - coord_b - coord_c)
        for coord_a in range(4)
        for coord_b in range(4 - coord_a)
        for coord_c in range(4 - coord_a - coord_b)
    ]
    face_points = [
        (coord_a, coord_b, 3 - coord_a - coord_b)
        for coord_a in range(4)
        for coord_b in range(4 - coord_a)
    ]
    select_rows = []
    for opposite in range(4):
        corners = [vertex for vertex in range(4) if vertex != opposite]
        members = []
        for triple in face_points:
            coords = [0, 0, 0, 0]
            for position in range(3):
                coords[corners[position]] = triple[position]
            members.append(element_points.index(tuple(coords)))
        select_rows.append(members)
    turn_rows = [
        [
            face_points.index((triple[sigma_row[0]], triple[sigma_row[1]], triple[sigma_row[2]]))
            for triple in face_points
        ]
        for sigma_row in PERMUTATIONS
    ]
    return select_rows, turn_rows


def trace_selector():
    select_rows, _ = trace_tables()
    column = lax.broadcasted_iota(I32, (1, 4 * HALF), 1)
    source = jnp.full((1, 4 * HALF), -1, I32)
    for side in range(4):
        for j in range(10):
            for c in range(6):
                here = column == side * HALF + c * 10 + j
                source = jnp.where(here, c * 20 + select_rows[side][j], source)
    row = lax.broadcasted_iota(I32, (2 * LANES, 4 * HALF), 0)
    row = jnp.where(row >= LANES, row - LANES, row)
    return (row == source).astype(F32).astype(BF16)


def split(value):
    high = value.astype(BF16)
    return high, (value - high.astype(F32)).astype(BF16)


def dot(a, b, dims=(((1,), (0,)), ((), ()))):
    return lax.dot_general(a, b, dims, preferred_element_type=F32)


VMEM = pl.BlockSpec(memory_space=pltpu.VMEM)
SMEM = pl.BlockSpec(memory_space=pltpu.SMEM)
ANY = pl.BlockSpec(memory_space=pl.ANY)
HBM = pl.BlockSpec(memory_space=pltpu.HBM)


def cost(microseconds):
    return pl.CostEstimate(
        flops=0, transcendentals=0, bytes_accessed=int(microseconds * 3_000_000)
    )


def live_lanes(count, first, width):
    return ((lax.broadcasted_iota(I32, (1, width), 1) + first) < count).astype(F32)


def rows_kernel(remote, count_ref, field_ref, list_ref, rows_ref, slot_ref, selector_ref):
    blocks = field_ref.shape[1] // LANES
    count = count_ref[0]
    for block in range(blocks):
        lanes = slice(block * LANES, (block + 1) * LANES)
        value = field_ref[:, lanes] * live_lanes(count, block * LANES, LANES)
        value = jnp.concatenate([value, jnp.zeros((LANES - UNK, LANES), F32)], axis=0)
        rows_ref[lanes, :] = value.T
    per_list = list_ref.shape[1] // LANES
    for index in range(8):
        for part in range(per_list):
            row = index * per_list + part
            face = list_ref[index : index + 1, part * LANES : (part + 1) * LANES]
            slot_ref[row : row + 1, :] = jnp.maximum(face, 0) + remote
    selector_ref[...] = trace_selector()


def first_rows(part_count, right_side, lists):
    remote = lists.shape[0] * lists.shape[1]
    return pl.pallas_call(
        functools.partial(rows_kernel, remote),
        out_shape=(
            jax.ShapeDtypeStruct((right_side.shape[1], LANES), F32),
            jax.ShapeDtypeStruct((remote // LANES, LANES), I32),
            jax.ShapeDtypeStruct((2 * LANES, 4 * HALF), BF16),
        ),
        in_specs=[SMEM, VMEM, VMEM],
        out_specs=(VMEM,) * 3,
        compiler_params=pltpu.CompilerParams(vmem_limit_bytes=4 * MIB),
        cost_estimate=cost(2),
        name="first_rows",
    )(part_count, right_side, lists)


def prep_kernel(
    remote, _, class_ref, lift_ref, link_ref, normal_ref,
    pos_ref, tile_ref, index_ref, lift_hi_ref, lift_lo_ref, plane_ref, spread_ref,
):
    blocks = class_ref.shape[0]

    class_row = lax.broadcasted_iota(I32, (CLASSES, LANES), 0)
    totals = jnp.zeros((CLASSES, LANES), F32)
    for block in range(blocks):
        totals = totals + (class_ref[block : block + 1, :] == class_row).astype(F32)
    total = jnp.sum(totals, axis=1, keepdims=True)
    tiles = jnp.floor((total + (TILE - 1)) * (1.0 / TILE))
    tiles = jnp.broadcast_to(tiles, (CLASSES, LANES))
    lower = (
        lax.broadcasted_iota(I32, (CLASSES, CLASSES), 1)
        < lax.broadcasted_iota(I32, (CLASSES, CLASSES), 0)
    ).astype(BF16)
    start = dot(lower, tiles.astype(BF16))
    end = start + tiles
    earlier = (
        lax.broadcasted_iota(I32, (LANES, 2 * LANES), 0)
        < lax.broadcasted_iota(I32, (LANES, 2 * LANES), 1)
    ).astype(BF16)
    carry = start * TILE
    for block in range(blocks):
        member = (class_ref[block : block + 1, :] == class_row).astype(F32)
        ranks = dot(member.astype(BF16), earlier)
        position = jnp.sum(member * (ranks[:, :LANES] + carry), axis=0, keepdims=True)
        pos_ref[block : block + 1, :] = position.astype(I32)
        carry = carry + ranks[:, LANES:]
    tile_ref[...] = jnp.zeros((8, LANES), I32)
    for row in range(4):
        tile = (lax.broadcasted_iota(I32, (CLASSES, LANES), 1) + row * LANES).astype(F32)
        owner = jnp.sum((end <= tile).astype(F32), axis=0, keepdims=True)
        tile_ref[row : row + 1, :] = jnp.minimum(owner.astype(I32), CLASSES - 1)
    tile_ref[4:5, :] = end[CLASSES - 1 :, :].astype(I32)

    spread_ref[...] = jnp.zeros(spread_ref.shape, F32)
    for side in range(4):
        block = lift_ref[:, side, :]
        for c in range(6):
            first = side * HALF + c * 10
            spread_ref[first : first + 10, c * 20 : (c + 1) * 20] = block
    high, low = split(spread_ref[...].T)
    lift_hi_ref[...] = high
    lift_lo_ref[...] = low

    link = link_ref[...]
    own = (
        lax.broadcasted_iota(I32, link.shape, 0) * LANES
        + lax.broadcasted_iota(I32, link.shape, 1)
        + remote
    )
    index_ref[...] = jnp.where(link < 0, own, link)

    for c in range(3):
        for row in range(link.shape[0]):
            plane_ref[c, row : row + 1, :] = normal_ref[c : c + 1, row * LANES : (row + 1) * LANES]


def prepare(after, elem_class, lift, link, normal, remote):
    elements, faces = elem_class.shape[0], link.shape[0]
    return pl.pallas_call(
        functools.partial(prep_kernel, remote),
        out_shape=(
            jax.ShapeDtypeStruct((elements // LANES, LANES), I32),
            jax.ShapeDtypeStruct((8, LANES), I32),
            jax.ShapeDtypeStruct((faces // LANES, LANES), I32),
            jax.ShapeDtypeStruct((LANES, 4 * HALF), BF16),
            jax.ShapeDtypeStruct((LANES, 4 * HALF), BF16),
            jax.ShapeDtypeStruct((3, faces // LANES, LANES), F32),
        ),
        in_specs=[ANY] + [VMEM] * 4,
        out_specs=(VMEM,) * 6,
        scratch_shapes=[pltpu.VMEM((4 * HALF, LANES), F32)],
        compiler_params=pltpu.CompilerParams(vmem_limit_bytes=4 * MIB),
        cost_estimate=cost(3),
        name="prepare",
    )(
        after, elem_class.reshape(elements // LANES, LANES), jnp.transpose(lift, (2, 0, 1)),
        link.reshape(faces // LANES, LANES), normal,
    )


def write_traces(rows_ref, selector_ref, table_ref, first):
    elements = rows_ref.shape[0]
    width = 2 * LANES
    left = lax.broadcasted_iota(I32, (width, LANES), 1) < HALF

    def block(index, carry):
        base = pl.multiple_of(index * width, width)
        high, low = split(rows_ref[pl.ds(base, width), :])
        traces = dot(jnp.concatenate([high, low], axis=1), selector_ref[...])
        for pair in range(2):
            both = traces[:, pair * LANES : (pair + 1) * LANES]
            swapped = pltpu.roll(both, HALF, 1)
            even, odd = first + 2 * pair * elements, first + (2 * pair + 1) * elements
            table_ref[pl.ds(even + base, width), :] = jnp.where(left, both, swapped)
            table_ref[pl.ds(odd + base, width), :] = jnp.where(left, swapped, both)
        return carry

    lax.fori_loop(0, elements // width, block, 0, unroll=4)


def gather_pairs(table_ref, index_ref, out_ref, first_a, first_b, offset, count, unroll):
    left = lax.broadcasted_iota(I32, (1, LANES), 1) < HALF

    def block(index, carry):
        base = pl.multiple_of(index * unroll, unroll)
        for step in range(unroll):
            row_a = table_ref[pl.ds(index_ref[first_a + base + step] + offset, 1), :]
            row_b = table_ref[pl.ds(index_ref[first_b + base + step] + offset, 1), :]
            out_ref[pl.ds(base + step, 1), :] = jnp.where(left, row_a, row_b)
        return carry

    lax.fori_loop(0, count // unroll, block, 0)


def class_major(native_ref, turned_ref, stage_ref, part_ref, class_hbm, sems):
    for half in range(2):
        for row in range(CHUNK):
            last = row * NODE_PITCH + UNK
            turned_ref[half, last : last + LANES - UNK, :] = jnp.zeros((LANES - UNK, LANES), F32)

    def store(first):
        slot = first // CHUNK % 2
        target = class_hbm.at[:, pl.ds(first, CHUNK), :]
        return pltpu.make_async_copy(part_ref.at[slot], target, sems.at[slot])

    for first in range(0, LANES, CHUNK):
        count = min(CHUNK, UNK - first)

        def collect(index, carry):
            value = native_ref[index, first : first + count, :].astype(F32)
            if count < CHUNK:
                value = jnp.concatenate([value, jnp.zeros((CHUNK - count, CLASSES), F32)], axis=0)
            for half in range(2):
                turned_ref[half, pl.ds(index, CHUNK, stride=NODE_PITCH), :] = value[
                    :, half * LANES : (half + 1) * LANES
                ]
            return carry

        lax.fori_loop(0, UNK, collect, 0, unroll=24)

        for row in range(CHUNK):
            for half in range(2):
                target = pl.ds(half * LANES * STAGE_PITCH + row, LANES, stride=STAGE_PITCH)
                rows = slice(row * NODE_PITCH, row * NODE_PITCH + LANES)
                stage_ref[target, :] = turned_ref[half, rows, :].T
        stage = stage_ref[...].reshape(CLASSES, STAGE_PITCH, LANES)[:, :CHUNK]
        if first >= 2 * CHUNK:
            store(first - 2 * CHUNK).wait()
        part_ref[first // CHUNK % 2] = stage.astype(BF16)
        store(first).start()
    return [store(LANES - 2 * CHUNK), store(LANES - CHUNK)]


def exchange_kernel(grid_rows, grid_columns, with_classes, *refs):
    if with_classes:
        (rows_ref, selector_ref, list_any, native_hbm, table_ref, class_hbm,
         list_ref, outgoing_ref, received_ref, local_sem, send_sem, recv_sem,
         native_ref, turned_ref, stage_ref, part_ref, native_sem, part_sems) = refs
        native_copy = pltpu.make_async_copy(native_hbm, native_ref, native_sem)
        native_copy.start()
    else:
        (rows_ref, selector_ref, list_any, table_ref,
         list_ref, outgoing_ref, received_ref, local_sem, send_sem, recv_sem) = refs
    list_copy = pltpu.make_async_copy(list_any, list_ref, local_sem)
    list_copy.start()
    slots = outgoing_ref.shape[1]
    row, column = lax.axis_index("prow"), lax.axis_index("pcol")

    def present(index):
        a, b = OFFSETS[index]
        inside = None
        for at, step, size in ((row, a, grid_rows), (column, b, grid_columns)):
            if step == 0:
                continue
            term = at > 0 if step < 0 else at < size - 1
            inside = term if inside is None else jnp.logical_and(inside, term)
        return inside

    def partner(index):
        a, b = OFFSETS[index]
        return (row + a, column + b)

    def transfer(index):
        return pltpu.make_async_remote_copy(
            src_ref=outgoing_ref.at[index],
            dst_ref=received_ref.at[7 - index],
            send_sem=send_sem.at[index],
            recv_sem=recv_sem.at[7 - index],
            device_id=partner(index),
            device_id_type=MESH,
        )

    barrier = pltpu.get_barrier_semaphore()
    for index in range(8):
        @pl.when(present(index))
        def _(index=index):
            pl.semaphore_signal(barrier, inc=1, device_id=partner(index), device_id_type=MESH)

    write_traces(rows_ref, selector_ref, table_ref, 16 * slots)
    list_copy.wait()

    def gather(index):
        first = index * 2 * slots
        gather_pairs(
            table_ref, list_ref, outgoing_ref.at[index], first, first + slots, 0, slots, 32
        )

    early, late = (0, 2, 5, 7), (3, 4, 1, 6)
    for index in early:
        gather(index)

    near_rows = 1 + (row > 0).astype(I32) + (row < grid_rows - 1).astype(I32)
    near_columns = 1 + (column > 0).astype(I32) + (column < grid_columns - 1).astype(I32)
    pl.semaphore_wait(barrier, near_rows * near_columns - 1)

    for index in early + late:
        if index in late:
            gather(index)

        @pl.when(present(index))
        def _(index=index):
            transfer(index).start()

    if with_classes:
        native_copy.wait()
        stores = class_major(native_ref, turned_ref, stage_ref, part_ref, class_hbm, part_sems)

    left = lax.broadcasted_iota(I32, (slots, LANES), 1) < HALF
    for index in (1, 6, 3, 4, 0, 2, 5, 7):
        @pl.when(present(index))
        def _(index=index):
            transfer(7 - index).wait_recv()
            packed = received_ref[index]
            swapped = pltpu.roll(packed, HALF, 1)
            first = index * 2 * slots
            table_ref[first : first + slots, :] = jnp.where(left, packed, swapped)
            table_ref[first + slots : first + 2 * slots, :] = jnp.where(left, swapped, packed)

    for index in range(8):
        @pl.when(present(index))
        def _(index=index):
            transfer(index).wait_send()

    if with_classes:
        for store in stores:
            store.wait()


def exchange(rows, selector, lists, native=None):
    slots = lists.shape[0] // 16
    with_classes = native is not None
    out_shape = [jax.ShapeDtypeStruct((16 * slots + 4 * rows.shape[0], LANES), F32)]
    scratch = [
        pltpu.SMEM(lists.shape, I32),
        pltpu.VMEM((8, slots, LANES), F32),
        pltpu.VMEM((8, slots, LANES), F32),
        pltpu.SemaphoreType.DMA(()),
        pltpu.SemaphoreType.DMA((8,)),
        pltpu.SemaphoreType.DMA((8,)),
    ]
    operands = [rows, selector, lists]
    if with_classes:
        out_shape.append(jax.ShapeDtypeStruct((CLASSES, LANES, LANES), BF16))
        scratch += [
            pltpu.VMEM(native.shape, BF16),
            pltpu.VMEM((2, CHUNK * NODE_PITCH, LANES), F32),
            pltpu.VMEM((CLASSES * STAGE_PITCH, LANES), F32),
            pltpu.VMEM((2, CLASSES, CHUNK, LANES), BF16),
            pltpu.SemaphoreType.DMA(()),
            pltpu.SemaphoreType.DMA((2,)),
        ]
        operands.append(native)
    return pl.pallas_call(
        functools.partial(
            exchange_kernel, lax.axis_size("prow"), lax.axis_size("pcol"), with_classes
        ),
        out_shape=tuple(out_shape),
        in_specs=[VMEM, VMEM, ANY] + [HBM] * with_classes,
        out_specs=(VMEM,) + (HBM,) * with_classes,
        scratch_shapes=scratch,
        compiler_params=pltpu.CompilerParams(
            collective_id=2 if with_classes else 0, has_side_effects=True,
            vmem_limit_bytes=(44 if with_classes else 8) * MIB,
        ),
        cost_estimate=cost(14),
        name="exchange_first" if with_classes else "exchange",
    )(*operands)


def turn_choices():
    _, turn_rows = trace_tables()
    choices = []
    for j in range(10):
        sources = {}
        for option in range(6):
            sources.setdefault(turn_rows[option][j], []).append(option)
        choices.append([(source, tuple(options)) for source, options in sources.items()])
    return choices


def turn_faces(node_ref, first, stride, orient):
    masks = {}

    def mask(options):
        if options not in masks:
            value = orient == options[0]
            for option in options[1:]:
                value = jnp.logical_or(value, orient == option)
            masks[options] = value
        return masks[options]

    choices = turn_choices()
    for c in range(6):
        at = [pl.ds(first + c * 10 + j, 8, stride=stride) for j in range(10)]
        nodes = [node_ref[at[j], :] for j in range(10)]
        for j in range(10):
            (source, _), *others = choices[j]
            value = nodes[source]
            for source, options in others:
                value = jnp.where(mask(options), nodes[source], value)
            if others:
                node_ref[at[j], :] = value


def face_flux(electric, magnetic, normal, scale):
    along_e = normal[0] * electric[0] + normal[1] * electric[1] + normal[2] * electric[2]
    along_h = normal[0] * magnetic[0] + normal[1] * magnetic[1] + normal[2] * magnetic[2]
    flux = []
    for c in range(3):
        a, b = (c + 1) % 3, (c + 2) % 3
        cross = normal[a] * magnetic[b] - normal[b] * magnetic[a]
        flux.append(scale * (electric[c] - normal[c] * along_e - cross))
    for c in range(3):
        a, b = (c + 1) % 3, (c + 2) % 3
        cross = normal[a] * electric[b] - normal[b] * electric[a]
        flux.append(scale * (magnetic[c] - normal[c] * along_h + cross))
    return flux


def image_kernel(
    count_ref, index_any, pos_any, tile_any,
    table_ref, lift_hi_ref, lift_lo_ref,
    link_ref, orient_ref, normal_ref, quotient_ref, class_hbm,
    image_ref,
    index_ref, pos_ref, tile_ref, smem_sems, class_ref, class_sem,
    picked_ref, node_ref, flux_ref, coupled_ref, sorted_ref, solved_ref,
):
    index_copy = pltpu.make_async_copy(index_any, index_ref, smem_sems.at[0])
    pos_copy = pltpu.make_async_copy(pos_any, pos_ref, smem_sems.at[1])
    tile_copy = pltpu.make_async_copy(tile_any, tile_ref, smem_sems.at[2])
    class_copy = pltpu.make_async_copy(class_hbm, class_ref, class_sem)
    for copy in (index_copy, pos_copy, tile_copy, class_copy):
        copy.start()
    elements = image_ref.shape[0]
    blocks = elements // LANES
    chunks = blocks // 8

    index_copy.wait()
    gather_pairs(table_ref, index_ref, picked_ref, 0, 2 * elements, 0, 2 * elements, 64)

    def transpose(index, carry):
        for step in range(4):
            block = index * 4 + step
            rows = pl.ds(pl.multiple_of(block * LANES, LANES), LANES)
            target = pl.multiple_of(block * NODE_PITCH, 8)
            node_ref[pl.ds(target, LANES), :] = picked_ref[rows, :].T
        return carry

    lax.fori_loop(0, 2 * blocks // 4, transpose, 0)

    for block in range(blocks):
        for side in range(4):
            last = block * FLUX_PITCH + (side + 1) * HALF
            flux_ref[last - 8 : last, :] = jnp.zeros((8, LANES), F32)

    count = count_ref[0]
    lane = (
        lax.broadcasted_iota(I32, (8, LANES), 0) * LANES + lax.broadcasted_iota(I32, (8, LANES), 1)
    )

    def chunk(index, carry):
        side, part = index // chunks, index % chunks
        pair, half = side % 2, side // 2
        faces = pl.ds(pl.multiple_of(side * blocks + part * 8, 8), 8)
        first = (pair * blocks + part * 8) * NODE_PITCH + half * HALF
        turn_faces(node_ref, first, NODE_PITCH, orient_ref[faces, :])
        alive = ((lane + part * (8 * LANES)) < count).astype(F32)
        scale = 0.5 * quotient_ref[faces, :] * alive
        sign = jnp.where(link_ref[faces, :] < 0, -1.0, 1.0)
        normal = [normal_ref[c, faces, :] for c in range(3)]
        target = part * (8 * FLUX_PITCH) + side * HALF
        for j in range(10):
            nodes = [node_ref[pl.ds(first + c * 10 + j, 8, stride=NODE_PITCH), :] for c in range(6)]
            electric = [value * sign for value in nodes[:3]]
            flux = face_flux(electric, nodes[3:], normal, scale)
            for c in range(6):
                flux_ref[pl.ds(target + c * 10 + j, 8, stride=FLUX_PITCH), :] = flux[c]
        return carry

    lax.fori_loop(0, 4 * chunks, chunk, 0)

    def lift(index, carry):
        rows = 4 * HALF
        first = pl.multiple_of(index * (2 * FLUX_PITCH), 8)
        second = pl.multiple_of(first + FLUX_PITCH, 8)
        value = jnp.concatenate(
            [flux_ref[pl.ds(first, rows), :], flux_ref[pl.ds(second, rows), :]], axis=1
        )
        high, low = split(value)
        coupled = dot(lift_hi_ref[...], high) + dot(lift_hi_ref[...], low) + dot(lift_lo_ref[...], high)
        base = pl.multiple_of(index * (2 * LANES), 2 * LANES)
        coupled_ref[pl.ds(base, 2 * LANES), :] = coupled.T
        return carry

    lax.fori_loop(0, blocks // 2, lift, 0, unroll=4)

    unroll = 16
    pos_copy.wait()
    tile_copy.wait()

    def place(index, carry):
        base = pl.multiple_of(index * unroll, unroll)
        for step in range(unroll):
            sorted_ref[pl.ds(pos_ref[base + step], 1), :] = coupled_ref[pl.ds(base + step, 1), :]
        return carry

    lax.fori_loop(0, elements // unroll, place, 0)

    class_copy.wait()

    def solve(index, carry):
        for step in range(GROUP):
            tile = index * GROUP + step
            base = pl.multiple_of(tile * TILE, TILE)
            high, low = split(sorted_ref[pl.ds(base, TILE), :])
            result = dot(jnp.concatenate([high, low], axis=0), class_ref[tile_ref[tile]])
            solved_ref[pl.ds(base, TILE), :] = result[:TILE] + result[TILE:]
        return carry

    lax.fori_loop(0, (tile_ref[4 * LANES] + (GROUP - 1)) // GROUP, solve, 0)

    def fetch(index, carry):
        base = pl.multiple_of(index * unroll, unroll)
        for step in range(unroll):
            image_ref[pl.ds(base + step, 1), :] = solved_ref[pl.ds(pos_ref[base + step], 1), :]
        return carry

    lax.fori_loop(0, elements // unroll, fetch, 0)


def image(part_count, indices, pos, tiles, table, lift_hi, lift_lo,
          link, orient, normal, quotient, classes):
    elements = pos.shape[0]
    slots = TILE_ROWS * TILE
    return pl.pallas_call(
        image_kernel,
        out_shape=jax.ShapeDtypeStruct((elements, LANES), F32),
        in_specs=[SMEM] + [ANY] * 3 + [VMEM] * 7 + [HBM],
        out_specs=VMEM,
        scratch_shapes=[
            pltpu.SMEM(indices.shape, I32),
            pltpu.SMEM(pos.shape, I32),
            pltpu.SMEM(tiles.shape, I32),
            pltpu.SemaphoreType.DMA((3,)),
            pltpu.VMEM(classes.shape, BF16),
            pltpu.SemaphoreType.DMA(()),
            pltpu.VMEM((2 * elements, LANES), F32),
            pltpu.VMEM((2 * elements // LANES * NODE_PITCH, LANES), F32),
            pltpu.VMEM((elements // LANES * FLUX_PITCH, LANES), F32),
            pltpu.VMEM((elements, LANES), F32),
            pltpu.VMEM((slots, LANES), F32),
            pltpu.VMEM((slots, LANES), F32),
        ],
        compiler_params=pltpu.CompilerParams(vmem_limit_bytes=44 * MIB),
        cost_estimate=cost(20),
        name="image",
    )(
        part_count, indices, pos, tiles, table, lift_hi, lift_lo,
        link.reshape(-1, LANES), orient.reshape(-1, LANES), normal,
        quotient.reshape(-1, LANES), classes,
    )


def gram_partials(first_ref, second_ref, third_ref, second_out, third_out, gram_ref):
    elements = first_ref.shape[0]

    def block(index, sums):
        rows = pl.ds(pl.multiple_of(index * LANES, LANES), LANES)
        f, t, u = first_ref[rows, :], second_ref[rows, :], third_ref[rows, :]
        second_out[:, rows] = t.T[:UNK]
        third_out[:, rows] = u.T[:UNK]
        pairs = (f * f, f * t, t * t, f * u, t * u, u * u)
        return tuple(
            total + jnp.sum(pair.reshape(LANES // 8, 8, LANES), axis=0)
            for total, pair in zip(sums, pairs)
        )

    zero = jnp.zeros((8, LANES), F32)
    sums = lax.fori_loop(0, elements // LANES, block, (zero,) * 6)
    for index in range(6):
        gram_ref[index : index + 1, :] = jnp.sum(sums[index], axis=0, keepdims=True)
    gram_ref[6:, :] = jnp.zeros((2, LANES), F32)


def total_kernel(grid_rows, grid_columns, first_ref, second_ref, third_ref,
                 total_ref, second_out, third_out, part_ref, over_rows, over_columns, send_row, recv_row, send_column, recv_column):
    row, column = lax.axis_index("prow"), lax.axis_index("pcol")

    def row_partner(step):
        return lax.rem(row + step, grid_rows)

    def column_partner(step):
        return lax.rem(column + step, grid_columns)

    barrier = pltpu.get_barrier_semaphore()
    for step in range(1, grid_rows):
        pl.semaphore_signal(
            barrier, inc=1, device_id=(row_partner(step), column), device_id_type=MESH
        )
    for step in range(1, grid_columns):
        pl.semaphore_signal(
            barrier, inc=1, device_id=(row, column_partner(step)), device_id_type=MESH
        )
    gram_partials(first_ref, second_ref, third_ref, second_out, third_out, part_ref)
    pl.semaphore_wait(barrier, grid_rows + grid_columns - 2)

    def row_copy(step):
        return pltpu.make_async_remote_copy(
            src_ref=part_ref,
            dst_ref=over_rows.at[step],
            send_sem=send_row,
            recv_sem=recv_row,
            device_id=(row_partner(step), column),
            device_id_type=MESH,
        )

    def wait_all(buffer, count, sem):
        landed = buffer.at[pl.ds(1, count)]
        pltpu.make_async_copy(landed, landed, sem).wait()

    for step in range(1, grid_rows):
        row_copy(step).start()
    over_rows[0] = part_ref[...]
    wait_all(over_rows, grid_rows - 1, recv_row)
    total = over_rows[row]
    for source in range(1, grid_rows):
        total = total + over_rows[lax.rem(row - source + grid_rows, grid_rows)]
    over_columns[0] = total

    def column_copy(step):
        return pltpu.make_async_remote_copy(
            src_ref=over_columns.at[0],
            dst_ref=over_columns.at[step],
            send_sem=send_column,
            recv_sem=recv_column,
            device_id=(row, column_partner(step)),
            device_id_type=MESH,
        )

    for step in range(1, grid_columns):
        column_copy(step).start()
    wait_all(over_columns, grid_columns - 1, recv_column)
    total = over_columns[column]
    for source in range(1, grid_columns):
        total = total + over_columns[lax.rem(column - source + grid_columns, grid_columns)]
    total_ref[...] = total
    wait_all(over_rows, grid_rows - 1, send_row)
    wait_all(over_columns, grid_columns - 1, send_column)


def total_over_devices(first, second, third):
    grid_rows, grid_columns = lax.axis_size("prow"), lax.axis_size("pcol")
    part = (8, LANES)
    return pl.pallas_call(
        functools.partial(total_kernel, grid_rows, grid_columns),
        out_shape=(
            jax.ShapeDtypeStruct(part, F32),
            jax.ShapeDtypeStruct((UNK, first.shape[0]), F32),
            jax.ShapeDtypeStruct((UNK, first.shape[0]), F32),
        ),
        in_specs=[VMEM] * 3,
        out_specs=(VMEM,) * 3,
        scratch_shapes=[
            pltpu.VMEM(part, F32),
            pltpu.VMEM((grid_rows,) + part, F32),
            pltpu.VMEM((grid_columns,) + part, F32),
            pltpu.SemaphoreType.DMA(()),
            pltpu.SemaphoreType.DMA(()),
            pltpu.SemaphoreType.DMA(()),
            pltpu.SemaphoreType.DMA(()),
        ],
        compiler_params=pltpu.CompilerParams(
            collective_id=1, has_side_effects=True, vmem_limit_bytes=8 * MIB
        ),
        cost_estimate=cost(12),
        name="total",
    )(first, second, third)


def finish_kernel(weight, count_ref, total_ref, field_ref, second_ref, third_ref, basis_ref, hess_ref):
    width = field_ref.shape[1]
    gram = jnp.sum(total_ref[...], axis=1, keepdims=True) * weight
    ff, ft, tt, fu, tu, uu = (gram[index : index + 1, :] for index in range(6))
    beta = jnp.sqrt(ff + EPSILON)
    square = beta * beta
    h00 = (ff + ft) / square
    p = (EPSILON - ft) / square
    h10 = jnp.sqrt((tt + 2 * p * ft + p * p * ff) / square + EPSILON)
    k1 = 1.0 / (beta * h10)
    h01 = k1 / beta * (fu + (1 + p) * ft + p * ff)
    h11 = k1 * k1 * (tu + (1 + p) * tt + p * ft + p * fu + p * (1 + p) * ft + p * p * ff)
    q = 1 + p - h11
    w = p * (1 - h11) - h01 * h10
    h21 = jnp.sqrt(
        k1 * k1 * (uu + 2 * q * tu + 2 * w * fu + q * q * tt + 2 * q * w * ft + w * w * ff)
        + EPSILON
    )
    k2 = k1 / h21

    alive = live_lanes(count_ref[0], pl.program_id(0) * width, width)
    f = field_ref[...] * alive
    t, u = second_ref[...], third_ref[...]
    basis_ref[0] = f * (1.0 / beta)
    basis_ref[1] = t * k1 + f * (p * k1)
    basis_ref[2] = u * k2 + t * (q * k2) + f * (w * k2)

    at_row = lax.broadcasted_iota(I32, (2, 3), 1)
    at_column = lax.broadcasted_iota(I32, (2, 3), 0)
    hess = jnp.zeros((2, 3), F32)
    for i, j, value in ((0, 0, h00), (1, 0, h10), (0, 1, h01), (1, 1, h11), (2, 1, h21)):
        hess = jnp.where(jnp.logical_and(at_row == i, at_column == j), value, hess)
    hess_ref[...] = hess


def finish(weight, part_count, total, right_side, second, third):
    elements = right_side.shape[1]
    width = 256
    field = pl.BlockSpec((UNK, width), lambda i: (0, i))
    return pl.pallas_call(
        functools.partial(finish_kernel, weight),
        grid=(elements // width,),
        out_shape=(
            jax.ShapeDtypeStruct((3, UNK, elements), F32),
            jax.ShapeDtypeStruct((2, 3), F32),
        ),
        in_specs=[
            pl.BlockSpec(memory_space=pltpu.SMEM),
            pl.BlockSpec((8, LANES), lambda i: (0, 0)),
            field, field, field,
        ],
        out_specs=(
            pl.BlockSpec((3, UNK, width), lambda i: (0, 0, i)),
            pl.BlockSpec((2, 3), lambda i: (0, 0)),
        ),
        compiler_params=pltpu.CompilerParams(vmem_limit_bytes=12 * MIB),
        name="finish",
    )(part_count, total, right_side, second, third)


def shards(
    right_side,
    part_count,
    elem_class,
    face_link,
    face_orient,
    face_normal,
    boundary_metric_quotient,
    bound_face,
    lift,
    inverse_table,
):
    unknowns, elements = right_side.shape
    all_subdomains = lax.axis_size("prow") * lax.axis_size("pcol")
    weight = 1.0 / (unknowns * elements * all_subdomains)
    native = jnp.transpose(inverse_table, (1, 2, 0))
    first, lists, selector = first_rows(part_count, right_side, bound_face[0])
    lists = lists.reshape(-1)
    first_table, classes = exchange(first, selector, lists, native)
    pos, tiles, indices, lift_hi, lift_lo, normal = prepare(
        first_table, elem_class, lift, face_link, face_normal, lists.shape[0]
    )
    pos, tiles, indices = pos.reshape(-1), tiles.reshape(-1), indices.reshape(-1)

    def operator_image(table):
        return image(
            part_count, indices, pos, tiles, table, lift_hi, lift_lo, face_link, face_orient,
            normal, boundary_metric_quotient, classes,
        )

    second = operator_image(first_table)
    (second_table,) = exchange(second, selector, lists)
    third = operator_image(second_table)
    total, second_columns, third_columns = total_over_devices(first, second, third)
    basis, hess = finish(weight, part_count, total, right_side, second_columns, third_columns)
    return (basis, hess.T)


def solution(mesh):
    in_specs = (
        P(None, ("prow", "pcol")),
        P(("prow", "pcol")),
        P(("prow", "pcol")),
        P(("prow", "pcol")),
        P(("prow", "pcol")),
        P(None, ("prow", "pcol")),
        P(("prow", "pcol")),
        P(("prow", "pcol"), None, None),
        P(),
        P(),
    )
    out_specs = (P(None, None, ("prow", "pcol")), P())
    return jax.shard_map(shards, mesh=mesh, in_specs=in_specs, out_specs=out_specs, check_vma=False)
```

```python
import functools

import jax
import jax.numpy as jnp
import numpy as np
from jax import lax
from jax.experimental import pallas as pl
from jax.experimental.pallas import tpu as pltpu
from jax.sharding import PartitionSpec as P

EPSILON = 1e-06
PERMUTATIONS = ((0, 1, 2), (0, 2, 1), (1, 0, 2), (1, 2, 0), (2, 0, 1), (2, 1, 0))
OFFSETS = tuple(((direction // 3 - 1, direction % 3 - 1) for direction in (0, 1, 2, 3, 5, 6, 7, 8)))
MESH = pl.DeviceIdType.MESH
F32, BF16, I32 = jnp.float32, jnp.bfloat16, jnp.int32
MIB = 1024 * 1024
UNK, CLASSES, LANES = 120, 256, 128
TILE = 16
HALF = 64
GROUP = 32
TILE_ROWS = 12 * GROUP
NODE_PITCH = 136
FLUX_PITCH = 264
STAGE_PITCH = 24
SLAB = 24
CHUNK = 16


def trace_tables():
    element_points = [
        (coord_a, coord_b, coord_c, 3 - coord_a - coord_b - coord_c)
        for coord_a in range(4)
        for coord_b in range(4 - coord_a)
        for coord_c in range(4 - coord_a - coord_b)
    ]
    face_points = [
        (coord_a, coord_b, 3 - coord_a - coord_b)
        for coord_a in range(4)
        for coord_b in range(4 - coord_a)
    ]
    select_rows = []
    for opposite in range(4):
        corners = [vertex for vertex in range(4) if vertex != opposite]
        members = []
        for triple in face_points:
            coords = [0, 0, 0, 0]
            for position in range(3):
                coords[corners[position]] = triple[position]
            members.append(element_points.index(tuple(coords)))
        select_rows.append(members)
    turn_rows = [
        [
            face_points.index((triple[sigma_row[0]], triple[sigma_row[1]], triple[sigma_row[2]]))
            for triple in face_points
        ]
        for sigma_row in PERMUTATIONS
    ]
    return select_rows, turn_rows


def trace_selector():
    select_rows, _ = trace_tables()
    column = lax.broadcasted_iota(I32, (1, 4 * HALF), 1)
    source = jnp.full((1, 4 * HALF), -1, I32)
    for side in range(4):
        for j in range(10):
            for c in range(6):
                here = column == side * HALF + c * 10 + j
                source = jnp.where(here, c * 20 + select_rows[side][j], source)
    row = lax.broadcasted_iota(I32, (2 * LANES, 4 * HALF), 0)
    row = jnp.where(row >= LANES, row - LANES, row)
    return (row == source).astype(F32).astype(BF16)


def split(value):
    high = value.astype(BF16)
    return high, (value - high.astype(F32)).astype(BF16)


def dot(a, b, dims=(((1,), (0,)), ((), ()))):
    return lax.dot_general(a, b, dims, preferred_element_type=F32)


VMEM = pl.BlockSpec(memory_space=pltpu.VMEM)
SMEM = pl.BlockSpec(memory_space=pltpu.SMEM)
ANY = pl.BlockSpec(memory_space=pl.ANY)
HBM = pl.BlockSpec(memory_space=pltpu.HBM)


def cost(microseconds):
    return pl.CostEstimate(
        flops=0, transcendentals=0, bytes_accessed=int(microseconds * 3_000_000)
    )


def live_lanes(count, first, width):
    return ((lax.broadcasted_iota(I32, (1, width), 1) + first) < count).astype(F32)


def rows_kernel(remote, count_ref, field_ref, list_ref, rows_ref, slot_ref, selector_ref):
    blocks = field_ref.shape[1] // LANES
    count = count_ref[0]
    for block in range(blocks):
        lanes = slice(block * LANES, (block + 1) * LANES)
        value = field_ref[:, lanes] * live_lanes(count, block * LANES, LANES)
        value = jnp.concatenate([value, jnp.zeros((LANES - UNK, LANES), F32)], axis=0)
        rows_ref[lanes, :] = value.T
    per_list = list_ref.shape[1] // LANES
    for index in range(8):
        for part in range(per_list):
            row = index * per_list + part
            face = list_ref[index : index + 1, part * LANES : (part + 1) * LANES]
            slot_ref[row : row + 1, :] = jnp.maximum(face, 0) + remote
    selector_ref[...] = trace_selector()


def first_rows(part_count, right_side, lists):
    remote = lists.shape[0] * lists.shape[1]
    return pl.pallas_call(
        functools.partial(rows_kernel, remote),
        out_shape=(
            jax.ShapeDtypeStruct((right_side.shape[1], LANES), F32),
            jax.ShapeDtypeStruct((remote // LANES, LANES), I32),
            jax.ShapeDtypeStruct((2 * LANES, 4 * HALF), BF16),
        ),
        in_specs=[SMEM, VMEM, VMEM],
        out_specs=(VMEM,) * 3,
        compiler_params=pltpu.CompilerParams(vmem_limit_bytes=4 * MIB),
        cost_estimate=cost(2),
        name="first_rows",
    )(part_count, right_side, lists)


def prep_kernel(
    remote, _, class_ref, lift_ref, link_ref, normal_ref,
    pos_ref, tile_ref, index_ref, lift_hi_ref, lift_lo_ref, plane_ref, spread_ref,
):
    blocks = class_ref.shape[0]

    class_row = lax.broadcasted_iota(I32, (CLASSES, LANES), 0)
    totals = jnp.zeros((CLASSES, LANES), F32)
    for block in range(blocks):
        totals = totals + (class_ref[block : block + 1, :] == class_row).astype(F32)
    total = jnp.sum(totals, axis=1, keepdims=True)
    tiles = jnp.floor((total + (TILE - 1)) * (1.0 / TILE))
    tiles = jnp.broadcast_to(tiles, (CLASSES, LANES))
    lower = (
        lax.broadcasted_iota(I32, (CLASSES, CLASSES), 1)
        < lax.broadcasted_iota(I32, (CLASSES, CLASSES), 0)
    ).astype(BF16)
    start = dot(lower, tiles.astype(BF16))
    end = start + tiles
    earlier = (
        lax.broadcasted_iota(I32, (LANES, 2 * LANES), 0)
        < lax.broadcasted_iota(I32, (LANES, 2 * LANES), 1)
    ).astype(BF16)
    carry = start * TILE
    for block in range(blocks):
        member = (class_ref[block : block + 1, :] == class_row).astype(F32)
        ranks = dot(member.astype(BF16), earlier)
        position = jnp.sum(member * (ranks[:, :LANES] + carry), axis=0, keepdims=True)
        pos_ref[block : block + 1, :] = position.astype(I32)
        carry = carry + ranks[:, LANES:]
    tile_ref[...] = jnp.zeros((8, LANES), I32)
    for row in range(4):
        tile = (lax.broadcasted_iota(I32, (CLASSES, LANES), 1) + row * LANES).astype(F32)
        owner = jnp.sum((end <= tile).astype(F32), axis=0, keepdims=True)
        tile_ref[row : row + 1, :] = jnp.minimum(owner.astype(I32), CLASSES - 1)
    tile_ref[4:5, :] = end[CLASSES - 1 :, :].astype(I32)

    spread_ref[...] = jnp.zeros(spread_ref.shape, F32)
    for side in range(4):
        block = lift_ref[:, side, :]
        for c in range(6):
            first = side * HALF + c * 10
            spread_ref[first : first + 10, c * 20 : (c + 1) * 20] = block
    high, low = split(spread_ref[...].T)
    lift_hi_ref[...] = high
    lift_lo_ref[...] = low

    link = link_ref[...]
    own = (
        lax.broadcasted_iota(I32, link.shape, 0) * LANES
        + lax.broadcasted_iota(I32, link.shape, 1)
        + remote
    )
    index_ref[...] = jnp.where(link < 0, own, link)

    for c in range(3):
        for row in range(link.shape[0]):
            plane_ref[c, row : row + 1, :] = normal_ref[c : c + 1, row * LANES : (row + 1) * LANES]


def prepare(after, elem_class, lift, link, normal, remote):
    elements, faces = elem_class.shape[0], link.shape[0]
    return pl.pallas_call(
        functools.partial(prep_kernel, remote),
        out_shape=(
            jax.ShapeDtypeStruct((elements // LANES, LANES), I32),
            jax.ShapeDtypeStruct((8, LANES), I32),
            jax.ShapeDtypeStruct((faces // LANES, LANES), I32),
            jax.ShapeDtypeStruct((LANES, 4 * HALF), BF16),
            jax.ShapeDtypeStruct((LANES, 4 * HALF), BF16),
            jax.ShapeDtypeStruct((3, faces // LANES, LANES), F32),
        ),
        in_specs=[ANY] + [VMEM] * 4,
        out_specs=(VMEM,) * 6,
        scratch_shapes=[pltpu.VMEM((4 * HALF, LANES), F32)],
        compiler_params=pltpu.CompilerParams(vmem_limit_bytes=4 * MIB),
        cost_estimate=cost(3),
        name="prepare",
    )(
        after, elem_class.reshape(elements // LANES, LANES), jnp.transpose(lift, (2, 0, 1)),
        link.reshape(faces // LANES, LANES), normal,
    )


def write_traces(rows_ref, selector_ref, table_ref, first):
    elements = rows_ref.shape[0]
    width = 2 * LANES
    left = lax.broadcasted_iota(I32, (width, LANES), 1) < HALF

    def block(index, carry):
        base = pl.multiple_of(index * width, width)
        high, low = split(rows_ref[pl.ds(base, width), :])
        traces = dot(jnp.concatenate([high, low], axis=1), selector_ref[...])
        for pair in range(2):
            both = traces[:, pair * LANES : (pair + 1) * LANES]
            swapped = pltpu.roll(both, HALF, 1)
            even, odd = first + 2 * pair * elements, first + (2 * pair + 1) * elements
            table_ref[pl.ds(even + base, width), :] = jnp.where(left, both, swapped)
            table_ref[pl.ds(odd + base, width), :] = jnp.where(left, swapped, both)
        return carry

    lax.fori_loop(0, elements // width, block, 0, unroll=4)


def gather_pairs(table_ref, index_ref, out_ref, first_a, first_b, offset, count, unroll):
    left = lax.broadcasted_iota(I32, (1, LANES), 1) < HALF

    def block(index, carry):
        base = pl.multiple_of(index * unroll, unroll)
        for step in range(unroll):
            row_a = table_ref[pl.ds(index_ref[first_a + base + step] + offset, 1), :]
            row_b = table_ref[pl.ds(index_ref[first_b + base + step] + offset, 1), :]
            out_ref[pl.ds(base + step, 1), :] = jnp.where(left, row_a, row_b)
        return carry

    lax.fori_loop(0, count // unroll, block, 0)


def element_order(solved_ref, pos_ref, rows_ref):
    unroll = 32

    def fetch(index, carry):
        base = pl.multiple_of(index * unroll, unroll)
        for step in range(unroll):
            rows_ref[pl.ds(base + step, 1), :] = solved_ref[pl.ds(pos_ref[base + step], 1), :]
        return carry

    lax.fori_loop(0, rows_ref.shape[0] // unroll, fetch, 0)


def class_major(native_ref, turned_ref, stage_ref, part_ref, class_hbm, sems):
    for half in range(2):
        for row in range(CHUNK):
            last = row * NODE_PITCH + UNK
            turned_ref[half, last : last + LANES - UNK, :] = jnp.zeros((LANES - UNK, LANES), F32)

    def store(first):
        slot = first // CHUNK % 2
        target = class_hbm.at[:, pl.ds(first, CHUNK), :]
        return pltpu.make_async_copy(part_ref.at[slot], target, sems.at[slot])

    for first in range(0, LANES, CHUNK):
        count = min(CHUNK, UNK - first)

        def collect(index, carry):
            value = native_ref[index, first : first + count, :].astype(F32)
            if count < CHUNK:
                value = jnp.concatenate([value, jnp.zeros((CHUNK - count, CLASSES), F32)], axis=0)
            for half in range(2):
                turned_ref[half, pl.ds(index, CHUNK, stride=NODE_PITCH), :] = value[
                    :, half * LANES : (half + 1) * LANES
                ]
            return carry

        lax.fori_loop(0, UNK, collect, 0, unroll=24)

        for row in range(CHUNK):
            for half in range(2):
                target = pl.ds(half * LANES * STAGE_PITCH + row, LANES, stride=STAGE_PITCH)
                rows = slice(row * NODE_PITCH, row * NODE_PITCH + LANES)
                stage_ref[target, :] = turned_ref[half, rows, :].T
        stage = stage_ref[...].reshape(CLASSES, STAGE_PITCH, LANES)[:, :CHUNK]
        if first >= 2 * CHUNK:
            store(first - 2 * CHUNK).wait()
        part_ref[first // CHUNK % 2] = stage.astype(BF16)
        store(first).start()
    return [store(LANES - 2 * CHUNK), store(LANES - CHUNK)]


def exchange_kernel(grid_rows, grid_columns, with_classes, *refs):
    if with_classes:
        (rows_ref, selector_ref, list_any, native_hbm, table_ref, class_hbm,
         list_ref, outgoing_ref, received_ref, local_sem, send_sem, recv_sem,
         native_ref, turned_ref, stage_ref, part_ref, native_sem, part_sems) = refs
        native_copy = pltpu.make_async_copy(native_hbm, native_ref, native_sem)
        native_copy.start()
    else:
        (solved_ref, pos_any, selector_ref, list_any, table_ref, rows_ref,
         list_ref, outgoing_ref, received_ref, local_sem, send_sem, recv_sem,
         pos_ref, pos_sem) = refs
        pos_copy = pltpu.make_async_copy(pos_any, pos_ref, pos_sem)
        pos_copy.start()
    list_copy = pltpu.make_async_copy(list_any, list_ref, local_sem)
    list_copy.start()
    slots = outgoing_ref.shape[1]
    row, column = lax.axis_index("prow"), lax.axis_index("pcol")

    def present(index):
        a, b = OFFSETS[index]
        inside = None
        for at, step, size in ((row, a, grid_rows), (column, b, grid_columns)):
            if step == 0:
                continue
            term = at > 0 if step < 0 else at < size - 1
            inside = term if inside is None else jnp.logical_and(inside, term)
        return inside

    def partner(index):
        a, b = OFFSETS[index]
        return (row + a, column + b)

    def transfer(index):
        return pltpu.make_async_remote_copy(
            src_ref=outgoing_ref.at[index],
            dst_ref=received_ref.at[7 - index],
            send_sem=send_sem.at[index],
            recv_sem=recv_sem.at[7 - index],
            device_id=partner(index),
            device_id_type=MESH,
        )

    barrier = pltpu.get_barrier_semaphore()
    for index in range(8):
        @pl.when(present(index))
        def _(index=index):
            pl.semaphore_signal(barrier, inc=1, device_id=partner(index), device_id_type=MESH)

    if not with_classes:
        pos_copy.wait()
        element_order(solved_ref, pos_ref, rows_ref)
    write_traces(rows_ref, selector_ref, table_ref, 16 * slots)
    list_copy.wait()

    def gather(index):
        first = index * 2 * slots
        gather_pairs(
            table_ref, list_ref, outgoing_ref.at[index], first, first + slots, 0, slots, 32
        )

    early, late = ((0, 2, 5, 7), (3, 4, 1, 6)) if with_classes else ((0,), (2, 5, 7, 3, 4, 1, 6))
    for index in early:
        gather(index)

    near_rows = 1 + (row > 0).astype(I32) + (row < grid_rows - 1).astype(I32)
    near_columns = 1 + (column > 0).astype(I32) + (column < grid_columns - 1).astype(I32)
    pl.semaphore_wait(barrier, near_rows * near_columns - 1)

    for index in early + late:
        if index in late:
            gather(index)

        @pl.when(present(index))
        def _(index=index):
            transfer(index).start()

    if with_classes:
        native_copy.wait()
        stores = class_major(native_ref, turned_ref, stage_ref, part_ref, class_hbm, part_sems)

    left = lax.broadcasted_iota(I32, (slots, LANES), 1) < HALF
    for index in (1, 6, 3, 4, 0, 2, 5, 7):
        @pl.when(present(index))
        def _(index=index):
            transfer(7 - index).wait_recv()
            packed = received_ref[index]
            swapped = pltpu.roll(packed, HALF, 1)
            first = index * 2 * slots
            table_ref[first : first + slots, :] = jnp.where(left, packed, swapped)
            table_ref[first + slots : first + 2 * slots, :] = jnp.where(left, swapped, packed)

    for index in range(8):
        @pl.when(present(index))
        def _(index=index):
            transfer(index).wait_send()

    if with_classes:
        for store in stores:
            store.wait()


def exchange(rows, selector, lists, native=None, pos=None):
    slots = lists.shape[0] // 16
    with_classes = native is not None
    elements = rows.shape[0] if with_classes else pos.shape[0]
    out_shape = [jax.ShapeDtypeStruct((16 * slots + 4 * elements, LANES), F32)]
    scratch = [
        pltpu.SMEM(lists.shape, I32),
        pltpu.VMEM((8, slots, LANES), F32),
        pltpu.VMEM((8, slots, LANES), F32),
        pltpu.SemaphoreType.DMA(()),
        pltpu.SemaphoreType.DMA((8,)),
        pltpu.SemaphoreType.DMA((8,)),
    ]
    if with_classes:
        operands = [rows, selector, lists, native]
        in_specs, out_specs = [VMEM, VMEM, ANY, HBM], (VMEM, HBM)
        out_shape.append(jax.ShapeDtypeStruct((CLASSES, LANES, LANES), BF16))
        scratch += [
            pltpu.VMEM(native.shape, BF16),
            pltpu.VMEM((2, CHUNK * NODE_PITCH, LANES), F32),
            pltpu.VMEM((CLASSES * STAGE_PITCH, LANES), F32),
            pltpu.VMEM((2, CLASSES, CHUNK, LANES), BF16),
            pltpu.SemaphoreType.DMA(()),
            pltpu.SemaphoreType.DMA((2,)),
        ]
    else:
        operands = [rows, pos, selector, lists]
        in_specs, out_specs = [VMEM, ANY, VMEM, ANY], (VMEM, VMEM)
        out_shape.append(jax.ShapeDtypeStruct((elements, LANES), F32))
        scratch += [pltpu.SMEM(pos.shape, I32), pltpu.SemaphoreType.DMA(())]
    return pl.pallas_call(
        functools.partial(
            exchange_kernel, lax.axis_size("prow"), lax.axis_size("pcol"), with_classes
        ),
        out_shape=tuple(out_shape),
        in_specs=in_specs,
        out_specs=out_specs,
        scratch_shapes=scratch,
        compiler_params=pltpu.CompilerParams(
            collective_id=2 if with_classes else 0, has_side_effects=True,
            vmem_limit_bytes=(44 if with_classes else 8) * MIB,
        ),
        cost_estimate=cost(14),
        name="exchange_first" if with_classes else "exchange",
    )(*operands)


def turn_choices():
    _, turn_rows = trace_tables()
    choices = []
    for j in range(10):
        sources = {}
        for option in range(6):
            sources.setdefault(turn_rows[option][j], []).append(option)
        choices.append([(source, tuple(options)) for source, options in sources.items()])
    return choices


def turn_faces(node_ref, first, stride, orient):
    masks = {}

    def mask(options):
        if options not in masks:
            value = orient == options[0]
            for option in options[1:]:
                value = jnp.logical_or(value, orient == option)
            masks[options] = value
        return masks[options]

    choices = turn_choices()
    for c in range(6):
        at = [pl.ds(first + c * 10 + j, 8, stride=stride) for j in range(10)]
        nodes = [node_ref[at[j], :] for j in range(10)]
        for j in range(10):
            (source, _), *others = choices[j]
            value = nodes[source]
            for source, options in others:
                value = jnp.where(mask(options), nodes[source], value)
            if others:
                node_ref[at[j], :] = value


def face_flux(electric, magnetic, normal, scale):
    along_e = normal[0] * electric[0] + normal[1] * electric[1] + normal[2] * electric[2]
    along_h = normal[0] * magnetic[0] + normal[1] * magnetic[1] + normal[2] * magnetic[2]
    flux = []
    for c in range(3):
        a, b = (c + 1) % 3, (c + 2) % 3
        cross = normal[a] * magnetic[b] - normal[b] * magnetic[a]
        flux.append(scale * (electric[c] - normal[c] * along_e - cross))
    for c in range(3):
        a, b = (c + 1) % 3, (c + 2) % 3
        cross = normal[a] * electric[b] - normal[b] * electric[a]
        flux.append(scale * (magnetic[c] - normal[c] * along_h + cross))
    return flux


def image_kernel(
    count_ref, index_any, pos_any, tile_any,
    table_ref, lift_hi_ref, lift_lo_ref,
    link_ref, orient_ref, normal_ref, quotient_ref, class_hbm,
    solved_ref,
    index_ref, pos_ref, tile_ref, smem_sems, class_ref, class_sem,
    picked_ref, node_ref, flux_ref, coupled_ref, sorted_ref,
):
    index_copy = pltpu.make_async_copy(index_any, index_ref, smem_sems.at[0])
    pos_copy = pltpu.make_async_copy(pos_any, pos_ref, smem_sems.at[1])
    tile_copy = pltpu.make_async_copy(tile_any, tile_ref, smem_sems.at[2])
    class_copy = pltpu.make_async_copy(class_hbm, class_ref, class_sem)
    for copy in (index_copy, pos_copy, tile_copy, class_copy):
        copy.start()
    elements = coupled_ref.shape[0]
    blocks = elements // LANES
    chunks = blocks // 8

    index_copy.wait()
    gather_pairs(table_ref, index_ref, picked_ref, 0, 2 * elements, 0, 2 * elements, 64)

    def transpose(index, carry):
        for step in range(4):
            block = index * 4 + step
            rows = pl.ds(pl.multiple_of(block * LANES, LANES), LANES)
            target = pl.multiple_of(block * NODE_PITCH, 8)
            node_ref[pl.ds(target, LANES), :] = picked_ref[rows, :].T
        return carry

    lax.fori_loop(0, 2 * blocks // 4, transpose, 0)

    for block in range(blocks):
        for side in range(4):
            last = block * FLUX_PITCH + (side + 1) * HALF
            flux_ref[last - 8 : last, :] = jnp.zeros((8, LANES), F32)

    count = count_ref[0]
    lane = (
        lax.broadcasted_iota(I32, (8, LANES), 0) * LANES + lax.broadcasted_iota(I32, (8, LANES), 1)
    )

    def chunk(index, carry):
        side, part = index // chunks, index % chunks
        pair, half = side % 2, side // 2
        faces = pl.ds(pl.multiple_of(side * blocks + part * 8, 8), 8)
        first = (pair * blocks + part * 8) * NODE_PITCH + half * HALF
        turn_faces(node_ref, first, NODE_PITCH, orient_ref[faces, :])
        alive = ((lane + part * (8 * LANES)) < count).astype(F32)
        scale = 0.5 * quotient_ref[faces, :] * alive
        sign = jnp.where(link_ref[faces, :] < 0, -1.0, 1.0)
        normal = [normal_ref[c, faces, :] for c in range(3)]
        target = part * (8 * FLUX_PITCH) + side * HALF
        for j in range(10):
            nodes = [node_ref[pl.ds(first + c * 10 + j, 8, stride=NODE_PITCH), :] for c in range(6)]
            electric = [value * sign for value in nodes[:3]]
            flux = face_flux(electric, nodes[3:], normal, scale)
            for c in range(6):
                flux_ref[pl.ds(target + c * 10 + j, 8, stride=FLUX_PITCH), :] = flux[c]
        return carry

    lax.fori_loop(0, 4 * chunks, chunk, 0)

    def lift(index, carry):
        rows = 4 * HALF
        first = pl.multiple_of(index * (2 * FLUX_PITCH), 8)
        second = pl.multiple_of(first + FLUX_PITCH, 8)
        value = jnp.concatenate(
            [flux_ref[pl.ds(first, rows), :], flux_ref[pl.ds(second, rows), :]], axis=1
        )
        high, low = split(value)
        coupled = dot(lift_hi_ref[...], high) + dot(lift_hi_ref[...], low) + dot(lift_lo_ref[...], high)
        base = pl.multiple_of(index * (2 * LANES), 2 * LANES)
        coupled_ref[pl.ds(base, 2 * LANES), :] = coupled.T
        return carry

    lax.fori_loop(0, blocks // 2, lift, 0, unroll=4)

    unroll = 16
    pos_copy.wait()
    tile_copy.wait()

    def place(index, carry):
        base = pl.multiple_of(index * unroll, unroll)
        for step in range(unroll):
            sorted_ref[pl.ds(pos_ref[base + step], 1), :] = coupled_ref[pl.ds(base + step, 1), :]
        return carry

    lax.fori_loop(0, elements // unroll, place, 0)

    class_copy.wait()

    def solve(index, carry):
        for step in range(GROUP):
            tile = index * GROUP + step
            base = pl.multiple_of(tile * TILE, TILE)
            high, low = split(sorted_ref[pl.ds(base, TILE), :])
            result = dot(jnp.concatenate([high, low], axis=0), class_ref[tile_ref[tile]])
            solved_ref[pl.ds(base, TILE), :] = result[:TILE] + result[TILE:]
        return carry

    lax.fori_loop(0, (tile_ref[4 * LANES] + (GROUP - 1)) // GROUP, solve, 0)


def image(part_count, indices, pos, tiles, table, lift_hi, lift_lo,
          link, orient, normal, quotient, classes):
    elements = pos.shape[0]
    slots = TILE_ROWS * TILE
    return pl.pallas_call(
        image_kernel,
        out_shape=jax.ShapeDtypeStruct((slots, LANES), F32),
        in_specs=[SMEM] + [ANY] * 3 + [VMEM] * 7 + [HBM],
        out_specs=VMEM,
        scratch_shapes=[
            pltpu.SMEM(indices.shape, I32),
            pltpu.SMEM(pos.shape, I32),
            pltpu.SMEM(tiles.shape, I32),
            pltpu.SemaphoreType.DMA((3,)),
            pltpu.VMEM(classes.shape, BF16),
            pltpu.SemaphoreType.DMA(()),
            pltpu.VMEM((2 * elements, LANES), F32),
            pltpu.VMEM((2 * elements // LANES * NODE_PITCH, LANES), F32),
            pltpu.VMEM((elements // LANES * FLUX_PITCH, LANES), F32),
            pltpu.VMEM((elements, LANES), F32),
            pltpu.VMEM((slots, LANES), F32),
        ],
        compiler_params=pltpu.CompilerParams(vmem_limit_bytes=44 * MIB),
        cost_estimate=cost(20),
        name="image",
    )(
        part_count, indices, pos, tiles, table, lift_hi, lift_lo,
        link.reshape(-1, LANES), orient.reshape(-1, LANES), normal,
        quotient.reshape(-1, LANES), classes,
    )


def gram_partials(first_ref, second_ref, third_ref, second_out, third_out, gram_ref):
    elements = first_ref.shape[0]

    def block(index, sums):
        rows = pl.ds(pl.multiple_of(index * LANES, LANES), LANES)
        f, t, u = first_ref[rows, :], second_ref[rows, :], third_ref[rows, :]
        second_out[:, rows] = t.T[:UNK]
        third_out[:, rows] = u.T[:UNK]
        pairs = (f * f, f * t, t * t, f * u, t * u, u * u)
        return tuple(
            total + jnp.sum(pair.reshape(LANES // 8, 8, LANES), axis=0)
            for total, pair in zip(sums, pairs)
        )

    zero = jnp.zeros((8, LANES), F32)
    sums = lax.fori_loop(0, elements // LANES, block, (zero,) * 6)
    for index in range(6):
        gram_ref[index : index + 1, :] = jnp.sum(sums[index], axis=0, keepdims=True)
    gram_ref[6:, :] = jnp.zeros((2, LANES), F32)


def total_kernel(grid_rows, grid_columns, first_ref, second_ref, solved_ref, pos_any,
                 total_ref, second_out, third_out, third_ref, pos_ref, pos_sem, part_ref, over_rows, over_columns, send_row, recv_row, send_column, recv_column):
    row, column = lax.axis_index("prow"), lax.axis_index("pcol")
    pos_copy = pltpu.make_async_copy(pos_any, pos_ref, pos_sem)
    pos_copy.start()

    def row_partner(step):
        return lax.rem(row + step, grid_rows)

    def column_partner(step):
        return lax.rem(column + step, grid_columns)

    barrier = pltpu.get_barrier_semaphore()
    for step in range(1, grid_rows):
        pl.semaphore_signal(
            barrier, inc=1, device_id=(row_partner(step), column), device_id_type=MESH
        )
    for step in range(1, grid_columns):
        pl.semaphore_signal(
            barrier, inc=1, device_id=(row, column_partner(step)), device_id_type=MESH
        )
    pos_copy.wait()
    element_order(solved_ref, pos_ref, third_ref)
    gram_partials(first_ref, second_ref, third_ref, second_out, third_out, part_ref)
    pl.semaphore_wait(barrier, grid_rows + grid_columns - 2)

    def row_copy(step):
        return pltpu.make_async_remote_copy(
            src_ref=part_ref,
            dst_ref=over_rows.at[step],
            send_sem=send_row,
            recv_sem=recv_row,
            device_id=(row_partner(step), column),
            device_id_type=MESH,
        )

    def wait_all(buffer, count, sem):
        landed = buffer.at[pl.ds(1, count)]
        pltpu.make_async_copy(landed, landed, sem).wait()

    for step in range(1, grid_rows):
        row_copy(step).start()
    over_rows[0] = part_ref[...]
    wait_all(over_rows, grid_rows - 1, recv_row)
    total = over_rows[row]
    for source in range(1, grid_rows):
        total = total + over_rows[lax.rem(row - source + grid_rows, grid_rows)]
    over_columns[0] = total

    def column_copy(step):
        return pltpu.make_async_remote_copy(
            src_ref=over_columns.at[0],
            dst_ref=over_columns.at[step],
            send_sem=send_column,
            recv_sem=recv_column,
            device_id=(row, column_partner(step)),
            device_id_type=MESH,
        )

    for step in range(1, grid_columns):
        column_copy(step).start()
    wait_all(over_columns, grid_columns - 1, recv_column)
    total = over_columns[column]
    for source in range(1, grid_columns):
        total = total + over_columns[lax.rem(column - source + grid_columns, grid_columns)]
    total_ref[...] = total
    wait_all(over_rows, grid_rows - 1, send_row)
    wait_all(over_columns, grid_columns - 1, send_column)


def total_over_devices(first, second, solved, pos):
    grid_rows, grid_columns = lax.axis_size("prow"), lax.axis_size("pcol")
    part = (8, LANES)
    return pl.pallas_call(
        functools.partial(total_kernel, grid_rows, grid_columns),
        out_shape=(
            jax.ShapeDtypeStruct(part, F32),
            jax.ShapeDtypeStruct((UNK, first.shape[0]), F32),
            jax.ShapeDtypeStruct((UNK, first.shape[0]), F32),
        ),
        in_specs=[VMEM] * 3 + [ANY],
        out_specs=(VMEM,) * 3,
        scratch_shapes=[
            pltpu.VMEM(first.shape, F32),
            pltpu.SMEM(pos.shape, I32),
            pltpu.SemaphoreType.DMA(()),
            pltpu.VMEM(part, F32),
            pltpu.VMEM((grid_rows,) + part, F32),
            pltpu.VMEM((grid_columns,) + part, F32),
            pltpu.SemaphoreType.DMA(()),
            pltpu.SemaphoreType.DMA(()),
            pltpu.SemaphoreType.DMA(()),
            pltpu.SemaphoreType.DMA(()),
        ],
        compiler_params=pltpu.CompilerParams(
            collective_id=1, has_side_effects=True, vmem_limit_bytes=8 * MIB
        ),
        cost_estimate=cost(12),
        name="total",
    )(first, second, solved, pos)


def finish_kernel(
    weight, count_ref, total_ref, field_ref, second_ref, third_ref, basis_hbm, hess_ref,
    basis_ref, sems,
):
    width = field_ref.shape[1]
    gram = jnp.sum(total_ref[...], axis=1, keepdims=True) * weight
    ff, ft, tt, fu, tu, uu = (gram[index : index + 1, :] for index in range(6))
    beta = jnp.sqrt(ff + EPSILON)
    square = beta * beta
    h00 = (ff + ft) / square
    p = (EPSILON - ft) / square
    h10 = jnp.sqrt((tt + 2 * p * ft + p * p * ff) / square + EPSILON)
    k1 = 1.0 / (beta * h10)
    h01 = k1 / beta * (fu + (1 + p) * ft + p * ff)
    h11 = k1 * k1 * (tu + (1 + p) * tt + p * ft + p * fu + p * (1 + p) * ft + p * p * ff)
    q = 1 + p - h11
    w = p * (1 - h11) - h01 * h10
    h21 = jnp.sqrt(
        k1 * k1 * (uu + 2 * q * tu + 2 * w * fu + q * q * tt + 2 * q * w * ft + w * w * ff)
        + EPSILON
    )
    k2 = k1 / h21

    alive = live_lanes(count_ref[0], 0, width)
    copies = []
    for first in range(0, UNK, SLAB):
        rows = pl.ds(first, SLAB)
        f = field_ref[rows, :] * alive
        t, u = second_ref[rows, :], third_ref[rows, :]
        basis_ref[0, rows, :] = f * (1.0 / beta)
        basis_ref[1, rows, :] = t * k1 + f * (p * k1)
        basis_ref[2, rows, :] = u * k2 + t * (q * k2) + f * (w * k2)
        at = (slice(None), rows, slice(None))
        copies.append(
            pltpu.make_async_copy(basis_ref.at[at], basis_hbm.at[at], sems.at[first // SLAB])
        )
        copies[-1].start()

    at_row = lax.broadcasted_iota(I32, (2, 3), 1)
    at_column = lax.broadcasted_iota(I32, (2, 3), 0)
    hess = jnp.zeros((2, 3), F32)
    for i, j, value in ((0, 0, h00), (1, 0, h10), (0, 1, h01), (1, 1, h11), (2, 1, h21)):
        hess = jnp.where(jnp.logical_and(at_row == i, at_column == j), value, hess)
    hess_ref[...] = hess
    for copy in copies:
        copy.wait()


def finish(weight, part_count, total, right_side, second, third):
    elements = right_side.shape[1]
    return pl.pallas_call(
        functools.partial(finish_kernel, weight),
        out_shape=(
            jax.ShapeDtypeStruct((3, UNK, elements), F32),
            jax.ShapeDtypeStruct((2, 3), F32),
        ),
        in_specs=[SMEM] + [VMEM] * 4,
        out_specs=(HBM, VMEM),
        scratch_shapes=[
            pltpu.VMEM((3, UNK, elements), F32),
            pltpu.SemaphoreType.DMA((UNK // SLAB,)),
        ],
        compiler_params=pltpu.CompilerParams(vmem_limit_bytes=12 * MIB),
        name="finish",
    )(part_count, total, right_side, second, third)


def shards(
    right_side,
    part_count,
    elem_class,
    face_link,
    face_orient,
    face_normal,
    boundary_metric_quotient,
    bound_face,
    lift,
    inverse_table,
):
    unknowns, elements = right_side.shape
    all_subdomains = lax.axis_size("prow") * lax.axis_size("pcol")
    weight = 1.0 / (unknowns * elements * all_subdomains)
    native = jnp.transpose(inverse_table, (1, 2, 0))
    first, lists, selector = first_rows(part_count, right_side, bound_face[0])
    lists = lists.reshape(-1)
    first_table, classes = exchange(first, selector, lists, native)
    pos, tiles, indices, lift_hi, lift_lo, normal = prepare(
        first_table, elem_class, lift, face_link, face_normal, lists.shape[0]
    )
    pos, tiles, indices = pos.reshape(-1), tiles.reshape(-1), indices.reshape(-1)

    def operator_image(table):
        return image(
            part_count, indices, pos, tiles, table, lift_hi, lift_lo, face_link, face_orient,
            normal, boundary_metric_quotient, classes,
        )

    solved = operator_image(first_table)
    second_table, second = exchange(solved, selector, lists, pos=pos)
    solved = operator_image(second_table)
    total, second_columns, third_columns = total_over_devices(first, second, solved, pos)
    basis, hess = finish(weight, part_count, total, right_side, second_columns, third_columns)
    return (basis, hess.T)


def solution(mesh):
    in_specs = (
        P(None, ("prow", "pcol")),
        P(("prow", "pcol")),
        P(("prow", "pcol")),
        P(("prow", "pcol")),
        P(("prow", "pcol")),
        P(None, ("prow", "pcol")),
        P(("prow", "pcol")),
        P(("prow", "pcol"), None, None),
        P(),
        P(),
    )
    out_specs = (P(None, None, ("prow", "pcol")), P())
    return jax.shard_map(shards, mesh=mesh, in_specs=in_specs, out_specs=out_specs, check_vma=False)
```

```python
import functools

import jax
import jax.numpy as jnp
import numpy as np
from jax import lax
from jax.experimental import pallas as pl
from jax.experimental.pallas import tpu as pltpu
from jax.sharding import PartitionSpec as P

EPSILON = 1e-06
PERMUTATIONS = ((0, 1, 2), (0, 2, 1), (1, 0, 2), (1, 2, 0), (2, 0, 1), (2, 1, 0))
OFFSETS = tuple(((direction // 3 - 1, direction % 3 - 1) for direction in (0, 1, 2, 3, 5, 6, 7, 8)))
MESH = pl.DeviceIdType.MESH
F32, BF16, I32 = jnp.float32, jnp.bfloat16, jnp.int32
MIB = 1024 * 1024
UNK, CLASSES, LANES = 120, 256, 128
TILE = 16
HALF = 64
GROUP = 32
TILE_ROWS = 12 * GROUP
NODE_PITCH = 136
FLUX_PITCH = 264
STAGE_PITCH = 24
SLAB = 24
CHUNK = 16


def trace_tables():
    element_points = [
        (coord_a, coord_b, coord_c, 3 - coord_a - coord_b - coord_c)
        for coord_a in range(4)
        for coord_b in range(4 - coord_a)
        for coord_c in range(4 - coord_a - coord_b)
    ]
    face_points = [
        (coord_a, coord_b, 3 - coord_a - coord_b)
        for coord_a in range(4)
        for coord_b in range(4 - coord_a)
    ]
    select_rows = []
    for opposite in range(4):
        corners = [vertex for vertex in range(4) if vertex != opposite]
        members = []
        for triple in face_points:
            coords = [0, 0, 0, 0]
            for position in range(3):
                coords[corners[position]] = triple[position]
            members.append(element_points.index(tuple(coords)))
        select_rows.append(members)
    turn_rows = [
        [
            face_points.index((triple[sigma_row[0]], triple[sigma_row[1]], triple[sigma_row[2]]))
            for triple in face_points
        ]
        for sigma_row in PERMUTATIONS
    ]
    return select_rows, turn_rows


def trace_selector():
    select_rows, _ = trace_tables()
    column = lax.broadcasted_iota(I32, (1, 4 * HALF), 1)
    source = jnp.full((1, 4 * HALF), -1, I32)
    for side in range(4):
        for j in range(10):
            for c in range(6):
                here = column == side * HALF + c * 10 + j
                source = jnp.where(here, c * 20 + select_rows[side][j], source)
    row = lax.broadcasted_iota(I32, (2 * LANES, 4 * HALF), 0)
    row = jnp.where(row >= LANES, row - LANES, row)
    return (row == source).astype(F32).astype(BF16)


def split(value):
    high = value.astype(BF16)
    return high, (value - high.astype(F32)).astype(BF16)


def dot(a, b, dims=(((1,), (0,)), ((), ()))):
    return lax.dot_general(a, b, dims, preferred_element_type=F32)


VMEM = pl.BlockSpec(memory_space=pltpu.VMEM)
SMEM = pl.BlockSpec(memory_space=pltpu.SMEM)
ANY = pl.BlockSpec(memory_space=pl.ANY)
HBM = pl.BlockSpec(memory_space=pltpu.HBM)


def cost(microseconds):
    return pl.CostEstimate(
        flops=0, transcendentals=0, bytes_accessed=int(microseconds * 3_000_000)
    )


def live_lanes(count, first, width):
    return ((lax.broadcasted_iota(I32, (1, width), 1) + first) < count).astype(F32)


def rows_kernel(remote, count_ref, field_ref, list_ref, rows_ref, slot_ref, selector_ref):
    blocks = field_ref.shape[1] // LANES
    count = count_ref[0]
    for block in range(blocks):
        lanes = slice(block * LANES, (block + 1) * LANES)
        value = field_ref[:, lanes] * live_lanes(count, block * LANES, LANES)
        value = jnp.concatenate([value, jnp.zeros((LANES - UNK, LANES), F32)], axis=0)
        rows_ref[lanes, :] = value.T
    per_list = list_ref.shape[1] // LANES
    for index in range(8):
        for part in range(per_list):
            row = index * per_list + part
            face = list_ref[index : index + 1, part * LANES : (part + 1) * LANES]
            slot_ref[row : row + 1, :] = jnp.maximum(face, 0) + remote
    selector_ref[...] = trace_selector()


def first_rows(part_count, right_side, lists):
    remote = lists.shape[0] * lists.shape[1]
    return pl.pallas_call(
        functools.partial(rows_kernel, remote),
        out_shape=(
            jax.ShapeDtypeStruct((right_side.shape[1], LANES), F32),
            jax.ShapeDtypeStruct((remote // LANES, LANES), I32),
            jax.ShapeDtypeStruct((2 * LANES, 4 * HALF), BF16),
        ),
        in_specs=[SMEM, VMEM, VMEM],
        out_specs=(VMEM,) * 3,
        compiler_params=pltpu.CompilerParams(vmem_limit_bytes=4 * MIB),
        cost_estimate=cost(2),
        name="first_rows",
    )(part_count, right_side, lists)


def prep_kernel(
    remote, _, class_ref, lift_ref, link_ref, normal_ref,
    pos_ref, tile_ref, index_ref, lift_hi_ref, lift_lo_ref, plane_ref, spread_ref,
):
    blocks = class_ref.shape[0]

    class_row = lax.broadcasted_iota(I32, (CLASSES, LANES), 0)
    totals = jnp.zeros((CLASSES, LANES), F32)
    for block in range(blocks):
        totals = totals + (class_ref[block : block + 1, :] == class_row).astype(F32)
    total = jnp.sum(totals, axis=1, keepdims=True)
    tiles = jnp.floor((total + (TILE - 1)) * (1.0 / TILE))
    tiles = jnp.broadcast_to(tiles, (CLASSES, LANES))
    lower = (
        lax.broadcasted_iota(I32, (CLASSES, CLASSES), 1)
        < lax.broadcasted_iota(I32, (CLASSES, CLASSES), 0)
    ).astype(BF16)
    start = dot(lower, tiles.astype(BF16))
    end = start + tiles
    earlier = (
        lax.broadcasted_iota(I32, (LANES, 2 * LANES), 0)
        < lax.broadcasted_iota(I32, (LANES, 2 * LANES), 1)
    ).astype(BF16)
    carry = start * TILE
    for block in range(blocks):
        member = (class_ref[block : block + 1, :] == class_row).astype(F32)
        ranks = dot(member.astype(BF16), earlier)
        position = jnp.sum(member * (ranks[:, :LANES] + carry), axis=0, keepdims=True)
        pos_ref[block : block + 1, :] = position.astype(I32)
        carry = carry + ranks[:, LANES:]
    tile_ref[...] = jnp.zeros((8, LANES), I32)
    for row in range(4):
        tile = (lax.broadcasted_iota(I32, (CLASSES, LANES), 1) + row * LANES).astype(F32)
        owner = jnp.sum((end <= tile).astype(F32), axis=0, keepdims=True)
        tile_ref[row : row + 1, :] = jnp.minimum(owner.astype(I32), CLASSES - 1)
    tile_ref[4:5, :] = end[CLASSES - 1 :, :].astype(I32)

    spread_ref[...] = jnp.zeros(spread_ref.shape, F32)
    for side in range(4):
        block = lift_ref[:, side, :]
        for c in range(6):
            first = side * HALF + c * 10
            spread_ref[first : first + 10, c * 20 : (c + 1) * 20] = block
    high, low = split(spread_ref[...].T)
    lift_hi_ref[...] = high
    lift_lo_ref[...] = low

    link = link_ref[...]
    own = (
        lax.broadcasted_iota(I32, link.shape, 0) * LANES
        + lax.broadcasted_iota(I32, link.shape, 1)
        + remote
    )
    index_ref[...] = jnp.where(link < 0, own, link)

    for c in range(3):
        for row in range(link.shape[0]):
            plane_ref[c, row : row + 1, :] = normal_ref[c : c + 1, row * LANES : (row + 1) * LANES]


def prepare(after, elem_class, lift, link, normal, remote):
    elements, faces = elem_class.shape[0], link.shape[0]
    return pl.pallas_call(
        functools.partial(prep_kernel, remote),
        out_shape=(
            jax.ShapeDtypeStruct((elements // LANES, LANES), I32),
            jax.ShapeDtypeStruct((8, LANES), I32),
            jax.ShapeDtypeStruct((faces // LANES, LANES), I32),
            jax.ShapeDtypeStruct((LANES, 4 * HALF), BF16),
            jax.ShapeDtypeStruct((LANES, 4 * HALF), BF16),
            jax.ShapeDtypeStruct((3, faces // LANES, LANES), F32),
        ),
        in_specs=[ANY] + [VMEM] * 4,
        out_specs=(VMEM,) * 6,
        scratch_shapes=[pltpu.VMEM((4 * HALF, LANES), F32)],
        compiler_params=pltpu.CompilerParams(vmem_limit_bytes=4 * MIB),
        cost_estimate=cost(3),
        name="prepare",
    )(
        after, elem_class.reshape(elements // LANES, LANES), jnp.transpose(lift, (2, 0, 1)),
        link.reshape(faces // LANES, LANES), normal,
    )


def trace_block(rows_ref, selector_ref, table_ref, first, index):
    elements = rows_ref.shape[0]
    width = 2 * LANES
    left = lax.broadcasted_iota(I32, (width, LANES), 1) < HALF
    base = pl.multiple_of(index * width, width)
    high, low = split(rows_ref[pl.ds(base, width), :])
    traces = dot(jnp.concatenate([high, low], axis=1), selector_ref[...])
    for pair in range(2):
        both = traces[:, pair * LANES : (pair + 1) * LANES]
        swapped = pltpu.roll(both, HALF, 1)
        even, odd = first + 2 * pair * elements, first + (2 * pair + 1) * elements
        table_ref[pl.ds(even + base, width), :] = jnp.where(left, both, swapped)
        table_ref[pl.ds(odd + base, width), :] = jnp.where(left, swapped, both)


def write_traces(rows_ref, selector_ref, table_ref, first):
    def block(index, carry):
        trace_block(rows_ref, selector_ref, table_ref, first, index)
        return carry

    lax.fori_loop(0, rows_ref.shape[0] // (2 * LANES), block, 0, unroll=4)


def staggered(count, before, after):
    before(0)

    def body(index, carry):
        after(index - 1)
        before(index)
        return carry

    lax.fori_loop(1, count, body, 0)
    after(count - 1)


def gather_pairs(table_ref, index_ref, out_ref, first_a, first_b, offset, count, unroll):
    left = lax.broadcasted_iota(I32, (1, LANES), 1) < HALF

    def block(index, carry):
        base = pl.multiple_of(index * unroll, unroll)
        for step in range(unroll):
            row_a = table_ref[pl.ds(index_ref[first_a + base + step] + offset, 1), :]
            row_b = table_ref[pl.ds(index_ref[first_b + base + step] + offset, 1), :]
            out_ref[pl.ds(base + step, 1), :] = jnp.where(left, row_a, row_b)
        return carry

    lax.fori_loop(0, count // unroll, block, 0)


def element_order(solved_ref, pos_ref, rows_ref):
    unroll = 64

    def fetch(index, carry):
        base = pl.multiple_of(index * unroll, unroll)
        for step in range(unroll):
            rows_ref[pl.ds(base + step, 1), :] = solved_ref[pl.ds(pos_ref[base + step], 1), :]
        return carry

    lax.fori_loop(0, rows_ref.shape[0] // unroll, fetch, 0)


def class_major(native_ref, turned_ref, stage_ref, part_ref, class_hbm, sems):
    for half in range(2):
        for row in range(CHUNK):
            last = row * NODE_PITCH + UNK
            turned_ref[half, last : last + LANES - UNK, :] = jnp.zeros((LANES - UNK, LANES), F32)

    def store(first):
        slot = first // CHUNK % 2
        target = class_hbm.at[:, pl.ds(first, CHUNK), :]
        return pltpu.make_async_copy(part_ref.at[slot], target, sems.at[slot])

    for first in range(0, LANES, CHUNK):
        count = min(CHUNK, UNK - first)

        def collect(index, carry):
            value = native_ref[index, first : first + count, :].astype(F32)
            if count < CHUNK:
                value = jnp.concatenate([value, jnp.zeros((CHUNK - count, CLASSES), F32)], axis=0)
            for half in range(2):
                turned_ref[half, pl.ds(index, CHUNK, stride=NODE_PITCH), :] = value[
                    :, half * LANES : (half + 1) * LANES
                ]
            return carry

        lax.fori_loop(0, UNK, collect, 0, unroll=24)

        for row in range(CHUNK):
            for half in range(2):
                target = pl.ds(half * LANES * STAGE_PITCH + row, LANES, stride=STAGE_PITCH)
                rows = slice(row * NODE_PITCH, row * NODE_PITCH + LANES)
                stage_ref[target, :] = turned_ref[half, rows, :].T
        stage = stage_ref[...].reshape(CLASSES, STAGE_PITCH, LANES)[:, :CHUNK]
        if first >= 2 * CHUNK:
            store(first - 2 * CHUNK).wait()
        part_ref[first // CHUNK % 2] = stage.astype(BF16)
        store(first).start()
    return [store(LANES - 2 * CHUNK), store(LANES - CHUNK)]


def exchange_kernel(grid_rows, grid_columns, with_classes, *refs):
    if with_classes:
        (rows_ref, selector_ref, list_any, native_hbm, table_ref, class_hbm,
         list_ref, outgoing_ref, received_ref, local_sem, send_sem, recv_sem,
         native_ref, turned_ref, stage_ref, part_ref, native_sem, part_sems) = refs
        native_copy = pltpu.make_async_copy(native_hbm, native_ref, native_sem)
        native_copy.start()
    else:
        (solved_ref, pos_any, selector_ref, list_any, table_ref, rows_ref,
         list_ref, outgoing_ref, received_ref, local_sem, send_sem, recv_sem,
         pos_ref, pos_sem) = refs
        pos_copy = pltpu.make_async_copy(pos_any, pos_ref, pos_sem)
        pos_copy.start()
    list_copy = pltpu.make_async_copy(list_any, list_ref, local_sem)
    list_copy.start()
    slots = outgoing_ref.shape[1]
    row, column = lax.axis_index("prow"), lax.axis_index("pcol")

    def present(index):
        a, b = OFFSETS[index]
        inside = None
        for at, step, size in ((row, a, grid_rows), (column, b, grid_columns)):
            if step == 0:
                continue
            term = at > 0 if step < 0 else at < size - 1
            inside = term if inside is None else jnp.logical_and(inside, term)
        return inside

    def partner(index):
        a, b = OFFSETS[index]
        return (row + a, column + b)

    def transfer(index):
        return pltpu.make_async_remote_copy(
            src_ref=outgoing_ref.at[index],
            dst_ref=received_ref.at[7 - index],
            send_sem=send_sem.at[index],
            recv_sem=recv_sem.at[7 - index],
            device_id=partner(index),
            device_id_type=MESH,
        )

    barrier = pltpu.get_barrier_semaphore()
    for index in range(8):
        @pl.when(present(index))
        def _(index=index):
            pl.semaphore_signal(barrier, inc=1, device_id=partner(index), device_id_type=MESH)

    if not with_classes:
        pos_copy.wait()
        element_order(solved_ref, pos_ref, rows_ref)
    write_traces(rows_ref, selector_ref, table_ref, 16 * slots)
    list_copy.wait()

    def gather(index):
        first = index * 2 * slots
        gather_pairs(
            table_ref, list_ref, outgoing_ref.at[index], first, first + slots, 0, slots, 32
        )

    early, late = ((0, 2, 5, 7), (3, 4, 1, 6)) if with_classes else ((0,), (2, 5, 7, 3, 4, 1, 6))
    for index in early:
        gather(index)

    near_rows = 1 + (row > 0).astype(I32) + (row < grid_rows - 1).astype(I32)
    near_columns = 1 + (column > 0).astype(I32) + (column < grid_columns - 1).astype(I32)
    pl.semaphore_wait(barrier, near_rows * near_columns - 1)

    for index in early + late:
        if index in late:
            gather(index)

        @pl.when(present(index))
        def _(index=index):
            transfer(index).start()

    if with_classes:
        native_copy.wait()
        stores = class_major(native_ref, turned_ref, stage_ref, part_ref, class_hbm, part_sems)

    left = lax.broadcasted_iota(I32, (slots, LANES), 1) < HALF
    for index in (1, 6, 3, 4, 0, 2, 5, 7):
        @pl.when(present(index))
        def _(index=index):
            transfer(7 - index).wait_recv()
            packed = received_ref[index]
            swapped = pltpu.roll(packed, HALF, 1)
            first = index * 2 * slots
            table_ref[first : first + slots, :] = jnp.where(left, packed, swapped)
            table_ref[first + slots : first + 2 * slots, :] = jnp.where(left, swapped, packed)

    for index in range(8):
        @pl.when(present(index))
        def _(index=index):
            transfer(index).wait_send()

    if with_classes:
        for store in stores:
            store.wait()


def exchange(rows, selector, lists, native=None, pos=None):
    slots = lists.shape[0] // 16
    with_classes = native is not None
    elements = rows.shape[0] if with_classes else pos.shape[0]
    out_shape = [jax.ShapeDtypeStruct((16 * slots + 4 * elements, LANES), F32)]
    scratch = [
        pltpu.SMEM(lists.shape, I32),
        pltpu.VMEM((8, slots, LANES), F32),
        pltpu.VMEM((8, slots, LANES), F32),
        pltpu.SemaphoreType.DMA(()),
        pltpu.SemaphoreType.DMA((8,)),
        pltpu.SemaphoreType.DMA((8,)),
    ]
    if with_classes:
        operands = [rows, selector, lists, native]
        in_specs, out_specs = [VMEM, VMEM, ANY, HBM], (VMEM, HBM)
        out_shape.append(jax.ShapeDtypeStruct((CLASSES, LANES, LANES), BF16))
        scratch += [
            pltpu.VMEM(native.shape, BF16),
            pltpu.VMEM((2, CHUNK * NODE_PITCH, LANES), F32),
            pltpu.VMEM((CLASSES * STAGE_PITCH, LANES), F32),
            pltpu.VMEM((2, CLASSES, CHUNK, LANES), BF16),
            pltpu.SemaphoreType.DMA(()),
            pltpu.SemaphoreType.DMA((2,)),
        ]
    else:
        operands = [rows, pos, selector, lists]
        in_specs, out_specs = [VMEM, ANY, VMEM, ANY], (VMEM, VMEM)
        out_shape.append(jax.ShapeDtypeStruct((elements, LANES), F32))
        scratch += [pltpu.SMEM(pos.shape, I32), pltpu.SemaphoreType.DMA(())]
    return pl.pallas_call(
        functools.partial(
            exchange_kernel, lax.axis_size("prow"), lax.axis_size("pcol"), with_classes
        ),
        out_shape=tuple(out_shape),
        in_specs=in_specs,
        out_specs=out_specs,
        scratch_shapes=scratch,
        compiler_params=pltpu.CompilerParams(
            collective_id=2 if with_classes else 0, has_side_effects=True,
            vmem_limit_bytes=(44 if with_classes else 8) * MIB,
        ),
        cost_estimate=cost(14),
        name="exchange_first" if with_classes else "exchange",
    )(*operands)


def turn_choices():
    _, turn_rows = trace_tables()
    choices = []
    for j in range(10):
        sources = {}
        for option in range(6):
            sources.setdefault(turn_rows[option][j], []).append(option)
        choices.append([(source, tuple(options)) for source, options in sources.items()])
    return choices


def turn_faces(node_ref, first, stride, orient):
    masks = {}

    def mask(options):
        if options not in masks:
            value = orient == options[0]
            for option in options[1:]:
                value = jnp.logical_or(value, orient == option)
            masks[options] = value
        return masks[options]

    choices = turn_choices()
    for c in range(6):
        at = [pl.ds(first + c * 10 + j, 8, stride=stride) for j in range(10)]
        nodes = [node_ref[at[j], :] for j in range(10)]
        for j in range(10):
            (source, _), *others = choices[j]
            value = nodes[source]
            for source, options in others:
                value = jnp.where(mask(options), nodes[source], value)
            if others:
                node_ref[at[j], :] = value


def face_flux(electric, magnetic, normal, scale):
    along_e = normal[0] * electric[0] + normal[1] * electric[1] + normal[2] * electric[2]
    along_h = normal[0] * magnetic[0] + normal[1] * magnetic[1] + normal[2] * magnetic[2]
    flux = []
    for c in range(3):
        a, b = (c + 1) % 3, (c + 2) % 3
        cross = normal[a] * magnetic[b] - normal[b] * magnetic[a]
        flux.append(scale * (electric[c] - normal[c] * along_e - cross))
    for c in range(3):
        a, b = (c + 1) % 3, (c + 2) % 3
        cross = normal[a] * electric[b] - normal[b] * electric[a]
        flux.append(scale * (magnetic[c] - normal[c] * along_h + cross))
    return flux


def image_kernel(
    count_ref, index_any, pos_any, tile_any,
    table_ref, lift_hi_ref, lift_lo_ref,
    link_ref, orient_ref, normal_ref, quotient_ref, class_hbm,
    solved_ref,
    index_ref, pos_ref, tile_ref, smem_sems, class_ref, class_sem,
    picked_ref, node_ref, flux_ref, coupled_ref, sorted_ref,
):
    index_copy = pltpu.make_async_copy(index_any, index_ref, smem_sems.at[0])
    pos_copy = pltpu.make_async_copy(pos_any, pos_ref, smem_sems.at[1])
    tile_copy = pltpu.make_async_copy(tile_any, tile_ref, smem_sems.at[2])
    class_copy = pltpu.make_async_copy(class_hbm, class_ref, class_sem)
    for copy in (index_copy, pos_copy, tile_copy, class_copy):
        copy.start()
    elements = coupled_ref.shape[0]
    blocks = elements // LANES
    chunks = blocks // 8

    index_copy.wait()
    left = lax.broadcasted_iota(I32, (1, LANES), 1) < HALF

    def gather(index):
        base = pl.multiple_of(index * LANES, LANES)
        for step in range(LANES):
            row_a = table_ref[pl.ds(index_ref[base + step], 1), :]
            row_b = table_ref[pl.ds(index_ref[2 * elements + base + step], 1), :]
            picked_ref[pl.ds(base + step, 1), :] = jnp.where(left, row_a, row_b)

    def transpose(index):
        rows = pl.ds(pl.multiple_of(index * LANES, LANES), LANES)
        target = pl.multiple_of(index * NODE_PITCH, 8)
        node_ref[pl.ds(target, LANES), :] = picked_ref[rows, :].T

    staggered(2 * blocks, gather, transpose)

    for block in range(blocks):
        for side in range(4):
            last = block * FLUX_PITCH + (side + 1) * HALF
            flux_ref[last - 8 : last, :] = jnp.zeros((8, LANES), F32)

    count = count_ref[0]
    lane = (
        lax.broadcasted_iota(I32, (8, LANES), 0) * LANES + lax.broadcasted_iota(I32, (8, LANES), 1)
    )

    def chunk(index, carry):
        side, part = index // chunks, index % chunks
        pair, half = side % 2, side // 2
        faces = pl.ds(pl.multiple_of(side * blocks + part * 8, 8), 8)
        first = (pair * blocks + part * 8) * NODE_PITCH + half * HALF
        turn_faces(node_ref, first, NODE_PITCH, orient_ref[faces, :])
        alive = ((lane + part * (8 * LANES)) < count).astype(F32)
        scale = 0.5 * quotient_ref[faces, :] * alive
        sign = jnp.where(link_ref[faces, :] < 0, -1.0, 1.0)
        normal = [normal_ref[c, faces, :] for c in range(3)]
        target = part * (8 * FLUX_PITCH) + side * HALF
        for j in range(10):
            nodes = [node_ref[pl.ds(first + c * 10 + j, 8, stride=NODE_PITCH), :] for c in range(6)]
            electric = [value * sign for value in nodes[:3]]
            flux = face_flux(electric, nodes[3:], normal, scale)
            for c in range(6):
                flux_ref[pl.ds(target + c * 10 + j, 8, stride=FLUX_PITCH), :] = flux[c]
        return carry

    lax.fori_loop(0, 4 * chunks, chunk, 0)

    def lift(index, carry):
        rows = 4 * HALF
        first = pl.multiple_of(index * (2 * FLUX_PITCH), 8)
        second = pl.multiple_of(first + FLUX_PITCH, 8)
        value = jnp.concatenate(
            [flux_ref[pl.ds(first, rows), :], flux_ref[pl.ds(second, rows), :]], axis=1
        )
        high, low = split(value)
        coupled = dot(lift_hi_ref[...], high) + dot(lift_hi_ref[...], low) + dot(lift_lo_ref[...], high)
        base = pl.multiple_of(index * (2 * LANES), 2 * LANES)
        coupled_ref[pl.ds(base, 2 * LANES), :] = coupled.T
        return carry

    lax.fori_loop(0, blocks // 2, lift, 0, unroll=8)

    unroll = 64
    pos_copy.wait()
    tile_copy.wait()

    def place(index, carry):
        base = pl.multiple_of(index * unroll, unroll)
        for step in range(unroll):
            sorted_ref[pl.ds(pos_ref[base + step], 1), :] = coupled_ref[pl.ds(base + step, 1), :]
        return carry

    lax.fori_loop(0, elements // unroll, place, 0)
    class_copy.wait()

    def solve(index, carry):
        for step in range(0, GROUP, 2):
            tile = index * GROUP + step
            base = pl.multiple_of(tile * TILE, 2 * TILE)
            high, low = split(sorted_ref[pl.ds(base, 2 * TILE), :])
            pair = jnp.concatenate(
                [class_ref[tile_ref[tile]], class_ref[tile_ref[tile + 1]]], axis=1
            )
            result = dot(jnp.concatenate([high, low], axis=0), pair)
            result = result[: 2 * TILE] + result[2 * TILE :]
            solved_ref[pl.ds(base, TILE), :] = result[:TILE, :LANES]
            solved_ref[pl.ds(base + TILE, TILE), :] = result[TILE:, LANES:]
        return carry

    lax.fori_loop(0, (tile_ref[4 * LANES] + (GROUP - 1)) // GROUP, solve, 0)


def image(part_count, indices, pos, tiles, table, lift_hi, lift_lo,
          link, orient, normal, quotient, classes):
    elements = pos.shape[0]
    slots = TILE_ROWS * TILE
    return pl.pallas_call(
        image_kernel,
        out_shape=jax.ShapeDtypeStruct((slots, LANES), F32),
        in_specs=[SMEM] + [ANY] * 3 + [VMEM] * 7 + [HBM],
        out_specs=VMEM,
        scratch_shapes=[
            pltpu.SMEM(indices.shape, I32),
            pltpu.SMEM(pos.shape, I32),
            pltpu.SMEM(tiles.shape, I32),
            pltpu.SemaphoreType.DMA((3,)),
            pltpu.VMEM(classes.shape, BF16),
            pltpu.SemaphoreType.DMA(()),
            pltpu.VMEM((2 * elements, LANES), F32),
            pltpu.VMEM((2 * elements // LANES * NODE_PITCH, LANES), F32),
            pltpu.VMEM((elements // LANES * FLUX_PITCH, LANES), F32),
            pltpu.VMEM((elements, LANES), F32),
            pltpu.VMEM((slots, LANES), F32),
        ],
        compiler_params=pltpu.CompilerParams(vmem_limit_bytes=44 * MIB),
        cost_estimate=cost(20),
        name="image",
    )(
        part_count, indices, pos, tiles, table, lift_hi, lift_lo,
        link.reshape(-1, LANES), orient.reshape(-1, LANES), normal,
        quotient.reshape(-1, LANES), classes,
    )


def gram_partials(first_ref, second_ref, third_ref, second_out, third_out, gram_ref):
    elements = first_ref.shape[0]

    def block(index, sums):
        rows = pl.ds(pl.multiple_of(index * LANES, LANES), LANES)
        f, t, u = first_ref[rows, :], second_ref[rows, :], third_ref[rows, :]
        second_out[:, rows] = t.T[:UNK]
        third_out[:, rows] = u.T[:UNK]
        pairs = (f * f, f * t, t * t, f * u, t * u, u * u)
        return tuple(
            total + jnp.sum(pair.reshape(LANES // 8, 8, LANES), axis=0)
            for total, pair in zip(sums, pairs)
        )

    zero = jnp.zeros((8, LANES), F32)
    sums = lax.fori_loop(0, elements // LANES, block, (zero,) * 6)
    lane = lax.broadcasted_iota(I32, (1, LANES), 1)
    row = jnp.zeros((1, LANES), F32)
    for index in range(6):
        value = jnp.sum(jnp.sum(sums[index], axis=0, keepdims=True), axis=1, keepdims=True)
        row = jnp.where(lane == index, value, row)
    gram_ref[...] = row


def total_kernel(grid_rows, grid_columns, first_ref, second_ref, solved_ref, pos_any,
                 total_ref, second_out, third_out, third_ref, pos_ref, pos_sem, part_ref, over_rows, over_columns, send_row, recv_row, send_column, recv_column):
    row, column = lax.axis_index("prow"), lax.axis_index("pcol")
    pos_copy = pltpu.make_async_copy(pos_any, pos_ref, pos_sem)
    pos_copy.start()

    def row_partner(step):
        return lax.rem(row + step, grid_rows)

    def column_partner(step):
        return lax.rem(column + step, grid_columns)

    barrier = pltpu.get_barrier_semaphore()
    for step in range(1, grid_rows):
        pl.semaphore_signal(
            barrier, inc=1, device_id=(row_partner(step), column), device_id_type=MESH
        )
    for step in range(1, grid_columns):
        pl.semaphore_signal(
            barrier, inc=1, device_id=(row, column_partner(step)), device_id_type=MESH
        )
    pos_copy.wait()
    element_order(solved_ref, pos_ref, third_ref)
    gram_partials(first_ref, second_ref, third_ref, second_out, third_out, part_ref)
    pl.semaphore_wait(barrier, grid_rows + grid_columns - 2)

    def row_copy(step):
        return pltpu.make_async_remote_copy(
            src_ref=part_ref,
            dst_ref=over_rows.at[step],
            send_sem=send_row,
            recv_sem=recv_row,
            device_id=(row_partner(step), column),
            device_id_type=MESH,
        )

    def wait_all(buffer, count, sem):
        landed = buffer.at[pl.ds(1, count)]
        pltpu.make_async_copy(landed, landed, sem).wait()

    for step in range(1, grid_rows):
        row_copy(step).start()
    over_rows[0] = part_ref[...]
    wait_all(over_rows, grid_rows - 1, recv_row)
    total = over_rows[row]
    for source in range(1, grid_rows):
        total = total + over_rows[lax.rem(row - source + grid_rows, grid_rows)]
    over_columns[0] = total

    def column_copy(step):
        return pltpu.make_async_remote_copy(
            src_ref=over_columns.at[0],
            dst_ref=over_columns.at[step],
            send_sem=send_column,
            recv_sem=recv_column,
            device_id=(row, column_partner(step)),
            device_id_type=MESH,
        )

    for step in range(1, grid_columns):
        column_copy(step).start()
    wait_all(over_columns, grid_columns - 1, recv_column)
    total = over_columns[column]
    for source in range(1, grid_columns):
        total = total + over_columns[lax.rem(column - source + grid_columns, grid_columns)]
    total_ref[...] = total
    wait_all(over_rows, grid_rows - 1, send_row)
    wait_all(over_columns, grid_columns - 1, send_column)


def total_over_devices(first, second, solved, pos):
    grid_rows, grid_columns = lax.axis_size("prow"), lax.axis_size("pcol")
    part = (1, LANES)
    return pl.pallas_call(
        functools.partial(total_kernel, grid_rows, grid_columns),
        out_shape=(
            jax.ShapeDtypeStruct(part, F32),
            jax.ShapeDtypeStruct((UNK, first.shape[0]), F32),
            jax.ShapeDtypeStruct((UNK, first.shape[0]), F32),
        ),
        in_specs=[VMEM] * 3 + [ANY],
        out_specs=(VMEM,) * 3,
        scratch_shapes=[
            pltpu.VMEM(first.shape, F32),
            pltpu.SMEM(pos.shape, I32),
            pltpu.SemaphoreType.DMA(()),
            pltpu.VMEM(part, F32),
            pltpu.VMEM((grid_rows,) + part, F32),
            pltpu.VMEM((grid_columns,) + part, F32),
            pltpu.SemaphoreType.DMA(()),
            pltpu.SemaphoreType.DMA(()),
            pltpu.SemaphoreType.DMA(()),
            pltpu.SemaphoreType.DMA(()),
        ],
        compiler_params=pltpu.CompilerParams(
            collective_id=1, has_side_effects=True, vmem_limit_bytes=8 * MIB
        ),
        cost_estimate=cost(12),
        name="total",
    )(first, second, solved, pos)


def finish_kernel(
    weight, count_ref, total_ref, field_ref, second_ref, third_ref, basis_hbm, hess_ref,
    basis_ref, sems,
):
    width = field_ref.shape[1]
    gram = total_ref[...] * weight
    ff, ft, tt, fu, tu, uu = (gram[:, index : index + 1] for index in range(6))
    beta = jnp.sqrt(ff + EPSILON)
    square = beta * beta
    h00 = (ff + ft) / square
    p = (EPSILON - ft) / square
    h10 = jnp.sqrt((tt + 2 * p * ft + p * p * ff) / square + EPSILON)
    k1 = 1.0 / (beta * h10)
    h01 = k1 / beta * (fu + (1 + p) * ft + p * ff)
    h11 = k1 * k1 * (tu + (1 + p) * tt + p * ft + p * fu + p * (1 + p) * ft + p * p * ff)
    q = 1 + p - h11
    w = p * (1 - h11) - h01 * h10
    h21 = jnp.sqrt(
        k1 * k1 * (uu + 2 * q * tu + 2 * w * fu + q * q * tt + 2 * q * w * ft + w * w * ff)
        + EPSILON
    )
    k2 = k1 / h21

    alive = live_lanes(count_ref[0], 0, width)
    copies = []
    for first in range(0, UNK, SLAB):
        rows = pl.ds(first, SLAB)
        f = field_ref[rows, :] * alive
        t, u = second_ref[rows, :], third_ref[rows, :]
        basis_ref[0, rows, :] = f * (1.0 / beta)
        basis_ref[1, rows, :] = t * k1 + f * (p * k1)
        basis_ref[2, rows, :] = u * k2 + t * (q * k2) + f * (w * k2)
        at = (slice(None), rows, slice(None))
        copies.append(
            pltpu.make_async_copy(basis_ref.at[at], basis_hbm.at[at], sems.at[first // SLAB])
        )
        copies[-1].start()

    at_row = lax.broadcasted_iota(I32, (2, 3), 1)
    at_column = lax.broadcasted_iota(I32, (2, 3), 0)
    hess = jnp.zeros((2, 3), F32)
    for i, j, value in ((0, 0, h00), (1, 0, h10), (0, 1, h01), (1, 1, h11), (2, 1, h21)):
        hess = jnp.where(jnp.logical_and(at_row == i, at_column == j), value, hess)
    hess_ref[...] = hess
    for copy in copies:
        copy.wait()


def finish(weight, part_count, total, right_side, second, third):
    elements = right_side.shape[1]
    return pl.pallas_call(
        functools.partial(finish_kernel, weight),
        out_shape=(
            jax.ShapeDtypeStruct((3, UNK, elements), F32),
            jax.ShapeDtypeStruct((2, 3), F32),
        ),
        in_specs=[SMEM] + [VMEM] * 4,
        out_specs=(HBM, VMEM),
        scratch_shapes=[
            pltpu.VMEM((3, UNK, elements), F32),
            pltpu.SemaphoreType.DMA((UNK // SLAB,)),
        ],
        compiler_params=pltpu.CompilerParams(vmem_limit_bytes=12 * MIB),
        name="finish",
    )(part_count, total, right_side, second, third)


def shards(
    right_side,
    part_count,
    elem_class,
    face_link,
    face_orient,
    face_normal,
    boundary_metric_quotient,
    bound_face,
    lift,
    inverse_table,
):
    unknowns, elements = right_side.shape
    all_subdomains = lax.axis_size("prow") * lax.axis_size("pcol")
    weight = 1.0 / (unknowns * elements * all_subdomains)
    native = jnp.transpose(inverse_table, (1, 2, 0))
    first, lists, selector = first_rows(part_count, right_side, bound_face[0])
    lists = lists.reshape(-1)
    first_table, classes = exchange(first, selector, lists, native)
    pos, tiles, indices, lift_hi, lift_lo, normal = prepare(
        first_table, elem_class, lift, face_link, face_normal, lists.shape[0]
    )
    pos, tiles, indices = pos.reshape(-1), tiles.reshape(-1), indices.reshape(-1)

    def operator_image(table):
        return image(
            part_count, indices, pos, tiles, table, lift_hi, lift_lo, face_link, face_orient,
            normal, boundary_metric_quotient, classes,
        )

    solved = operator_image(first_table)
    second_table, second = exchange(solved, selector, lists, pos=pos)
    solved = operator_image(second_table)
    total, second_columns, third_columns = total_over_devices(first, second, solved, pos)
    basis, hess = finish(weight, part_count, total, right_side, second_columns, third_columns)
    return (basis, hess.T)


def solution(mesh):
    in_specs = (
        P(None, ("prow", "pcol")),
        P(("prow", "pcol")),
        P(("prow", "pcol")),
        P(("prow", "pcol")),
        P(("prow", "pcol")),
        P(None, ("prow", "pcol")),
        P(("prow", "pcol")),
        P(("prow", "pcol"), None, None),
        P(),
        P(),
    )
    out_specs = (P(None, None, ("prow", "pcol")), P())
    return jax.shard_map(shards, mesh=mesh, in_specs=in_specs, out_specs=out_specs, check_vma=False)
```

```python
import functools

import jax
import jax.numpy as jnp
import numpy as np
from jax import lax
from jax.experimental import pallas as pl
from jax.experimental.pallas import tpu as pltpu
from jax.sharding import PartitionSpec as P

EPSILON = 1e-06
PERMUTATIONS = ((0, 1, 2), (0, 2, 1), (1, 0, 2), (1, 2, 0), (2, 0, 1), (2, 1, 0))
OFFSETS = tuple(((direction // 3 - 1, direction % 3 - 1) for direction in (0, 1, 2, 3, 5, 6, 7, 8)))
MESH = pl.DeviceIdType.MESH
F32, BF16, I32 = jnp.float32, jnp.bfloat16, jnp.int32
MIB = 1024 * 1024
UNK, CLASSES, LANES = 120, 256, 128
TILE = 16
HALF = 64
GROUP = 32
TILE_ROWS = 12 * GROUP
NODE_PITCH = 136
FLUX_PITCH = 264
STAGE_PITCH = 24
SLAB = 24
CHUNK = 16


def trace_tables():
    element_points = [
        (coord_a, coord_b, coord_c, 3 - coord_a - coord_b - coord_c)
        for coord_a in range(4)
        for coord_b in range(4 - coord_a)
        for coord_c in range(4 - coord_a - coord_b)
    ]
    face_points = [
        (coord_a, coord_b, 3 - coord_a - coord_b)
        for coord_a in range(4)
        for coord_b in range(4 - coord_a)
    ]
    select_rows = []
    for opposite in range(4):
        corners = [vertex for vertex in range(4) if vertex != opposite]
        members = []
        for triple in face_points:
            coords = [0, 0, 0, 0]
            for position in range(3):
                coords[corners[position]] = triple[position]
            members.append(element_points.index(tuple(coords)))
        select_rows.append(members)
    turn_rows = [
        [
            face_points.index((triple[sigma_row[0]], triple[sigma_row[1]], triple[sigma_row[2]]))
            for triple in face_points
        ]
        for sigma_row in PERMUTATIONS
    ]
    return select_rows, turn_rows


def trace_selector():
    select_rows, _ = trace_tables()
    column = lax.broadcasted_iota(I32, (1, 4 * HALF), 1)
    source = jnp.full((1, 4 * HALF), -1, I32)
    for side in range(4):
        for j in range(10):
            for c in range(6):
                here = column == side * HALF + c * 10 + j
                source = jnp.where(here, c * 20 + select_rows[side][j], source)
    row = lax.broadcasted_iota(I32, (2 * LANES, 4 * HALF), 0)
    row = jnp.where(row >= LANES, row - LANES, row)
    return (row == source).astype(F32).astype(BF16)


def split(value):
    high = value.astype(BF16)
    return high, (value - high.astype(F32)).astype(BF16)


def dot(a, b, dims=(((1,), (0,)), ((), ()))):
    return lax.dot_general(a, b, dims, preferred_element_type=F32)


VMEM = pl.BlockSpec(memory_space=pltpu.VMEM)
SMEM = pl.BlockSpec(memory_space=pltpu.SMEM)
ANY = pl.BlockSpec(memory_space=pl.ANY)
HBM = pl.BlockSpec(memory_space=pltpu.HBM)


def cost(microseconds):
    return pl.CostEstimate(
        flops=0, transcendentals=0, bytes_accessed=int(microseconds * 3_000_000)
    )


def live_lanes(count, first, width):
    return ((lax.broadcasted_iota(I32, (1, width), 1) + first) < count).astype(F32)


def rows_kernel(remote, count_ref, field_ref, list_ref, rows_ref, slot_ref, selector_ref):
    blocks = field_ref.shape[1] // LANES
    count = count_ref[0]
    for block in range(blocks):
        lanes = slice(block * LANES, (block + 1) * LANES)
        value = field_ref[:, lanes] * live_lanes(count, block * LANES, LANES)
        value = jnp.concatenate([value, jnp.zeros((LANES - UNK, LANES), F32)], axis=0)
        rows_ref[lanes, :] = value.T
    per_list = list_ref.shape[1] // LANES
    for index in range(8):
        for part in range(per_list):
            row = index * per_list + part
            face = list_ref[index : index + 1, part * LANES : (part + 1) * LANES]
            slot_ref[row : row + 1, :] = jnp.maximum(face, 0) + remote
    selector_ref[...] = trace_selector()


def first_rows(part_count, right_side, lists):
    remote = lists.shape[0] * lists.shape[1]
    return pl.pallas_call(
        functools.partial(rows_kernel, remote),
        out_shape=(
            jax.ShapeDtypeStruct((right_side.shape[1], LANES), F32),
            jax.ShapeDtypeStruct((remote // LANES, LANES), I32),
            jax.ShapeDtypeStruct((2 * LANES, 4 * HALF), BF16),
        ),
        in_specs=[SMEM, VMEM, VMEM],
        out_specs=(VMEM,) * 3,
        compiler_params=pltpu.CompilerParams(vmem_limit_bytes=4 * MIB),
        cost_estimate=cost(2),
        name="first_rows",
    )(part_count, right_side, lists)


def prep_kernel(
    remote, _, class_ref, lift_ref, link_ref, normal_ref,
    pos_ref, tile_ref, index_ref, lift_hi_ref, lift_lo_ref, plane_ref, spread_ref,
):
    blocks = class_ref.shape[0]

    class_row = lax.broadcasted_iota(I32, (CLASSES, LANES), 0)
    totals = jnp.zeros((CLASSES, LANES), F32)
    for block in range(blocks):
        totals = totals + (class_ref[block : block + 1, :] == class_row).astype(F32)
    total = jnp.sum(totals, axis=1, keepdims=True)
    tiles = jnp.floor((total + (TILE - 1)) * (1.0 / TILE))
    tiles = jnp.broadcast_to(tiles, (CLASSES, LANES))
    lower = (
        lax.broadcasted_iota(I32, (CLASSES, CLASSES), 1)
        < lax.broadcasted_iota(I32, (CLASSES, CLASSES), 0)
    ).astype(BF16)
    start = dot(lower, tiles.astype(BF16))
    end = start + tiles
    earlier = (
        lax.broadcasted_iota(I32, (LANES, 2 * LANES), 0)
        < lax.broadcasted_iota(I32, (LANES, 2 * LANES), 1)
    ).astype(BF16)
    carry = start * TILE
    for block in range(blocks):
        member = (class_ref[block : block + 1, :] == class_row).astype(F32)
        ranks = dot(member.astype(BF16), earlier)
        position = jnp.sum(member * (ranks[:, :LANES] + carry), axis=0, keepdims=True)
        pos_ref[block : block + 1, :] = position.astype(I32)
        carry = carry + ranks[:, LANES:]
    tile_ref[...] = jnp.zeros((8, LANES), I32)
    for row in range(4):
        tile = (lax.broadcasted_iota(I32, (CLASSES, LANES), 1) + row * LANES).astype(F32)
        owner = jnp.sum((end <= tile).astype(F32), axis=0, keepdims=True)
        tile_ref[row : row + 1, :] = jnp.minimum(owner.astype(I32), CLASSES - 1)
    tile_ref[4:5, :] = end[CLASSES - 1 :, :].astype(I32)

    spread_ref[...] = jnp.zeros(spread_ref.shape, F32)
    for side in range(4):
        block = lift_ref[:, side, :]
        for c in range(6):
            first = side * HALF + c * 10
            spread_ref[first : first + 10, c * 20 : (c + 1) * 20] = block
    high, low = split(spread_ref[...].T)
    lift_hi_ref[...] = high
    lift_lo_ref[...] = low

    link = link_ref[...]
    own = (
        lax.broadcasted_iota(I32, link.shape, 0) * LANES
        + lax.broadcasted_iota(I32, link.shape, 1)
        + remote
    )
    index_ref[...] = jnp.where(link < 0, own, link)

    for c in range(3):
        for row in range(link.shape[0]):
            plane_ref[c, row : row + 1, :] = normal_ref[c : c + 1, row * LANES : (row + 1) * LANES]


def prepare(after, elem_class, lift, link, normal, remote):
    elements, faces = elem_class.shape[0], link.shape[0]
    return pl.pallas_call(
        functools.partial(prep_kernel, remote),
        out_shape=(
            jax.ShapeDtypeStruct((elements // LANES, LANES), I32),
            jax.ShapeDtypeStruct((8, LANES), I32),
            jax.ShapeDtypeStruct((faces // LANES, LANES), I32),
            jax.ShapeDtypeStruct((LANES, 4 * HALF), BF16),
            jax.ShapeDtypeStruct((LANES, 4 * HALF), BF16),
            jax.ShapeDtypeStruct((3, faces // LANES, LANES), F32),
        ),
        in_specs=[ANY] + [VMEM] * 4,
        out_specs=(VMEM,) * 6,
        scratch_shapes=[pltpu.VMEM((4 * HALF, LANES), F32)],
        compiler_params=pltpu.CompilerParams(vmem_limit_bytes=4 * MIB),
        cost_estimate=cost(3),
        name="prepare",
    )(
        after, elem_class.reshape(elements // LANES, LANES), jnp.transpose(lift, (2, 0, 1)),
        link.reshape(faces // LANES, LANES), normal,
    )


def trace_block(rows_ref, selector_ref, table_ref, first, index):
    elements = rows_ref.shape[0]
    width = 2 * LANES
    left = lax.broadcasted_iota(I32, (width, LANES), 1) < HALF
    base = pl.multiple_of(index * width, width)
    high, low = split(rows_ref[pl.ds(base, width), :])
    traces = dot(jnp.concatenate([high, low], axis=1), selector_ref[...])
    for pair in range(2):
        both = traces[:, pair * LANES : (pair + 1) * LANES]
        swapped = pltpu.roll(both, HALF, 1)
        even, odd = first + 2 * pair * elements, first + (2 * pair + 1) * elements
        table_ref[pl.ds(even + base, width), :] = jnp.where(left, both, swapped)
        table_ref[pl.ds(odd + base, width), :] = jnp.where(left, swapped, both)


def write_traces(rows_ref, selector_ref, table_ref, first):
    def block(index, carry):
        trace_block(rows_ref, selector_ref, table_ref, first, index)
        return carry

    lax.fori_loop(0, rows_ref.shape[0] // (2 * LANES), block, 0, unroll=4)


def staggered(count, before, after):
    before(0)

    def body(index, carry):
        after(index - 1)
        before(index)
        return carry

    lax.fori_loop(1, count, body, 0)
    after(count - 1)


def gather_pairs(table_ref, index_ref, out_ref, first_a, first_b, offset, count, unroll):
    left = lax.broadcasted_iota(I32, (1, LANES), 1) < HALF

    def block(index, carry):
        base = pl.multiple_of(index * unroll, unroll)
        for step in range(unroll):
            row_a = table_ref[pl.ds(index_ref[first_a + base + step] + offset, 1), :]
            row_b = table_ref[pl.ds(index_ref[first_b + base + step] + offset, 1), :]
            out_ref[pl.ds(base + step, 1), :] = jnp.where(left, row_a, row_b)
        return carry

    lax.fori_loop(0, count // unroll, block, 0)


def element_order(solved_ref, pos_ref, rows_ref):
    unroll = 256

    def fetch(index, carry):
        base = pl.multiple_of(index * unroll, unroll)
        for step in range(unroll):
            rows_ref[pl.ds(base + step, 1), :] = solved_ref[pl.ds(pos_ref[base + step], 1), :]
        return carry

    lax.fori_loop(0, rows_ref.shape[0] // unroll, fetch, 0)


def class_major(native_ref, turned_ref, stage_ref, part_ref, class_hbm, sems):
    for half in range(2):
        for row in range(CHUNK):
            last = row * NODE_PITCH + UNK
            turned_ref[half, last : last + LANES - UNK, :] = jnp.zeros((LANES - UNK, LANES), F32)

    def store(first):
        slot = first // CHUNK % 2
        target = class_hbm.at[:, pl.ds(first, CHUNK), :]
        return pltpu.make_async_copy(part_ref.at[slot], target, sems.at[slot])

    for first in range(0, LANES, CHUNK):
        count = min(CHUNK, UNK - first)

        def collect(index, carry):
            value = native_ref[index, first : first + count, :].astype(F32)
            if count < CHUNK:
                value = jnp.concatenate([value, jnp.zeros((CHUNK - count, CLASSES), F32)], axis=0)
            for half in range(2):
                turned_ref[half, pl.ds(index, CHUNK, stride=NODE_PITCH), :] = value[
                    :, half * LANES : (half + 1) * LANES
                ]
            return carry

        lax.fori_loop(0, UNK, collect, 0, unroll=24)

        for row in range(CHUNK):
            for half in range(2):
                target = pl.ds(half * LANES * STAGE_PITCH + row, LANES, stride=STAGE_PITCH)
                rows = slice(row * NODE_PITCH, row * NODE_PITCH + LANES)
                stage_ref[target, :] = turned_ref[half, rows, :].T
        stage = stage_ref[...].reshape(CLASSES, STAGE_PITCH, LANES)[:, :CHUNK]
        if first >= 2 * CHUNK:
            store(first - 2 * CHUNK).wait()
        part_ref[first // CHUNK % 2] = stage.astype(BF16)
        store(first).start()
    return [store(LANES - 2 * CHUNK), store(LANES - CHUNK)]


def exchange_kernel(grid_rows, grid_columns, with_classes, *refs):
    if with_classes:
        (rows_ref, selector_ref, list_any, native_hbm, table_ref, class_hbm,
         list_ref, outgoing_ref, received_ref, local_sem, send_sem, recv_sem,
         native_ref, turned_ref, stage_ref, part_ref, native_sem, part_sems) = refs
        native_copy = pltpu.make_async_copy(native_hbm, native_ref, native_sem)
        native_copy.start()
    else:
        (solved_ref, pos_any, selector_ref, list_any, table_ref, rows_ref,
         list_ref, outgoing_ref, received_ref, local_sem, send_sem, recv_sem,
         pos_ref, pos_sem) = refs
        pos_copy = pltpu.make_async_copy(pos_any, pos_ref, pos_sem)
        pos_copy.start()
    list_copy = pltpu.make_async_copy(list_any, list_ref, local_sem)
    list_copy.start()
    slots = outgoing_ref.shape[1]
    row, column = lax.axis_index("prow"), lax.axis_index("pcol")

    def present(index):
        a, b = OFFSETS[index]
        inside = None
        for at, step, size in ((row, a, grid_rows), (column, b, grid_columns)):
            if step == 0:
                continue
            term = at > 0 if step < 0 else at < size - 1
            inside = term if inside is None else jnp.logical_and(inside, term)
        return inside

    def partner(index):
        a, b = OFFSETS[index]
        return (row + a, column + b)

    def transfer(index):
        return pltpu.make_async_remote_copy(
            src_ref=outgoing_ref.at[index],
            dst_ref=received_ref.at[7 - index],
            send_sem=send_sem.at[index],
            recv_sem=recv_sem.at[7 - index],
            device_id=partner(index),
            device_id_type=MESH,
        )

    barrier = pltpu.get_barrier_semaphore()
    for index in range(8):
        @pl.when(present(index))
        def _(index=index):
            pl.semaphore_signal(barrier, inc=1, device_id=partner(index), device_id_type=MESH)

    if not with_classes:
        pos_copy.wait()
        element_order(solved_ref, pos_ref, rows_ref)
    write_traces(rows_ref, selector_ref, table_ref, 16 * slots)
    list_copy.wait()

    def gather(index):
        first = index * 2 * slots
        gather_pairs(
            table_ref, list_ref, outgoing_ref.at[index], first, first + slots, 0, slots, 32
        )

    early, late = ((0, 2, 5, 7), (3, 4, 1, 6)) if with_classes else ((0,), (2, 5, 7, 3, 4, 1, 6))
    for index in early:
        gather(index)

    near_rows = 1 + (row > 0).astype(I32) + (row < grid_rows - 1).astype(I32)
    near_columns = 1 + (column > 0).astype(I32) + (column < grid_columns - 1).astype(I32)
    pl.semaphore_wait(barrier, near_rows * near_columns - 1)

    for index in early + late:
        if index in late:
            gather(index)

        @pl.when(present(index))
        def _(index=index):
            transfer(index).start()

    if with_classes:
        native_copy.wait()
        stores = class_major(native_ref, turned_ref, stage_ref, part_ref, class_hbm, part_sems)

    left = lax.broadcasted_iota(I32, (slots, LANES), 1) < HALF
    for index in (1, 6, 3, 4, 0, 2, 5, 7):
        @pl.when(present(index))
        def _(index=index):
            transfer(7 - index).wait_recv()
            packed = received_ref[index]
            swapped = pltpu.roll(packed, HALF, 1)
            first = index * 2 * slots
            table_ref[first : first + slots, :] = jnp.where(left, packed, swapped)
            table_ref[first + slots : first + 2 * slots, :] = jnp.where(left, swapped, packed)

    for index in range(8):
        @pl.when(present(index))
        def _(index=index):
            transfer(index).wait_send()

    if with_classes:
        for store in stores:
            store.wait()


def exchange(rows, selector, lists, native=None, pos=None):
    slots = lists.shape[0] // 16
    with_classes = native is not None
    elements = rows.shape[0] if with_classes else pos.shape[0]
    out_shape = [jax.ShapeDtypeStruct((16 * slots + 4 * elements, LANES), F32)]
    scratch = [
        pltpu.SMEM(lists.shape, I32),
        pltpu.VMEM((8, slots, LANES), F32),
        pltpu.VMEM((8, slots, LANES), F32),
        pltpu.SemaphoreType.DMA(()),
        pltpu.SemaphoreType.DMA((8,)),
        pltpu.SemaphoreType.DMA((8,)),
    ]
    if with_classes:
        operands = [rows, selector, lists, native]
        in_specs, out_specs = [VMEM, VMEM, ANY, HBM], (VMEM, HBM)
        out_shape.append(jax.ShapeDtypeStruct((CLASSES, LANES, LANES), BF16))
        scratch += [
            pltpu.VMEM(native.shape, BF16),
            pltpu.VMEM((2, CHUNK * NODE_PITCH, LANES), F32),
            pltpu.VMEM((CLASSES * STAGE_PITCH, LANES), F32),
            pltpu.VMEM((2, CLASSES, CHUNK, LANES), BF16),
            pltpu.SemaphoreType.DMA(()),
            pltpu.SemaphoreType.DMA((2,)),
        ]
    else:
        operands = [rows, pos, selector, lists]
        in_specs, out_specs = [VMEM, ANY, VMEM, ANY], (VMEM, VMEM)
        out_shape.append(jax.ShapeDtypeStruct((elements, LANES), F32))
        scratch += [pltpu.SMEM(pos.shape, I32), pltpu.SemaphoreType.DMA(())]
    return pl.pallas_call(
        functools.partial(
            exchange_kernel, lax.axis_size("prow"), lax.axis_size("pcol"), with_classes
        ),
        out_shape=tuple(out_shape),
        in_specs=in_specs,
        out_specs=out_specs,
        scratch_shapes=scratch,
        compiler_params=pltpu.CompilerParams(
            collective_id=2 if with_classes else 0, has_side_effects=True,
            vmem_limit_bytes=(44 if with_classes else 8) * MIB,
        ),
        cost_estimate=cost(14),
        name="exchange_first" if with_classes else "exchange",
    )(*operands)


def turn_choices():
    _, turn_rows = trace_tables()
    choices = []
    for j in range(10):
        sources = {}
        for option in range(6):
            sources.setdefault(turn_rows[option][j], []).append(option)
        choices.append([(source, tuple(options)) for source, options in sources.items()])
    return choices


def turn_faces(node_ref, first, stride, orient):
    masks = {}

    def mask(options):
        if options not in masks:
            value = orient == options[0]
            for option in options[1:]:
                value = jnp.logical_or(value, orient == option)
            masks[options] = value
        return masks[options]

    choices = turn_choices()
    for c in range(6):
        at = [pl.ds(first + c * 10 + j, 8, stride=stride) for j in range(10)]
        nodes = [node_ref[at[j], :] for j in range(10)]
        for j in range(10):
            (source, _), *others = choices[j]
            value = nodes[source]
            for source, options in others:
                value = jnp.where(mask(options), nodes[source], value)
            if others:
                node_ref[at[j], :] = value


def face_flux(electric, magnetic, normal, scale):
    along_e = normal[0] * electric[0] + normal[1] * electric[1] + normal[2] * electric[2]
    along_h = normal[0] * magnetic[0] + normal[1] * magnetic[1] + normal[2] * magnetic[2]
    flux = []
    for c in range(3):
        a, b = (c + 1) % 3, (c + 2) % 3
        cross = normal[a] * magnetic[b] - normal[b] * magnetic[a]
        flux.append(scale * (electric[c] - normal[c] * along_e - cross))
    for c in range(3):
        a, b = (c + 1) % 3, (c + 2) % 3
        cross = normal[a] * electric[b] - normal[b] * electric[a]
        flux.append(scale * (magnetic[c] - normal[c] * along_h + cross))
    return flux


def image_kernel(
    count_ref, index_any, pos_any, tile_any,
    table_ref, lift_hi_ref, lift_lo_ref,
    link_ref, orient_ref, normal_ref, quotient_ref, class_hbm,
    solved_ref,
    index_ref, pos_ref, tile_ref, smem_sems, class_ref, class_sem,
    picked_ref, node_ref, flux_ref, coupled_ref, sorted_ref,
):
    index_copy = pltpu.make_async_copy(index_any, index_ref, smem_sems.at[0])
    pos_copy = pltpu.make_async_copy(pos_any, pos_ref, smem_sems.at[1])
    tile_copy = pltpu.make_async_copy(tile_any, tile_ref, smem_sems.at[2])
    class_copy = pltpu.make_async_copy(class_hbm, class_ref, class_sem)
    for copy in (index_copy, pos_copy, tile_copy, class_copy):
        copy.start()
    elements = coupled_ref.shape[0]
    blocks = elements // LANES
    chunks = blocks // 8

    index_copy.wait()
    left = lax.broadcasted_iota(I32, (1, LANES), 1) < HALF

    def gather(index):
        base = pl.multiple_of(index * LANES, LANES)
        for step in range(LANES):
            row_a = table_ref[pl.ds(index_ref[base + step], 1), :]
            row_b = table_ref[pl.ds(index_ref[2 * elements + base + step], 1), :]
            picked_ref[pl.ds(base + step, 1), :] = jnp.where(left, row_a, row_b)

    def transpose(index):
        rows = pl.ds(pl.multiple_of(index * LANES, LANES), LANES)
        target = pl.multiple_of(index * NODE_PITCH, 8)
        node_ref[pl.ds(target, LANES), :] = picked_ref[rows, :].T

    staggered(2 * blocks, gather, transpose)

    for block in range(blocks):
        for side in range(4):
            last = block * FLUX_PITCH + (side + 1) * HALF
            flux_ref[last - 8 : last, :] = jnp.zeros((8, LANES), F32)

    count = count_ref[0]
    lane = (
        lax.broadcasted_iota(I32, (8, LANES), 0) * LANES + lax.broadcasted_iota(I32, (8, LANES), 1)
    )

    def chunk(index, carry):
        side, part = index // chunks, index % chunks
        pair, half = side % 2, side // 2
        faces = pl.ds(pl.multiple_of(side * blocks + part * 8, 8), 8)
        first = (pair * blocks + part * 8) * NODE_PITCH + half * HALF
        turn_faces(node_ref, first, NODE_PITCH, orient_ref[faces, :])
        alive = ((lane + part * (8 * LANES)) < count).astype(F32)
        scale = 0.5 * quotient_ref[faces, :] * alive
        sign = jnp.where(link_ref[faces, :] < 0, -1.0, 1.0)
        normal = [normal_ref[c, faces, :] for c in range(3)]
        target = part * (8 * FLUX_PITCH) + side * HALF
        for j in range(10):
            nodes = [node_ref[pl.ds(first + c * 10 + j, 8, stride=NODE_PITCH), :] for c in range(6)]
            electric = [value * sign for value in nodes[:3]]
            flux = face_flux(electric, nodes[3:], normal, scale)
            for c in range(6):
                flux_ref[pl.ds(target + c * 10 + j, 8, stride=FLUX_PITCH), :] = flux[c]
        return carry

    lax.fori_loop(0, 4 * chunks, chunk, 0)

    def lift(index, carry):
        rows = 4 * HALF
        first = pl.multiple_of(index * (2 * FLUX_PITCH), 8)
        second = pl.multiple_of(first + FLUX_PITCH, 8)
        value = jnp.concatenate(
            [flux_ref[pl.ds(first, rows), :], flux_ref[pl.ds(second, rows), :]], axis=1
        )
        high, low = split(value)
        coupled = dot(lift_hi_ref[...], high) + dot(lift_hi_ref[...], low) + dot(lift_lo_ref[...], high)
        base = pl.multiple_of(index * (2 * LANES), 2 * LANES)
        coupled_ref[pl.ds(base, 2 * LANES), :] = coupled.T
        return carry

    lax.fori_loop(0, blocks // 2, lift, 0, unroll=8)

    pos_copy.wait()
    tile_copy.wait()
    for row in range(elements):
        sorted_ref[pl.ds(pos_ref[row], 1), :] = coupled_ref[row : row + 1, :]
    class_copy.wait()

    def solve(index, carry):
        for step in range(0, GROUP, 2):
            tile = index * GROUP + step
            base = pl.multiple_of(tile * TILE, 2 * TILE)
            high, low = split(sorted_ref[pl.ds(base, 2 * TILE), :])
            pair = jnp.concatenate(
                [class_ref[tile_ref[tile]], class_ref[tile_ref[tile + 1]]], axis=1
            )
            result = dot(jnp.concatenate([high, low], axis=0), pair)
            result = result[: 2 * TILE] + result[2 * TILE :]
            solved_ref[pl.ds(base, TILE), :] = result[:TILE, :LANES]
            solved_ref[pl.ds(base + TILE, TILE), :] = result[TILE:, LANES:]
        return carry

    lax.fori_loop(0, (tile_ref[4 * LANES] + (GROUP - 1)) // GROUP, solve, 0)


def image(part_count, indices, pos, tiles, table, lift_hi, lift_lo,
          link, orient, normal, quotient, classes):
    elements = pos.shape[0]
    slots = TILE_ROWS * TILE
    return pl.pallas_call(
        image_kernel,
        out_shape=jax.ShapeDtypeStruct((slots, LANES), F32),
        in_specs=[SMEM] + [ANY] * 3 + [VMEM] * 7 + [HBM],
        out_specs=VMEM,
        scratch_shapes=[
            pltpu.SMEM(indices.shape, I32),
            pltpu.SMEM(pos.shape, I32),
            pltpu.SMEM(tiles.shape, I32),
            pltpu.SemaphoreType.DMA((3,)),
            pltpu.VMEM(classes.shape, BF16),
            pltpu.SemaphoreType.DMA(()),
            pltpu.VMEM((2 * elements, LANES), F32),
            pltpu.VMEM((2 * elements // LANES * NODE_PITCH, LANES), F32),
            pltpu.VMEM((elements // LANES * FLUX_PITCH, LANES), F32),
            pltpu.VMEM((elements, LANES), F32),
            pltpu.VMEM((slots, LANES), F32),
        ],
        compiler_params=pltpu.CompilerParams(vmem_limit_bytes=44 * MIB),
        cost_estimate=cost(20),
        name="image",
    )(
        part_count, indices, pos, tiles, table, lift_hi, lift_lo,
        link.reshape(-1, LANES), orient.reshape(-1, LANES), normal,
        quotient.reshape(-1, LANES), classes,
    )


def gram_partials(first_ref, second_ref, third_ref, second_out, third_out, gram_ref):
    elements = first_ref.shape[0]

    def block(index, sums):
        rows = pl.ds(pl.multiple_of(index * LANES, LANES), LANES)
        f, t, u = first_ref[rows, :], second_ref[rows, :], third_ref[rows, :]
        second_out[:, rows] = t.T[:UNK]
        third_out[:, rows] = u.T[:UNK]
        pairs = (f * f, f * t, t * t, f * u, t * u, u * u)
        return tuple(
            total + jnp.sum(pair.reshape(LANES // 8, 8, LANES), axis=0)
            for total, pair in zip(sums, pairs)
        )

    zero = jnp.zeros((8, LANES), F32)
    sums = lax.fori_loop(0, elements // LANES, block, (zero,) * 6)
    lane = lax.broadcasted_iota(I32, (1, LANES), 1)
    row = jnp.zeros((1, LANES), F32)
    for index in range(6):
        value = jnp.sum(jnp.sum(sums[index], axis=0, keepdims=True), axis=1, keepdims=True)
        row = jnp.where(lane == index, value, row)
    gram_ref[...] = row


def total_kernel(grid_rows, grid_columns, first_ref, second_ref, solved_ref, pos_any,
                 total_ref, second_out, third_out, third_ref, pos_ref, pos_sem, part_ref, over_rows, over_columns, send_row, recv_row, send_column, recv_column):
    row, column = lax.axis_index("prow"), lax.axis_index("pcol")
    pos_copy = pltpu.make_async_copy(pos_any, pos_ref, pos_sem)
    pos_copy.start()

    def row_partner(step):
        return lax.rem(row + step, grid_rows)

    def column_partner(step):
        return lax.rem(column + step, grid_columns)

    barrier = pltpu.get_barrier_semaphore()
    for step in range(1, grid_rows):
        pl.semaphore_signal(
            barrier, inc=1, device_id=(row_partner(step), column), device_id_type=MESH
        )
    for step in range(1, grid_columns):
        pl.semaphore_signal(
            barrier, inc=1, device_id=(row, column_partner(step)), device_id_type=MESH
        )
    pos_copy.wait()
    element_order(solved_ref, pos_ref, third_ref)
    gram_partials(first_ref, second_ref, third_ref, second_out, third_out, part_ref)
    pl.semaphore_wait(barrier, grid_rows + grid_columns - 2)

    def row_copy(step):
        return pltpu.make_async_remote_copy(
            src_ref=part_ref,
            dst_ref=over_rows.at[step],
            send_sem=send_row,
            recv_sem=recv_row,
            device_id=(row_partner(step), column),
            device_id_type=MESH,
        )

    def wait_all(buffer, count, sem):
        landed = buffer.at[pl.ds(1, count)]
        pltpu.make_async_copy(landed, landed, sem).wait()

    for step in range(1, grid_rows):
        row_copy(step).start()
    over_rows[0] = part_ref[...]
    wait_all(over_rows, grid_rows - 1, recv_row)
    total = over_rows[row]
    for source in range(1, grid_rows):
        total = total + over_rows[lax.rem(row - source + grid_rows, grid_rows)]
    over_columns[0] = total

    def column_copy(step):
        return pltpu.make_async_remote_copy(
            src_ref=over_columns.at[0],
            dst_ref=over_columns.at[step],
            send_sem=send_column,
            recv_sem=recv_column,
            device_id=(row, column_partner(step)),
            device_id_type=MESH,
        )

    for step in range(1, grid_columns):
        column_copy(step).start()
    wait_all(over_columns, grid_columns - 1, recv_column)
    total = over_columns[column]
    for source in range(1, grid_columns):
        total = total + over_columns[lax.rem(column - source + grid_columns, grid_columns)]
    total_ref[...] = total
    wait_all(over_rows, grid_rows - 1, send_row)
    wait_all(over_columns, grid_columns - 1, send_column)


def total_over_devices(first, second, solved, pos):
    grid_rows, grid_columns = lax.axis_size("prow"), lax.axis_size("pcol")
    part = (1, LANES)
    return pl.pallas_call(
        functools.partial(total_kernel, grid_rows, grid_columns),
        out_shape=(
            jax.ShapeDtypeStruct(part, F32),
            jax.ShapeDtypeStruct((UNK, first.shape[0]), F32),
            jax.ShapeDtypeStruct((UNK, first.shape[0]), F32),
        ),
        in_specs=[VMEM] * 3 + [ANY],
        out_specs=(VMEM,) * 3,
        scratch_shapes=[
            pltpu.VMEM(first.shape, F32),
            pltpu.SMEM(pos.shape, I32),
            pltpu.SemaphoreType.DMA(()),
            pltpu.VMEM(part, F32),
            pltpu.VMEM((grid_rows,) + part, F32),
            pltpu.VMEM((grid_columns,) + part, F32),
            pltpu.SemaphoreType.DMA(()),
            pltpu.SemaphoreType.DMA(()),
            pltpu.SemaphoreType.DMA(()),
            pltpu.SemaphoreType.DMA(()),
        ],
        compiler_params=pltpu.CompilerParams(
            collective_id=1, has_side_effects=True, vmem_limit_bytes=8 * MIB
        ),
        cost_estimate=cost(12),
        name="total",
    )(first, second, solved, pos)


def finish_kernel(
    weight, count_ref, total_ref, field_ref, second_ref, third_ref, basis_hbm, hess_ref,
    basis_ref, sems,
):
    width = field_ref.shape[1]
    gram = total_ref[...] * weight
    ff, ft, tt, fu, tu, uu = (gram[:, index : index + 1] for index in range(6))
    square = ff + EPSILON
    inverse = 1.0 / square
    p = (EPSILON - ft) * inverse
    h10_square = jnp.maximum(tt + 2 * p * ft + p * p * ff, 0.0) * inverse + EPSILON
    k1_square = inverse / h10_square
    h11 = k1_square * (tu + (1 + p) * tt + p * ft + p * fu + p * (1 + p) * ft + p * p * ff)
    along = (fu + (1 + p) * ft + p * ff) * inverse
    q = 1 + p - h11
    w = p * (1 - h11) - along
    rest = uu + 2 * q * tu + 2 * w * fu + q * q * tt + 2 * q * w * ft + w * w * ff
    h21_square = k1_square * jnp.maximum(rest, 0.0) + EPSILON
    k0 = 1.0 / jnp.sqrt(square)
    k1 = jnp.sqrt(k1_square)
    h10, h21 = jnp.sqrt(h10_square), jnp.sqrt(h21_square)
    h00, h01 = (ff + ft) * inverse, along / h10
    k2 = k1 / h21

    alive = live_lanes(count_ref[0], 0, width)
    copies = []
    for first in range(0, UNK, SLAB):
        rows = pl.ds(first, SLAB)
        f = field_ref[rows, :] * alive
        t, u = second_ref[rows, :], third_ref[rows, :]
        basis_ref[0, rows, :] = f * k0
        basis_ref[1, rows, :] = t * k1 + f * (p * k1)
        basis_ref[2, rows, :] = u * k2 + t * (q * k2) + f * (w * k2)
        at = (slice(None), rows, slice(None))
        copies.append(
            pltpu.make_async_copy(basis_ref.at[at], basis_hbm.at[at], sems.at[first // SLAB])
        )
        copies[-1].start()

    at_row = lax.broadcasted_iota(I32, (2, 3), 1)
    at_column = lax.broadcasted_iota(I32, (2, 3), 0)
    hess = jnp.zeros((2, 3), F32)
    for i, j, value in ((0, 0, h00), (1, 0, h10), (0, 1, h01), (1, 1, h11), (2, 1, h21)):
        hess = jnp.where(jnp.logical_and(at_row == i, at_column == j), value, hess)
    hess_ref[...] = hess
    for copy in copies:
        copy.wait()


def finish(weight, part_count, total, right_side, second, third):
    elements = right_side.shape[1]
    return pl.pallas_call(
        functools.partial(finish_kernel, weight),
        out_shape=(
            jax.ShapeDtypeStruct((3, UNK, elements), F32),
            jax.ShapeDtypeStruct((2, 3), F32),
        ),
        in_specs=[SMEM] + [VMEM] * 4,
        out_specs=(HBM, VMEM),
        scratch_shapes=[
            pltpu.VMEM((3, UNK, elements), F32),
            pltpu.SemaphoreType.DMA((UNK // SLAB,)),
        ],
        compiler_params=pltpu.CompilerParams(vmem_limit_bytes=12 * MIB),
        name="finish",
    )(part_count, total, right_side, second, third)


def shards(
    right_side,
    part_count,
    elem_class,
    face_link,
    face_orient,
    face_normal,
    boundary_metric_quotient,
    bound_face,
    lift,
    inverse_table,
):
    unknowns, elements = right_side.shape
    all_subdomains = lax.axis_size("prow") * lax.axis_size("pcol")
    weight = 1.0 / (unknowns * elements * all_subdomains)
    native = jnp.transpose(inverse_table, (1, 2, 0))
    first, lists, selector = first_rows(part_count, right_side, bound_face[0])
    lists = lists.reshape(-1)
    first_table, classes = exchange(first, selector, lists, native)
    pos, tiles, indices, lift_hi, lift_lo, normal = prepare(
        first_table, elem_class, lift, face_link, face_normal, lists.shape[0]
    )
    pos, tiles, indices = pos.reshape(-1), tiles.reshape(-1), indices.reshape(-1)

    def operator_image(table):
        return image(
            part_count, indices, pos, tiles, table, lift_hi, lift_lo, face_link, face_orient,
            normal, boundary_metric_quotient, classes,
        )

    solved = operator_image(first_table)
    second_table, second = exchange(solved, selector, lists, pos=pos)
    solved = operator_image(second_table)
    total, second_columns, third_columns = total_over_devices(first, second, solved, pos)
    basis, hess = finish(weight, part_count, total, right_side, second_columns, third_columns)
    return (basis, hess.T)


def solution(mesh):
    in_specs = (
        P(None, ("prow", "pcol")),
        P(("prow", "pcol")),
        P(("prow", "pcol")),
        P(("prow", "pcol")),
        P(("prow", "pcol")),
        P(None, ("prow", "pcol")),
        P(("prow", "pcol")),
        P(("prow", "pcol"), None, None),
        P(),
        P(),
    )
    out_specs = (P(None, None, ("prow", "pcol")), P())
    return jax.shard_map(shards, mesh=mesh, in_specs=in_specs, out_specs=out_specs, check_vma=False)
```

```python
import functools

import jax
import jax.numpy as jnp
import numpy as np
from jax import lax
from jax.experimental import pallas as pl
from jax.experimental.pallas import tpu as pltpu
from jax.sharding import PartitionSpec as P

EPSILON = 1e-06
PERMUTATIONS = ((0, 1, 2), (0, 2, 1), (1, 0, 2), (1, 2, 0), (2, 0, 1), (2, 1, 0))
OFFSETS = tuple(((direction // 3 - 1, direction % 3 - 1) for direction in (0, 1, 2, 3, 5, 6, 7, 8)))
MESH = pl.DeviceIdType.MESH
F32, BF16, I32 = jnp.float32, jnp.bfloat16, jnp.int32
MIB = 1024 * 1024
UNK, CLASSES, LANES = 120, 256, 128
TILE = 16
HALF = 64
GROUP = 32
TILE_ROWS = 12 * GROUP
NODE_PITCH = 136
FLUX_PITCH = 264
STAGE_PITCH = 24
SLAB = 24
CHUNK = 16


def trace_tables():
    element_points = [
        (coord_a, coord_b, coord_c, 3 - coord_a - coord_b - coord_c)
        for coord_a in range(4)
        for coord_b in range(4 - coord_a)
        for coord_c in range(4 - coord_a - coord_b)
    ]
    face_points = [
        (coord_a, coord_b, 3 - coord_a - coord_b)
        for coord_a in range(4)
        for coord_b in range(4 - coord_a)
    ]
    select_rows = []
    for opposite in range(4):
        corners = [vertex for vertex in range(4) if vertex != opposite]
        members = []
        for triple in face_points:
            coords = [0, 0, 0, 0]
            for position in range(3):
                coords[corners[position]] = triple[position]
            members.append(element_points.index(tuple(coords)))
        select_rows.append(members)
    turn_rows = [
        [
            face_points.index((triple[sigma_row[0]], triple[sigma_row[1]], triple[sigma_row[2]]))
            for triple in face_points
        ]
        for sigma_row in PERMUTATIONS
    ]
    return select_rows, turn_rows


def trace_selector():
    select_rows, _ = trace_tables()
    column = lax.broadcasted_iota(I32, (1, 4 * HALF), 1)
    source = jnp.full((1, 4 * HALF), -1, I32)
    for side in range(4):
        for j in range(10):
            for c in range(6):
                here = column == side * HALF + c * 10 + j
                source = jnp.where(here, c * 20 + select_rows[side][j], source)
    row = lax.broadcasted_iota(I32, (2 * LANES, 4 * HALF), 0)
    row = jnp.where(row >= LANES, row - LANES, row)
    return (row == source).astype(F32).astype(BF16)


def split(value):
    high = value.astype(BF16)
    return high, (value - high.astype(F32)).astype(BF16)


def dot(a, b, dims=(((1,), (0,)), ((), ()))):
    return lax.dot_general(a, b, dims, preferred_element_type=F32)


VMEM = pl.BlockSpec(memory_space=pltpu.VMEM)
SMEM = pl.BlockSpec(memory_space=pltpu.SMEM)
ANY = pl.BlockSpec(memory_space=pl.ANY)
HBM = pl.BlockSpec(memory_space=pltpu.HBM)


def cost(microseconds):
    return pl.CostEstimate(
        flops=0, transcendentals=0, bytes_accessed=int(microseconds * 3_000_000)
    )


def live_lanes(count, first, width):
    return ((lax.broadcasted_iota(I32, (1, width), 1) + first) < count).astype(F32)


def rows_kernel(remote, count_ref, field_ref, list_ref, rows_ref, slot_ref, selector_ref):
    blocks = field_ref.shape[1] // LANES
    count = count_ref[0]
    for block in range(blocks):
        lanes = slice(block * LANES, (block + 1) * LANES)
        value = field_ref[:, lanes] * live_lanes(count, block * LANES, LANES)
        value = jnp.concatenate([value, jnp.zeros((LANES - UNK, LANES), F32)], axis=0)
        rows_ref[lanes, :] = value.T
    per_list = list_ref.shape[1] // LANES
    for index in range(8):
        for part in range(per_list):
            row = index * per_list + part
            face = list_ref[index : index + 1, part * LANES : (part + 1) * LANES]
            slot_ref[row : row + 1, :] = jnp.maximum(face, 0) + remote
    selector_ref[...] = trace_selector()


def first_rows(part_count, right_side, lists):
    remote = lists.shape[0] * lists.shape[1]
    return pl.pallas_call(
        functools.partial(rows_kernel, remote),
        out_shape=(
            jax.ShapeDtypeStruct((right_side.shape[1], LANES), F32),
            jax.ShapeDtypeStruct((remote // LANES, LANES), I32),
            jax.ShapeDtypeStruct((2 * LANES, 4 * HALF), BF16),
        ),
        in_specs=[SMEM, VMEM, VMEM],
        out_specs=(VMEM,) * 3,
        compiler_params=pltpu.CompilerParams(vmem_limit_bytes=4 * MIB),
        cost_estimate=cost(2),
        name="first_rows",
    )(part_count, right_side, lists)


def prep_kernel(
    remote, _, class_ref, lift_ref, link_ref, normal_ref,
    pos_ref, tile_ref, index_ref, lift_hi_ref, lift_lo_ref, plane_ref, spread_ref,
):
    blocks = class_ref.shape[0]

    class_row = lax.broadcasted_iota(I32, (CLASSES, LANES), 0)
    totals = jnp.zeros((CLASSES, LANES), F32)
    for block in range(blocks):
        totals = totals + (class_ref[block : block + 1, :] == class_row).astype(F32)
    total = jnp.sum(totals, axis=1, keepdims=True)
    tiles = jnp.floor((total + (TILE - 1)) * (1.0 / TILE))
    tiles = jnp.broadcast_to(tiles, (CLASSES, LANES))
    lower = (
        lax.broadcasted_iota(I32, (CLASSES, CLASSES), 1)
        < lax.broadcasted_iota(I32, (CLASSES, CLASSES), 0)
    ).astype(BF16)
    start = dot(lower, tiles.astype(BF16))
    end = start + tiles
    earlier = (
        lax.broadcasted_iota(I32, (LANES, 2 * LANES), 0)
        < lax.broadcasted_iota(I32, (LANES, 2 * LANES), 1)
    ).astype(BF16)
    carry = start * TILE
    for block in range(blocks):
        member = (class_ref[block : block + 1, :] == class_row).astype(F32)
        ranks = dot(member.astype(BF16), earlier)
        position = jnp.sum(member * (ranks[:, :LANES] + carry), axis=0, keepdims=True)
        pos_ref[block : block + 1, :] = position.astype(I32)
        carry = carry + ranks[:, LANES:]
    tile_ref[...] = jnp.zeros((8, LANES), I32)
    for row in range(4):
        tile = (lax.broadcasted_iota(I32, (CLASSES, LANES), 1) + row * LANES).astype(F32)
        owner = jnp.sum((end <= tile).astype(F32), axis=0, keepdims=True)
        tile_ref[row : row + 1, :] = jnp.minimum(owner.astype(I32), CLASSES - 1)
    tile_ref[4:5, :] = end[CLASSES - 1 :, :].astype(I32)

    spread_ref[...] = jnp.zeros(spread_ref.shape, F32)
    for side in range(4):
        block = lift_ref[:, side, :]
        for c in range(6):
            first = side * HALF + c * 10
            spread_ref[first : first + 10, c * 20 : (c + 1) * 20] = block
    high, low = split(spread_ref[...].T)
    lift_hi_ref[...] = high
    lift_lo_ref[...] = low

    link = link_ref[...]
    own = (
        lax.broadcasted_iota(I32, link.shape, 0) * LANES
        + lax.broadcasted_iota(I32, link.shape, 1)
        + remote
    )
    index_ref[...] = jnp.where(link < 0, own, link)

    for c in range(3):
        for row in range(link.shape[0]):
            plane_ref[c, row : row + 1, :] = normal_ref[c : c + 1, row * LANES : (row + 1) * LANES]


def prepare(after, elem_class, lift, link, normal, remote):
    elements, faces = elem_class.shape[0], link.shape[0]
    return pl.pallas_call(
        functools.partial(prep_kernel, remote),
        out_shape=(
            jax.ShapeDtypeStruct((elements // LANES, LANES), I32),
            jax.ShapeDtypeStruct((8, LANES), I32),
            jax.ShapeDtypeStruct((faces // LANES, LANES), I32),
            jax.ShapeDtypeStruct((LANES, 4 * HALF), BF16),
            jax.ShapeDtypeStruct((LANES, 4 * HALF), BF16),
            jax.ShapeDtypeStruct((3, faces // LANES, LANES), F32),
        ),
        in_specs=[ANY] + [VMEM] * 4,
        out_specs=(VMEM,) * 6,
        scratch_shapes=[pltpu.VMEM((4 * HALF, LANES), F32)],
        compiler_params=pltpu.CompilerParams(vmem_limit_bytes=4 * MIB),
        cost_estimate=cost(3),
        name="prepare",
    )(
        after, elem_class.reshape(elements // LANES, LANES), jnp.transpose(lift, (2, 0, 1)),
        link.reshape(faces // LANES, LANES), normal,
    )


def trace_block(rows_ref, selector_ref, table_ref, first, index):
    elements = rows_ref.shape[0]
    width = 2 * LANES
    left = lax.broadcasted_iota(I32, (width, LANES), 1) < HALF
    base = pl.multiple_of(index * width, width)
    high, low = split(rows_ref[pl.ds(base, width), :])
    traces = dot(jnp.concatenate([high, low], axis=1), selector_ref[...])
    for pair in range(2):
        both = traces[:, pair * LANES : (pair + 1) * LANES]
        swapped = pltpu.roll(both, HALF, 1)
        even, odd = first + 2 * pair * elements, first + (2 * pair + 1) * elements
        table_ref[pl.ds(even + base, width), :] = jnp.where(left, both, swapped)
        table_ref[pl.ds(odd + base, width), :] = jnp.where(left, swapped, both)


def write_traces(rows_ref, selector_ref, table_ref, first):
    def block(index, carry):
        trace_block(rows_ref, selector_ref, table_ref, first, index)
        return carry

    lax.fori_loop(0, rows_ref.shape[0] // (2 * LANES), block, 0, unroll=4)


def staggered(count, before, after):
    before(0)

    def body(index, carry):
        after(index - 1)
        before(index)
        return carry

    lax.fori_loop(1, count, body, 0)
    after(count - 1)


def gather_pairs(table_ref, index_ref, out_ref, first_a, first_b, offset, count, unroll):
    left = lax.broadcasted_iota(I32, (1, LANES), 1) < HALF

    def block(index, carry):
        base = pl.multiple_of(index * unroll, unroll)
        for step in range(unroll):
            row_a = table_ref[pl.ds(index_ref[first_a + base + step] + offset, 1), :]
            row_b = table_ref[pl.ds(index_ref[first_b + base + step] + offset, 1), :]
            out_ref[pl.ds(base + step, 1), :] = jnp.where(left, row_a, row_b)
        return carry

    lax.fori_loop(0, count // unroll, block, 0)


def element_order(solved_ref, pos_ref, rows_ref):
    unroll = 256

    def fetch(index, carry):
        base = pl.multiple_of(index * unroll, unroll)
        for step in range(unroll):
            rows_ref[pl.ds(base + step, 1), :] = solved_ref[pl.ds(pos_ref[base + step], 1), :]
        return carry

    lax.fori_loop(0, rows_ref.shape[0] // unroll, fetch, 0)


def inner_partials(refs, pairs_of, lanes, turned):
    elements = refs[0].shape[0]
    source, target = turned

    def block(index, sums):
        rows = pl.ds(pl.multiple_of(index * LANES, LANES), LANES)
        values = [ref[rows, :] for ref in refs]
        target[:, rows] = values[source].T[:UNK]
        return tuple(
            total + jnp.sum(pair.reshape(LANES // 8, 8, LANES), axis=0)
            for total, pair in zip(sums, pairs_of(*values))
        )

    zero = jnp.zeros((8, LANES), F32)
    sums = lax.fori_loop(0, elements // LANES, block, (zero,) * len(lanes))
    lane = lax.broadcasted_iota(I32, (1, LANES), 1)
    row = jnp.zeros((1, LANES), F32)
    for index, value in zip(lanes, sums):
        value = jnp.sum(jnp.sum(value, axis=0, keepdims=True), axis=1, keepdims=True)
        row = jnp.where(lane == index, value, row)
    return row


def class_major(native_ref, turned_ref, stage_ref, part_ref, class_hbm, sems):
    for half in range(2):
        for row in range(CHUNK):
            last = row * NODE_PITCH + UNK
            turned_ref[half, last : last + LANES - UNK, :] = jnp.zeros((LANES - UNK, LANES), F32)

    def store(first):
        slot = first // CHUNK % 2
        target = class_hbm.at[:, pl.ds(first, CHUNK), :]
        return pltpu.make_async_copy(part_ref.at[slot], target, sems.at[slot])

    for first in range(0, LANES, CHUNK):
        count = min(CHUNK, UNK - first)

        def collect(index, carry):
            value = native_ref[index, first : first + count, :].astype(F32)
            if count < CHUNK:
                value = jnp.concatenate([value, jnp.zeros((CHUNK - count, CLASSES), F32)], axis=0)
            for half in range(2):
                turned_ref[half, pl.ds(index, CHUNK, stride=NODE_PITCH), :] = value[
                    :, half * LANES : (half + 1) * LANES
                ]
            return carry

        lax.fori_loop(0, UNK, collect, 0, unroll=24)

        for row in range(CHUNK):
            for half in range(2):
                target = pl.ds(half * LANES * STAGE_PITCH + row, LANES, stride=STAGE_PITCH)
                rows = slice(row * NODE_PITCH, row * NODE_PITCH + LANES)
                stage_ref[target, :] = turned_ref[half, rows, :].T
        stage = stage_ref[...].reshape(CLASSES, STAGE_PITCH, LANES)[:, :CHUNK]
        if first >= 2 * CHUNK:
            store(first - 2 * CHUNK).wait()
        part_ref[first // CHUNK % 2] = stage.astype(BF16)
        store(first).start()
    return [store(LANES - 2 * CHUNK), store(LANES - CHUNK)]


def exchange_kernel(grid_rows, grid_columns, with_classes, *refs):
    if with_classes:
        (rows_ref, selector_ref, list_any, native_hbm, table_ref, class_hbm,
         list_ref, outgoing_ref, received_ref, local_sem, send_sem, recv_sem,
         native_ref, turned_ref, stage_ref, part_ref, native_sem, part_sems) = refs
        native_copy = pltpu.make_async_copy(native_hbm, native_ref, native_sem)
        native_copy.start()
    else:
        (solved_ref, first_ref, pos_any, selector_ref, list_any,
         table_ref, rows_ref, columns_ref, part_ref, list_ref, outgoing_ref, received_ref, local_sem, send_sem, recv_sem,
         pos_ref, pos_sem) = refs
        pos_copy = pltpu.make_async_copy(pos_any, pos_ref, pos_sem)
        pos_copy.start()
    list_copy = pltpu.make_async_copy(list_any, list_ref, local_sem)
    list_copy.start()
    slots = outgoing_ref.shape[1]
    row, column = lax.axis_index("prow"), lax.axis_index("pcol")

    def present(index):
        a, b = OFFSETS[index]
        inside = None
        for at, step, size in ((row, a, grid_rows), (column, b, grid_columns)):
            if step == 0:
                continue
            term = at > 0 if step < 0 else at < size - 1
            inside = term if inside is None else jnp.logical_and(inside, term)
        return inside

    def partner(index):
        a, b = OFFSETS[index]
        return (row + a, column + b)

    def transfer(index):
        return pltpu.make_async_remote_copy(
            src_ref=outgoing_ref.at[index],
            dst_ref=received_ref.at[7 - index],
            send_sem=send_sem.at[index],
            recv_sem=recv_sem.at[7 - index],
            device_id=partner(index),
            device_id_type=MESH,
        )

    barrier = pltpu.get_barrier_semaphore()
    for index in range(8):
        @pl.when(present(index))
        def _(index=index):
            pl.semaphore_signal(barrier, inc=1, device_id=partner(index), device_id_type=MESH)

    if not with_classes:
        pos_copy.wait()
        element_order(solved_ref, pos_ref, rows_ref)
    write_traces(rows_ref, selector_ref, table_ref, 16 * slots)
    list_copy.wait()

    def gather(index):
        first = index * 2 * slots
        gather_pairs(
            table_ref, list_ref, outgoing_ref.at[index], first, first + slots, 0, slots, 32
        )

    early, late = ((0, 2, 5, 7), (3, 4, 1, 6)) if with_classes else ((0,), (2, 5, 7, 3, 4, 1, 6))
    for index in early:
        gather(index)

    near_rows = 1 + (row > 0).astype(I32) + (row < grid_rows - 1).astype(I32)
    near_columns = 1 + (column > 0).astype(I32) + (column < grid_columns - 1).astype(I32)
    pl.semaphore_wait(barrier, near_rows * near_columns - 1)

    for index in early + late:
        if index in late:
            gather(index)

        @pl.when(present(index))
        def _(index=index):
            transfer(index).start()

    if with_classes:
        native_copy.wait()
        stores = class_major(native_ref, turned_ref, stage_ref, part_ref, class_hbm, part_sems)
    else:
        part_ref[...] = inner_partials(
            (first_ref, rows_ref), lambda f, t: (f * f, f * t, t * t), (0, 1, 2), (1, columns_ref)
        )

    left = lax.broadcasted_iota(I32, (slots, LANES), 1) < HALF
    for index in (1, 6, 3, 4, 0, 2, 5, 7):
        @pl.when(present(index))
        def _(index=index):
            transfer(7 - index).wait_recv()
            packed = received_ref[index]
            swapped = pltpu.roll(packed, HALF, 1)
            first = index * 2 * slots
            table_ref[first : first + slots, :] = jnp.where(left, packed, swapped)
            table_ref[first + slots : first + 2 * slots, :] = jnp.where(left, swapped, packed)

    for index in range(8):
        @pl.when(present(index))
        def _(index=index):
            transfer(index).wait_send()

    if with_classes:
        for store in stores:
            store.wait()


def exchange(rows, selector, lists, native=None, first=None, pos=None):
    slots = lists.shape[0] // 16
    with_classes = native is not None
    elements = rows.shape[0] if with_classes else pos.shape[0]
    out_shape = [jax.ShapeDtypeStruct((16 * slots + 4 * elements, LANES), F32)]
    scratch = [
        pltpu.SMEM(lists.shape, I32),
        pltpu.VMEM((8, slots, LANES), F32),
        pltpu.VMEM((8, slots, LANES), F32),
        pltpu.SemaphoreType.DMA(()),
        pltpu.SemaphoreType.DMA((8,)),
        pltpu.SemaphoreType.DMA((8,)),
    ]
    if with_classes:
        operands = [rows, selector, lists, native]
        in_specs, out_specs = [VMEM, VMEM, ANY, HBM], (VMEM, HBM)
        out_shape.append(jax.ShapeDtypeStruct((CLASSES, LANES, LANES), BF16))
        scratch += [
            pltpu.VMEM(native.shape, BF16),
            pltpu.VMEM((2, CHUNK * NODE_PITCH, LANES), F32),
            pltpu.VMEM((CLASSES * STAGE_PITCH, LANES), F32),
            pltpu.VMEM((2, CLASSES, CHUNK, LANES), BF16),
            pltpu.SemaphoreType.DMA(()),
            pltpu.SemaphoreType.DMA((2,)),
        ]
    else:
        operands = [rows, first, pos, selector, lists]
        in_specs, out_specs = [VMEM, VMEM, ANY, VMEM, ANY], (VMEM,) * 4
        out_shape += [
            jax.ShapeDtypeStruct((elements, LANES), F32),
            jax.ShapeDtypeStruct((UNK, elements), F32),
            jax.ShapeDtypeStruct((1, LANES), F32),
        ]
        scratch += [pltpu.SMEM(pos.shape, I32), pltpu.SemaphoreType.DMA(())]
    return pl.pallas_call(
        functools.partial(
            exchange_kernel, lax.axis_size("prow"), lax.axis_size("pcol"), with_classes
        ),
        out_shape=tuple(out_shape),
        in_specs=in_specs,
        out_specs=out_specs,
        scratch_shapes=scratch,
        compiler_params=pltpu.CompilerParams(
            collective_id=2 if with_classes else 0, has_side_effects=True,
            vmem_limit_bytes=(44 if with_classes else 8) * MIB,
        ),
        cost_estimate=cost(14),
        name="exchange_first" if with_classes else "exchange",
    )(*operands)


def turn_choices():
    _, turn_rows = trace_tables()
    choices = []
    for j in range(10):
        sources = {}
        for option in range(6):
            sources.setdefault(turn_rows[option][j], []).append(option)
        choices.append([(source, tuple(options)) for source, options in sources.items()])
    return choices


def turn_faces(node_ref, first, stride, orient):
    masks = {}

    def mask(options):
        if options not in masks:
            value = orient == options[0]
            for option in options[1:]:
                value = jnp.logical_or(value, orient == option)
            masks[options] = value
        return masks[options]

    choices = turn_choices()
    for c in range(6):
        at = [pl.ds(first + c * 10 + j, 8, stride=stride) for j in range(10)]
        nodes = [node_ref[at[j], :] for j in range(10)]
        for j in range(10):
            (source, _), *others = choices[j]
            value = nodes[source]
            for source, options in others:
                value = jnp.where(mask(options), nodes[source], value)
            if others:
                node_ref[at[j], :] = value


def face_flux(electric, magnetic, normal, scale):
    along_e = normal[0] * electric[0] + normal[1] * electric[1] + normal[2] * electric[2]
    along_h = normal[0] * magnetic[0] + normal[1] * magnetic[1] + normal[2] * magnetic[2]
    flux = []
    for c in range(3):
        a, b = (c + 1) % 3, (c + 2) % 3
        cross = normal[a] * magnetic[b] - normal[b] * magnetic[a]
        flux.append(scale * (electric[c] - normal[c] * along_e - cross))
    for c in range(3):
        a, b = (c + 1) % 3, (c + 2) % 3
        cross = normal[a] * electric[b] - normal[b] * electric[a]
        flux.append(scale * (magnetic[c] - normal[c] * along_h + cross))
    return flux


def image_kernel(
    count_ref, index_any, pos_any, tile_any,
    table_ref, lift_hi_ref, lift_lo_ref,
    link_ref, orient_ref, normal_ref, quotient_ref, class_hbm,
    solved_ref,
    index_ref, pos_ref, tile_ref, smem_sems, class_ref, class_sem,
    picked_ref, node_ref, flux_ref, coupled_ref, sorted_ref,
):
    index_copy = pltpu.make_async_copy(index_any, index_ref, smem_sems.at[0])
    pos_copy = pltpu.make_async_copy(pos_any, pos_ref, smem_sems.at[1])
    tile_copy = pltpu.make_async_copy(tile_any, tile_ref, smem_sems.at[2])
    class_copy = pltpu.make_async_copy(class_hbm, class_ref, class_sem)
    for copy in (index_copy, pos_copy, tile_copy, class_copy):
        copy.start()
    elements = coupled_ref.shape[0]
    blocks = elements // LANES
    chunks = blocks // 8

    index_copy.wait()
    left = lax.broadcasted_iota(I32, (1, LANES), 1) < HALF

    def gather(index):
        base = pl.multiple_of(index * LANES, LANES)
        for step in range(LANES):
            row_a = table_ref[pl.ds(index_ref[base + step], 1), :]
            row_b = table_ref[pl.ds(index_ref[2 * elements + base + step], 1), :]
            picked_ref[pl.ds(base + step, 1), :] = jnp.where(left, row_a, row_b)

    def transpose(index):
        rows = pl.ds(pl.multiple_of(index * LANES, LANES), LANES)
        target = pl.multiple_of(index * NODE_PITCH, 8)
        node_ref[pl.ds(target, LANES), :] = picked_ref[rows, :].T

    staggered(2 * blocks, gather, transpose)

    for block in range(blocks):
        for side in range(4):
            last = block * FLUX_PITCH + (side + 1) * HALF
            flux_ref[last - 8 : last, :] = jnp.zeros((8, LANES), F32)

    count = count_ref[0]
    lane = (
        lax.broadcasted_iota(I32, (8, LANES), 0) * LANES + lax.broadcasted_iota(I32, (8, LANES), 1)
    )

    def chunk(index, carry):
        side, part = index // chunks, index % chunks
        pair, half = side % 2, side // 2
        faces = pl.ds(pl.multiple_of(side * blocks + part * 8, 8), 8)
        first = (pair * blocks + part * 8) * NODE_PITCH + half * HALF
        turn_faces(node_ref, first, NODE_PITCH, orient_ref[faces, :])
        alive = ((lane + part * (8 * LANES)) < count).astype(F32)
        scale = 0.5 * quotient_ref[faces, :] * alive
        sign = jnp.where(link_ref[faces, :] < 0, -1.0, 1.0)
        normal = [normal_ref[c, faces, :] for c in range(3)]
        target = part * (8 * FLUX_PITCH) + side * HALF
        for j in range(10):
            nodes = [node_ref[pl.ds(first + c * 10 + j, 8, stride=NODE_PITCH), :] for c in range(6)]
            electric = [value * sign for value in nodes[:3]]
            flux = face_flux(electric, nodes[3:], normal, scale)
            for c in range(6):
                flux_ref[pl.ds(target + c * 10 + j, 8, stride=FLUX_PITCH), :] = flux[c]
        return carry

    lax.fori_loop(0, 4 * chunks, chunk, 0)

    def lift(index, carry):
        rows = 4 * HALF
        first = pl.multiple_of(index * (2 * FLUX_PITCH), 8)
        second = pl.multiple_of(first + FLUX_PITCH, 8)
        value = jnp.concatenate(
            [flux_ref[pl.ds(first, rows), :], flux_ref[pl.ds(second, rows), :]], axis=1
        )
        high, low = split(value)
        coupled = dot(lift_hi_ref[...], high) + dot(lift_hi_ref[...], low) + dot(lift_lo_ref[...], high)
        base = pl.multiple_of(index * (2 * LANES), 2 * LANES)
        coupled_ref[pl.ds(base, 2 * LANES), :] = coupled.T
        return carry

    lax.fori_loop(0, blocks // 2, lift, 0, unroll=8)

    pos_copy.wait()
    tile_copy.wait()
    for row in range(elements):
        sorted_ref[pl.ds(pos_ref[row], 1), :] = coupled_ref[row : row + 1, :]
    class_copy.wait()

    def solve(index, carry):
        for step in range(0, GROUP, 2):
            tile = index * GROUP + step
            base = pl.multiple_of(tile * TILE, 2 * TILE)
            high, low = split(sorted_ref[pl.ds(base, 2 * TILE), :])
            pair = jnp.concatenate(
                [class_ref[tile_ref[tile]], class_ref[tile_ref[tile + 1]]], axis=1
            )
            result = dot(jnp.concatenate([high, low], axis=0), pair)
            result = result[: 2 * TILE] + result[2 * TILE :]
            solved_ref[pl.ds(base, TILE), :] = result[:TILE, :LANES]
            solved_ref[pl.ds(base + TILE, TILE), :] = result[TILE:, LANES:]
        return carry

    lax.fori_loop(0, (tile_ref[4 * LANES] + (GROUP - 1)) // GROUP, solve, 0)


def image(part_count, indices, pos, tiles, table, lift_hi, lift_lo,
          link, orient, normal, quotient, classes):
    elements = pos.shape[0]
    slots = TILE_ROWS * TILE
    return pl.pallas_call(
        image_kernel,
        out_shape=jax.ShapeDtypeStruct((slots, LANES), F32),
        in_specs=[SMEM] + [ANY] * 3 + [VMEM] * 7 + [HBM],
        out_specs=VMEM,
        scratch_shapes=[
            pltpu.SMEM(indices.shape, I32),
            pltpu.SMEM(pos.shape, I32),
            pltpu.SMEM(tiles.shape, I32),
            pltpu.SemaphoreType.DMA((3,)),
            pltpu.VMEM(classes.shape, BF16),
            pltpu.SemaphoreType.DMA(()),
            pltpu.VMEM((2 * elements, LANES), F32),
            pltpu.VMEM((2 * elements // LANES * NODE_PITCH, LANES), F32),
            pltpu.VMEM((elements // LANES * FLUX_PITCH, LANES), F32),
            pltpu.VMEM((elements, LANES), F32),
            pltpu.VMEM((slots, LANES), F32),
        ],
        compiler_params=pltpu.CompilerParams(vmem_limit_bytes=44 * MIB),
        cost_estimate=cost(20),
        name="image",
    )(
        part_count, indices, pos, tiles, table, lift_hi, lift_lo,
        link.reshape(-1, LANES), orient.reshape(-1, LANES), normal,
        quotient.reshape(-1, LANES), classes,
    )


def total_kernel(grid_rows, grid_columns, first_ref, second_ref, solved_ref, known_ref, pos_any,
                 total_ref, columns_ref, third_ref, pos_ref, pos_sem, part_ref, over_rows, over_columns, send_row, recv_row, send_column, recv_column):
    row, column = lax.axis_index("prow"), lax.axis_index("pcol")
    pos_copy = pltpu.make_async_copy(pos_any, pos_ref, pos_sem)
    pos_copy.start()

    def row_partner(step):
        return lax.rem(row + step, grid_rows)

    def column_partner(step):
        return lax.rem(column + step, grid_columns)

    barrier = pltpu.get_barrier_semaphore()
    for step in range(1, grid_rows):
        pl.semaphore_signal(
            barrier, inc=1, device_id=(row_partner(step), column), device_id_type=MESH
        )
    for step in range(1, grid_columns):
        pl.semaphore_signal(
            barrier, inc=1, device_id=(row, column_partner(step)), device_id_type=MESH
        )
    pos_copy.wait()
    element_order(solved_ref, pos_ref, third_ref)
    part_ref[...] = known_ref[...] + inner_partials(
        (first_ref, second_ref, third_ref), lambda f, t, u: (f * u, t * u, u * u), (3, 4, 5),
        (2, columns_ref),
    )
    pl.semaphore_wait(barrier, grid_rows + grid_columns - 2)

    def row_copy(step):
        return pltpu.make_async_remote_copy(
            src_ref=part_ref,
            dst_ref=over_rows.at[step],
            send_sem=send_row,
            recv_sem=recv_row,
            device_id=(row_partner(step), column),
            device_id_type=MESH,
        )

    def wait_all(buffer, count, sem):
        landed = buffer.at[pl.ds(1, count)]
        pltpu.make_async_copy(landed, landed, sem).wait()

    for step in range(1, grid_rows):
        row_copy(step).start()
    over_rows[0] = part_ref[...]
    wait_all(over_rows, grid_rows - 1, recv_row)
    total = over_rows[row]
    for source in range(1, grid_rows):
        total = total + over_rows[lax.rem(row - source + grid_rows, grid_rows)]
    over_columns[0] = total

    def column_copy(step):
        return pltpu.make_async_remote_copy(
            src_ref=over_columns.at[0],
            dst_ref=over_columns.at[step],
            send_sem=send_column,
            recv_sem=recv_column,
            device_id=(row, column_partner(step)),
            device_id_type=MESH,
        )

    for step in range(1, grid_columns):
        column_copy(step).start()
    wait_all(over_columns, grid_columns - 1, recv_column)
    total = over_columns[column]
    for source in range(1, grid_columns):
        total = total + over_columns[lax.rem(column - source + grid_columns, grid_columns)]
    total_ref[...] = total
    wait_all(over_rows, grid_rows - 1, send_row)
    wait_all(over_columns, grid_columns - 1, send_column)


def total_over_devices(first, second, solved, known, pos):
    grid_rows, grid_columns = lax.axis_size("prow"), lax.axis_size("pcol")
    part = (1, LANES)
    return pl.pallas_call(
        functools.partial(total_kernel, grid_rows, grid_columns),
        out_shape=(
            jax.ShapeDtypeStruct(part, F32),
            jax.ShapeDtypeStruct((UNK, first.shape[0]), F32),
        ),
        in_specs=[VMEM] * 4 + [ANY],
        out_specs=(VMEM,) * 2,
        scratch_shapes=[
            pltpu.VMEM(first.shape, F32),
            pltpu.SMEM(pos.shape, I32),
            pltpu.SemaphoreType.DMA(()),
            pltpu.VMEM(part, F32),
            pltpu.VMEM((grid_rows,) + part, F32),
            pltpu.VMEM((grid_columns,) + part, F32),
            pltpu.SemaphoreType.DMA(()),
            pltpu.SemaphoreType.DMA(()),
            pltpu.SemaphoreType.DMA(()),
            pltpu.SemaphoreType.DMA(()),
        ],
        compiler_params=pltpu.CompilerParams(
            collective_id=1, has_side_effects=True, vmem_limit_bytes=8 * MIB
        ),
        cost_estimate=cost(12),
        name="total",
    )(first, second, solved, known, pos)


def finish_kernel(
    weight, count_ref, total_ref, field_ref, second_ref, third_ref, basis_hbm, hess_ref,
    basis_ref, sems,
):
    width = field_ref.shape[1]
    gram = total_ref[...] * weight
    lane = lax.broadcasted_iota(I32, gram.shape, 1)
    ff, ft, tt, fu, tu, uu = (
        jnp.sum(jnp.where(lane == index, gram, 0.0), axis=1, keepdims=True) for index in range(6)
    )
    square = ff + EPSILON
    inverse = 1.0 / square
    p = (EPSILON - ft) * inverse
    h10_square = jnp.maximum(tt + 2 * p * ft + p * p * ff, 0.0) * inverse + EPSILON
    k1_square = inverse / h10_square
    h11 = k1_square * (tu + (1 + p) * tt + p * ft + p * fu + p * (1 + p) * ft + p * p * ff)
    along = (fu + (1 + p) * ft + p * ff) * inverse
    q = 1 + p - h11
    w = p * (1 - h11) - along
    rest = uu + 2 * q * tu + 2 * w * fu + q * q * tt + 2 * q * w * ft + w * w * ff
    h21_square = k1_square * jnp.maximum(rest, 0.0) + EPSILON
    k0 = 1.0 / jnp.sqrt(square)
    k1 = jnp.sqrt(k1_square)
    h10, h21 = jnp.sqrt(h10_square), jnp.sqrt(h21_square)
    h00, h01 = (ff + ft) * inverse, along / h10
    k2 = k1 / h21

    alive = live_lanes(count_ref[0], 0, width)
    copies = []
    for first in range(0, UNK, SLAB):
        rows = pl.ds(first, SLAB)
        f = field_ref[rows, :] * alive
        t, u = second_ref[rows, :], third_ref[rows, :]
        basis_ref[0, rows, :] = f * k0
        basis_ref[1, rows, :] = t * k1 + f * (p * k1)
        basis_ref[2, rows, :] = u * k2 + t * (q * k2) + f * (w * k2)
        at = (slice(None), rows, slice(None))
        copies.append(
            pltpu.make_async_copy(basis_ref.at[at], basis_hbm.at[at], sems.at[first // SLAB])
        )
        copies[-1].start()

    at_row = lax.broadcasted_iota(I32, (2, 3), 1)
    at_column = lax.broadcasted_iota(I32, (2, 3), 0)
    hess = jnp.zeros((2, 3), F32)
    for i, j, value in ((0, 0, h00), (1, 0, h10), (0, 1, h01), (1, 1, h11), (2, 1, h21)):
        hess = jnp.where(jnp.logical_and(at_row == i, at_column == j), value, hess)
    hess_ref[...] = hess
    for copy in copies:
        copy.wait()


def finish(weight, part_count, total, right_side, second, third):
    elements = right_side.shape[1]
    return pl.pallas_call(
        functools.partial(finish_kernel, weight),
        out_shape=(
            jax.ShapeDtypeStruct((3, UNK, elements), F32),
            jax.ShapeDtypeStruct((2, 3), F32),
        ),
        in_specs=[SMEM] + [VMEM] * 4,
        out_specs=(HBM, VMEM),
        scratch_shapes=[
            pltpu.VMEM((3, UNK, elements), F32),
            pltpu.SemaphoreType.DMA((UNK // SLAB,)),
        ],
        compiler_params=pltpu.CompilerParams(vmem_limit_bytes=12 * MIB),
        name="finish",
    )(part_count, total, right_side, second, third)


def shards(
    right_side,
    part_count,
    elem_class,
    face_link,
    face_orient,
    face_normal,
    boundary_metric_quotient,
    bound_face,
    lift,
    inverse_table,
):
    unknowns, elements = right_side.shape
    all_subdomains = lax.axis_size("prow") * lax.axis_size("pcol")
    weight = 1.0 / (unknowns * elements * all_subdomains)
    native = jnp.transpose(inverse_table, (1, 2, 0))
    first, lists, selector = first_rows(part_count, right_side, bound_face[0])
    lists = lists.reshape(-1)
    first_table, classes = exchange(first, selector, lists, native)
    pos, tiles, indices, lift_hi, lift_lo, normal = prepare(
        first_table, elem_class, lift, face_link, face_normal, lists.shape[0]
    )
    pos, tiles, indices = pos.reshape(-1), tiles.reshape(-1), indices.reshape(-1)

    def operator_image(table):
        return image(
            part_count, indices, pos, tiles, table, lift_hi, lift_lo, face_link, face_orient,
            normal, boundary_metric_quotient, classes,
        )

    solved = operator_image(first_table)
    second_table, second, second_columns, known = exchange(
        solved, selector, lists, first=first, pos=pos
    )
    solved = operator_image(second_table)
    total, third_columns = total_over_devices(first, second, solved, known, pos)
    basis, hess = finish(weight, part_count, total, right_side, second_columns, third_columns)
    return (basis, hess.T)


def solution(mesh):
    in_specs = (
        P(None, ("prow", "pcol")),
        P(("prow", "pcol")),
        P(("prow", "pcol")),
        P(("prow", "pcol")),
        P(("prow", "pcol")),
        P(None, ("prow", "pcol")),
        P(("prow", "pcol")),
        P(("prow", "pcol"), None, None),
        P(),
        P(),
    )
    out_specs = (P(None, None, ("prow", "pcol")), P())
    return jax.shard_map(shards, mesh=mesh, in_specs=in_specs, out_specs=out_specs, check_vma=False)
```
